32 devices in a mesh: dp: 4 (over y, x), fsdp: 8 (over z, core).
Axes of the slice: x: 2, y: 2, z: 4, core: 2. Of those that a mesh axis runs over, the one named last changes fastest.
Arguments:
- tokens: bfloat16 [32768, 768], P(('dp', 'fsdp')), may hold values from -6 to 6
- counts: int32 [32], P(('dp', 'fsdp')), may hold values from 897 to 1024, as said below
- inner_attend: bfloat16 [768, 2304], P(('dp', 'fsdp')), may hold values from -0.21875 to 0.21875
- inner_attend_bias: bfloat16 [2304], P(('dp', 'fsdp')), may hold values from -1.796875 to 1.796875
- inner_merge: bfloat16 [768, 768], P(('dp', 'fsdp')), may hold values from -2.5 to 2.5
- inner_merge_bias: bfloat16 [768], P(('dp', 'fsdp')), may hold values from -1.796875 to 1.796875
- inner_gain: bfloat16 [768], P(('dp', 'fsdp')), may hold values from 0.5 to 1.5
- inner_shift: bfloat16 [768], P(('dp', 'fsdp')), may hold values from -1.796875 to 1.796875
- inner_expand: bfloat16 [768, 3072], P(('dp', 'fsdp')), may hold values from -0.21875 to 0.21875
- inner_expand_bias: bfloat16 [3072], P(('dp', 'fsdp')), may hold values from -1.796875 to 1.796875
- inner_reduce: bfloat16 [3072, 768], P(('dp', 'fsdp')), may hold values from -0.109375 to 0.109375
- inner_reduce_bias: bfloat16 [768], P(('dp', 'fsdp')), may hold values from -1.796875 to 1.796875
- inner_final_gain: bfloat16 [768], P(('dp', 'fsdp')), may hold values from 0.5 to 1.5
- inner_final_shift: bfloat16 [768], P(('dp', 'fsdp')), may hold values from -1.796875 to 1.796875
- outer_attend: bfloat16 [768, 2304], P(('dp', 'fsdp')), may hold values from -0.21875 to 0.21875
- outer_attend_bias: bfloat16 [2304], P(('dp', 'fsdp')), may hold values from -1.796875 to 1.796875
- outer_merge: bfloat16 [768, 768], P(('dp', 'fsdp')), may hold values from -0.625 to 0.625
- outer_merge_bias: bfloat16 [768], P(('dp', 'fsdp')), may hold values from -1.796875 to 1.796875
- outer_gain: bfloat16 [768], P(('dp', 'fsdp')), may hold values from 0.5 to 1.5
- outer_shift: bfloat16 [768], P(('dp', 'fsdp')), may hold values from -1.796875 to 1.796875
- outer_expand: bfloat16 [768, 3072], P(('dp', 'fsdp')), may hold values from -0.21875 to 0.21875
- outer_expand_bias: bfloat16 [3072], P(('dp', 'fsdp')), may hold values from -1.796875 to 1.796875
- outer_reduce: bfloat16 [3072, 768], P(('dp', 'fsdp')), may hold values from -0.109375 to 0.109375
- outer_reduce_bias: bfloat16 [768], P(('dp', 'fsdp')), may hold values from -1.796875 to 1.796875
- outer_final_gain: bfloat16 [768], P(('dp', 'fsdp')), may hold values from 0.5 to 1.5
- outer_final_shift: bfloat16 [768], P(('dp', 'fsdp')), may hold values from -1.796875 to 1.796875
- segment_place: bfloat16 [768, 8], P(('dp', 'fsdp')), may hold values from -3 to 3
- cotangent: bfloat16 [32768, 768], P(('dp', 'fsdp')), may hold values from -6 to 6
Outputs:
- mixed: bfloat16 [32768, 768], P(('dp', 'fsdp'))
- tokens_grad: float32 [32768, 768], P(('dp', 'fsdp'))
- grad_inner_attend: float32 [768, 2304], P(('dp', 'fsdp'))
- grad_inner_attend_bias: float32 [2304], P(('dp', 'fsdp'))
- grad_inner_merge: float32 [768, 768], P(('dp', 'fsdp'))
- grad_inner_merge_bias: float32 [768], P(('dp', 'fsdp'))
- grad_inner_gain: float32 [768], P(('dp', 'fsdp'))
- grad_inner_shift: float32 [768], P(('dp', 'fsdp'))
- grad_inner_expand: float32 [768, 3072], P(('dp', 'fsdp'))
- grad_inner_expand_bias: float32 [3072], P(('dp', 'fsdp'))
- grad_inner_reduce: float32 [3072, 768], P(('dp', 'fsdp'))
- grad_inner_reduce_bias: float32 [768], P(('dp', 'fsdp'))
- grad_inner_final_gain: float32 [768], P(('dp', 'fsdp'))
- grad_inner_final_shift: float32 [768], P(('dp', 'fsdp'))
- grad_outer_attend: float32 [768, 2304], P(('dp', 'fsdp'))
- grad_outer_attend_bias: float32 [2304], P(('dp', 'fsdp'))
- grad_outer_merge: float32 [768, 768], P(('dp', 'fsdp'))
- grad_outer_merge_bias: float32 [768], P(('dp', 'fsdp'))
- grad_outer_gain: float32 [768], P(('dp', 'fsdp'))
- grad_outer_shift: float32 [768], P(('dp', 'fsdp'))
- grad_outer_expand: float32 [768, 3072], P(('dp', 'fsdp'))
- grad_outer_expand_bias: float32 [3072], P(('dp', 'fsdp'))
- grad_outer_reduce: float32 [3072, 768], P(('dp', 'fsdp'))
- grad_outer_reduce_bias: float32 [768], P(('dp', 'fsdp'))
- grad_outer_final_gain: float32 [768], P(('dp', 'fsdp'))
- grad_outer_final_shift: float32 [768], P(('dp', 'fsdp'))
- grad_segment_place: float32 [768, 8], P(('dp', 'fsdp'))
The draws below stay inside these ranges and needn't reach their ends.
Inputs may be any that keep to these rules, and one draw needn't show every extreme that they name: `counts`: each document fills all its segments but the last, which holds at least one token; some document is full and some holds exactly 897 tokens.
All inputs are finite; a program needn't handle non-finite values.
Results may differ from the reference program's by a relative error of at most 0.025.
Values may be sent and summed in bfloat16 or wider, within the bound.
No kernel may reach another device: no remote copies, remote signals or barrier semaphores. Data moves between devices by JAX's collectives and lax.ppermute only.
A program may use at most 256 MiB of HBM per device.

```python
import jax
import jax.numpy as jnp
from jax import lax

D = 768
HEADS = 12
HD = 64
FF = 3072
SEG = 128
SLOTS = 1024
SEGS = 8
DOCS = 32
TOKENS = 32768


def draw_counts(key, part):
    key = jax.random.fold_in(key, 5)
    first_key, second_key = jax.random.split(key)
    base = jax.random.randint(first_key, (DOCS,), SLOTS - SEG + 1, SLOTS + 1)
    order = jax.random.permutation(second_key, DOCS)
    base = jnp.where(order == 0, SLOTS, base)
    base = jnp.where(order == 1, SLOTS - SEG + 1, base)
    return base.astype(jnp.int32)


def level_of(stream_key, shape, shards, least, top_value):
    gain, own = 1.0, jax.random.fold_in(stream_key, 6)
    for position, blocks in shards:
        heights = jnp.exp(jax.random.uniform(jax.random.fold_in(own, position), (blocks,), jnp.float32, least / len(shards), top_value / len(shards)))
        gain = gain * jnp.repeat(heights, shape[position] // blocks).reshape([-1 if axis == position else 1 for axis in range(len(shape))])
    return gain


def bell_draw(rng, dims, scale, bound, pieces=(), kind=jnp.bfloat16):
    level = level_of(rng, dims, pieces, -0.22, 0.18) if pieces else 1.0
    array = jax.random.normal(rng, dims, jnp.float32) * scale * level
    return jnp.minimum(jnp.maximum(array, -bound), bound).astype(kind)


def setup_inputs(seed: int = 0) -> dict:
    keys = jax.random.split(jax.random.key(seed), 29)
    tokens = bell_draw(keys[0], (TOKENS, D), 1.0, 6.0, ((0, 32),))
    counts = draw_counts(jax.random.fold_in(keys[28], 71), 0)
    inner_attend = bell_draw(keys[2], (D, 3 * D), D ** -0.5, 0.21875, ((0, 32),))
    inner_attend_bias = bell_draw(keys[3], (3 * D,), 0.3, 1.796875, ((0, 32),))
    inner_merge = bell_draw(keys[4], (D, D), (D // SEG) ** -0.5, 2.5, ((0, 32),))
    inner_merge_bias = bell_draw(keys[5], (D,), 0.3, 1.796875, ((0, 32),))
    inner_gain = jnp.clip(1.0 + 0.1 * jax.random.normal(keys[6], (D,), jnp.float32), 0.5, 1.5).astype(jnp.bfloat16)
    inner_shift = bell_draw(keys[7], (D,), 0.3, 1.796875, ((0, 32),))
    inner_expand = bell_draw(keys[8], (D, FF), D ** -0.5, 0.21875, ((0, 32),))
    inner_expand_bias = bell_draw(keys[9], (FF,), 0.3, 1.796875, ((0, 32),))
    inner_reduce = bell_draw(keys[10], (FF, D), FF ** -0.5, 0.109375, ((0, 32),))
    inner_reduce_bias = bell_draw(keys[11], (D,), 0.3, 1.796875, ((0, 32),))
    inner_final_gain = jnp.clip(1.0 + 0.1 * jax.random.normal(keys[12], (D,), jnp.float32), 0.5, 1.5).astype(jnp.bfloat16)
    inner_final_shift = bell_draw(keys[13], (D,), 0.3, 1.796875, ((0, 32),))
    outer_attend = bell_draw(keys[14], (D, 3 * D), D ** -0.5, 0.21875, ((0, 32),))
    outer_attend_bias = bell_draw(keys[15], (3 * D,), 0.3, 1.796875, ((0, 32),))
    outer_merge = bell_draw(keys[16], (D, D), (D // SEGS) ** -0.5, 0.625, ((0, 32),))
    outer_merge_bias = bell_draw(keys[17], (D,), 0.3, 1.796875, ((0, 32),))
    outer_gain = jnp.clip(1.0 + 0.1 * jax.random.normal(keys[18], (D,), jnp.float32), 0.5, 1.5).astype(jnp.bfloat16)
    outer_shift = bell_draw(keys[19], (D,), 0.3, 1.796875, ((0, 32),))
    outer_expand = bell_draw(keys[20], (D, FF), D ** -0.5, 0.21875, ((0, 32),))
    outer_expand_bias = bell_draw(keys[21], (FF,), 0.3, 1.796875, ((0, 32),))
    outer_reduce = bell_draw(keys[22], (FF, D), FF ** -0.5, 0.109375, ((0, 32),))
    outer_reduce_bias = bell_draw(keys[23], (D,), 0.3, 1.796875, ((0, 32),))
    outer_final_gain = jnp.clip(1.0 + 0.1 * jax.random.normal(keys[24], (D,), jnp.float32), 0.5, 1.5).astype(jnp.bfloat16)
    outer_final_shift = bell_draw(keys[25], (D,), 0.3, 1.796875, ((0, 32),))
    segment_place = bell_draw(keys[26], (D, SEGS), 0.5, 3.0, ((0, 32),))
    cotangent = bell_draw(keys[27], (TOKENS, D), 1.0, 6.0, ((0, 32),))
    return {"tokens": tokens, "counts": counts, "inner_attend": inner_attend, "inner_attend_bias": inner_attend_bias, "inner_merge": inner_merge, "inner_merge_bias": inner_merge_bias, "inner_gain": inner_gain, "inner_shift": inner_shift, "inner_expand": inner_expand, "inner_expand_bias": inner_expand_bias, "inner_reduce": inner_reduce, "inner_reduce_bias": inner_reduce_bias, "inner_final_gain": inner_final_gain, "inner_final_shift": inner_final_shift, "outer_attend": outer_attend, "outer_attend_bias": outer_attend_bias, "outer_merge": outer_merge, "outer_merge_bias": outer_merge_bias, "outer_gain": outer_gain, "outer_shift": outer_shift, "outer_expand": outer_expand, "outer_expand_bias": outer_expand_bias, "outer_reduce": outer_reduce, "outer_reduce_bias": outer_reduce_bias, "outer_final_gain": outer_final_gain, "outer_final_shift": outer_final_shift, "segment_place": segment_place, "cotangent": cotangent}


@jax.custom_vjp
def low(v):
    return lax.optimization_barrier(v.astype(jnp.bfloat16)).astype(jnp.float32)

@jax.custom_vjp
def low_back(v):
    return v

def low_keep(v):
    return (low(v), None)

def low_pass(kept, grad):
    return (grad,)

def back_keep(v):
    return (v, None)

def back_low(kept, grad):
    return (low(grad),)
low.defvjp(low_keep, low_pass)
low_back.defvjp(back_keep, back_low)

def norm_apply(rows, norm_gain, norm_shift):
    centre = lax.optimization_barrier(jnp.mean(rows, axis=-1, keepdims=True))
    centred = rows - centre
    spread = lax.optimization_barrier(jnp.mean(centred * centred, axis=-1, keepdims=True))
    return centred * lax.rsqrt(spread + 1e-05) * norm_gain + norm_shift

def matmul(left_rows, right_rows):
    return jnp.dot(left_rows, right_rows, precision=lax.Precision.HIGHEST)

def block(source, key_mask, weights):
    attend, attend_bias, merge, merge_bias, norm_gain, norm_shift, expand, expand_bias, reduce_matrix, reduce_bias, final_gain, final_shift = weights
    groups, length, row_width = source.shape
    source_rows = source.reshape(groups * length, row_width)
    projected = low_back(low(matmul(source_rows, attend) + attend_bias))
    projected = projected.reshape(groups, length, 3, HEADS, HD)
    query_heads = projected[:, :, 0]
    key_heads = projected[:, :, 1]
    value_heads = projected[:, :, 2]
    scores = jnp.einsum('gqhe,gkhe->ghqk', query_heads, key_heads, precision=lax.Precision.HIGHEST) * HD ** (-0.5)
    scores = low_back(scores)
    if key_mask is not None:
        scores = jnp.where(key_mask[:, None, None, :], scores, -1e+30)
    probs = low(jax.nn.softmax(scores, axis=-1))
    context = jnp.einsum('ghqk,gkhe->gqhe', probs, value_heads, precision=lax.Precision.HIGHEST)
    context = low_back(low(context)).reshape(groups * length, row_width)
    attn_rows = low_back(matmul(context, merge) + merge_bias)
    first_sum = source_rows + attn_rows
    normed = low(norm_apply(first_sum, norm_gain, norm_shift))
    hidden = low_back(matmul(normed, expand) + expand_bias)
    active = low(jax.nn.gelu(hidden, approximate=False))
    branch = low_back(matmul(active, reduce_matrix) + reduce_bias)
    return norm_apply(normed + branch, final_gain, final_shift)

def forward_docs(rows, lengths, weights):
    docs = lengths.shape[0]
    keep_mask = jnp.arange(SLOTS)[None, :] < lengths[:, None]
    segment_mask = keep_mask.reshape(docs * SEGS, SEG)
    inner_rows = block(rows.reshape(docs * SEGS, SEG, D), segment_mask, weights[0:12])
    inner_rows = inner_rows.reshape(docs * SEGS, SEG, D)
    heads_in = low(inner_rows[:, 0, :].reshape(docs, SEGS, D) + jnp.transpose(weights[24])[None])
    outer_out = block(heads_in, None, weights[12:24])
    joined = jnp.concatenate([outer_out.reshape(docs * SEGS, 1, D), inner_rows[:, 1:]], axis=1)
    joined = joined * segment_mask.astype(jnp.float32)[:, :, None]
    return joined.reshape(docs * SLOTS, D)

def reference(tokens, counts, inner_attend, inner_attend_bias, inner_merge, inner_merge_bias, inner_gain, inner_shift, inner_expand, inner_expand_bias, inner_reduce, inner_reduce_bias, inner_final_gain, inner_final_shift, outer_attend, outer_attend_bias, outer_merge, outer_merge_bias, outer_gain, outer_shift, outer_expand, outer_expand_bias, outer_reduce, outer_reduce_bias, outer_final_gain, outer_final_shift, segment_place, cotangent):
    params = tuple((entry.astype(jnp.float32) for entry in (inner_attend, inner_attend_bias, inner_merge, inner_merge_bias, inner_gain, inner_shift, inner_expand, inner_expand_bias, inner_reduce, inner_reduce_bias, inner_final_gain, inner_final_shift, outer_attend, outer_attend_bias, outer_merge, outer_merge_bias, outer_gain, outer_shift, outer_expand, outer_expand_bias, outer_reduce, outer_reduce_bias, outer_final_gain, outer_final_shift, segment_place)))
    batch_docs = 4 if DOCS % 4 == 0 else 1
    turns = DOCS // batch_docs
    source = tokens.astype(jnp.float32).reshape(turns, batch_docs * SLOTS, D)
    lengths_all = counts.reshape(turns, batch_docs)
    seeds = cotangent.astype(jnp.float32).reshape(turns, batch_docs * SLOTS, D)

    def advance(carry, entry):
        rows, lengths, seed_rows = entry

        def forward(rows_in, weights):
            return forward_docs(rows_in, lengths, weights)
        result, pull = jax.vjp(forward, rows, params)
        grad_rows, grad_params = pull(seed_rows)
        carry = jax.tree.map(lambda left_sum, right_sum: left_sum + right_sum, carry, grad_params)
        return (carry, (result.astype(jnp.bfloat16), grad_rows))
    start = jax.tree.map(jnp.zeros_like, params)
    totals, outputs = lax.scan(advance, start, (source, lengths_all, seeds))
    mixed = outputs[0].reshape(TOKENS, D)
    tokens_grad = outputs[1].reshape(TOKENS, D)
    return (mixed, tokens_grad, totals[0], totals[1], totals[2], totals[3], totals[4], totals[5], totals[6], totals[7], totals[8], totals[9], totals[10], totals[11], totals[12], totals[13], totals[14], totals[15], totals[16], totals[17], totals[18], totals[19], totals[20], totals[21], totals[22], totals[23], totals[24])
```

```python
from functools import partial

import jax
import jax.numpy as jnp
from jax import lax
from jax.sharding import PartitionSpec as P

D = 768
HEADS = 12
HD = 64
SEG = 128
SLOTS = 1024
SEGS = 8


def norm_apply(rows, norm_gain, norm_shift):
    centre = jnp.mean(rows, axis=-1, keepdims=True)
    centred = rows - centre
    spread = jnp.mean(centred * centred, axis=-1, keepdims=True)
    return centred * lax.rsqrt(spread + 1e-05) * norm_gain + norm_shift


def prepare(group):
    return tuple(
        (
            entry if place_index in (0, 2, 6, 8) else entry.astype(jnp.float32)
            for place_index, entry in enumerate(group)
        )
    )


def cross_rows(left_rows, right_rows):
    return lax.dot_general(
        left_rows, right_rows, (((0,), (0,)), ((), ())), preferred_element_type=jnp.float32
    )


def back_cols(left_rows, right_rows):
    return lax.dot_general(
        left_rows, right_rows, (((1,), (1,)), ((), ())), preferred_element_type=jnp.float32
    )


def block_forward(source, source_float, key_mask, weights):
    (
        attend,
        attend_bias,
        merge,
        merge_bias,
        norm_gain,
        norm_shift,
        expand,
        expand_bias,
        reduce_matrix,
        reduce_bias,
        final_gain,
        final_shift,
    ) = weights
    groups, length, row_width = source.shape
    source_rows = source.reshape(groups * length, row_width)
    projected = (
        jnp.dot(source_rows, attend, preferred_element_type=jnp.float32) + attend_bias
    ).astype(jnp.bfloat16)
    projected = projected.reshape(groups, length, 3, HEADS, HD)
    query_heads = projected[:, :, 0]
    key_heads = projected[:, :, 1]
    value_heads = projected[:, :, 2]
    scores = jnp.einsum(
        "gqhe,gkhe->ghqk", query_heads, key_heads, preferred_element_type=jnp.float32
    ) * HD ** (-0.5)
    if key_mask is not None:
        scores = jnp.where(key_mask[:, None, None, :], scores, -1e30)
    softmax_out = jax.nn.softmax(scores, axis=-1)
    probs_low = softmax_out.astype(jnp.bfloat16)
    context = jnp.einsum(
        "ghqk,gkhe->gqhe", probs_low, value_heads, preferred_element_type=jnp.float32
    )
    context = context.astype(jnp.bfloat16).reshape(groups * length, row_width)
    first_sum = (
        source_float.reshape(groups * length, row_width)
        + jnp.dot(context, merge, preferred_element_type=jnp.float32)
        + merge_bias
    )
    normed = norm_apply(first_sum, norm_gain, norm_shift).astype(jnp.bfloat16)
    hidden = jnp.dot(normed, expand, preferred_element_type=jnp.float32) + expand_bias
    active = jax.nn.gelu(hidden, approximate=False).astype(jnp.bfloat16)
    second_sum = (
        normed.astype(jnp.float32)
        + jnp.dot(active, reduce_matrix, preferred_element_type=jnp.float32)
        + reduce_bias
    )
    result = norm_apply(second_sum, final_gain, final_shift)
    saved = (
        source_rows,
        query_heads,
        key_heads,
        value_heads,
        softmax_out,
        probs_low,
        context,
        first_sum,
        normed,
        hidden,
        active,
        second_sum,
    )
    return (result, saved)


def block_backward(grad_out, saved, weights, factors_only):
    (
        attend,
        attend_bias,
        merge,
        merge_bias,
        norm_gain,
        norm_shift,
        expand,
        expand_bias,
        reduce_matrix,
        reduce_bias,
        final_gain,
        final_shift,
    ) = weights
    (
        source_rows,
        query_heads,
        key_heads,
        value_heads,
        softmax_out,
        probs_low,
        context,
        first_sum,
        normed,
        hidden,
        active,
        second_sum,
    ) = saved
    groups, length = (query_heads.shape[0], query_heads.shape[1])
    row_width = source_rows.shape[1]
    scale = HD ** (-0.5)
    _, pull_final = jax.vjp(norm_apply, second_sum, final_gain, final_shift)
    grad_second, grad_final_gain, grad_final_shift = pull_final(grad_out)
    grad_branch = grad_second.astype(jnp.bfloat16)
    _, pull_gelu = jax.vjp(partial(jax.nn.gelu, approximate=False), hidden)
    grad_hidden = pull_gelu(back_cols(grad_branch, reduce_matrix))[0].astype(jnp.bfloat16)
    grad_normed = grad_second + back_cols(grad_hidden, expand)
    _, pull_first = jax.vjp(norm_apply, first_sum, norm_gain, norm_shift)
    grad_first, grad_gain, grad_shift = pull_first(grad_normed)
    grad_attn = grad_first.astype(jnp.bfloat16)
    grad_context = (
        back_cols(grad_attn, merge).astype(jnp.bfloat16).reshape(groups, length, HEADS, HD)
    )
    grad_values = jnp.einsum(
        "ghqk,gqhe->gkhe", probs_low, grad_context, preferred_element_type=jnp.float32
    )
    grad_probs = jnp.einsum(
        "gqhe,gkhe->ghqk", grad_context, value_heads, preferred_element_type=jnp.float32
    )
    row_total = jnp.sum(grad_probs * softmax_out, axis=-1, keepdims=True)
    grad_scores = (softmax_out * (grad_probs - row_total)).astype(jnp.bfloat16)
    grad_query = (
        jnp.einsum("ghqk,gkhe->gqhe", grad_scores, key_heads, preferred_element_type=jnp.float32)
        * scale
    )
    grad_key = (
        jnp.einsum("ghqk,gqhe->gkhe", grad_scores, query_heads, preferred_element_type=jnp.float32)
        * scale
    )
    grad_projected = jnp.stack([grad_query, grad_key, grad_values], axis=2)
    grad_projected = grad_projected.reshape(groups * length, 3 * row_width).astype(jnp.bfloat16)
    grad_source = grad_first + back_cols(grad_projected, attend)
    if factors_only:
        return (
            grad_source,
            (
                (source_rows, context, normed, active),
                (grad_projected, grad_attn, grad_hidden, grad_branch),
            ),
            (grad_gain, grad_shift, grad_final_gain, grad_final_shift),
        )
    return (
        grad_source,
        (
            cross_rows(source_rows, grad_projected),
            jnp.sum(grad_projected.astype(jnp.float32), axis=0),
            cross_rows(context, grad_attn),
            jnp.sum(grad_attn.astype(jnp.float32), axis=0),
            grad_gain,
            grad_shift,
            cross_rows(normed, grad_hidden),
            jnp.sum(grad_hidden.astype(jnp.float32), axis=0),
            cross_rows(active, grad_branch),
            jnp.sum(grad_branch.astype(jnp.float32), axis=0),
            grad_final_gain,
            grad_final_shift,
        ),
    )


AXES = ("dp", "fsdp")


def gather(rows):
    return lax.all_gather(rows, AXES, axis=0, tiled=True)


def scatter(rows):
    return lax.psum_scatter(rows, AXES, scatter_dimension=0, tiled=True)


def split_cols(packed, widths):
    pieces, start = [], 0
    for width in widths:
        pieces.append(packed[..., start : start + width])
        start += width
    return pieces


def on_device(
    tokens,
    counts,
    inner_attend,
    inner_attend_bias,
    inner_merge,
    inner_merge_bias,
    inner_gain,
    inner_shift,
    inner_expand,
    inner_expand_bias,
    inner_reduce,
    inner_reduce_bias,
    inner_final_gain,
    inner_final_shift,
    outer_attend,
    outer_attend_bias,
    outer_merge,
    outer_merge_bias,
    outer_gain,
    outer_shift,
    outer_expand,
    outer_expand_bias,
    outer_reduce,
    outer_reduce_bias,
    outer_final_gain,
    outer_final_shift,
    segment_place,
    cotangent,
):
    parts = inner_merge.shape[0]
    devices = D // parts
    ratio = inner_reduce.shape[0] // parts
    here = lax.axis_index(AXES)
    small_parts = (
        inner_attend_bias,
        inner_merge_bias,
        inner_gain,
        inner_shift,
        inner_expand_bias,
        inner_reduce_bias,
        inner_final_gain,
        inner_final_shift,
        outer_attend_bias,
        outer_merge_bias,
        outer_gain,
        outer_shift,
        outer_expand_bias,
        outer_reduce_bias,
        outer_final_gain,
        outer_final_shift,
        segment_place.reshape(parts * SEGS),
    )
    small_widths = [part.shape[0] for part in small_parts]
    small = gather(jnp.concatenate(small_parts)[None])
    small = [piece.reshape(-1) for piece in split_cols(small, small_widths)]
    place_table = small[16].reshape(D, SEGS).astype(jnp.float32)

    def rest_pack(merge, expand, reduce_matrix):
        return jnp.concatenate([merge, expand, fold(reduce_matrix)], axis=1)

    def fold(reduce_rows):
        return jnp.concatenate(jnp.split(reduce_rows, ratio, axis=0), axis=1)

    def unfold(packed):
        return jnp.transpose(packed.reshape(devices, parts, ratio, D), (0, 2, 1, 3)).reshape(
            devices * parts * ratio, D
        )

    def refold(grad):
        return jnp.transpose(grad.reshape(devices, ratio, parts, D), (0, 2, 1, 3)).reshape(
            D, ratio * D
        )

    wide = inner_expand.shape[1]
    inner_attend_full = gather(inner_attend)
    merge_full, expand_full, reduce_full = split_cols(
        gather(rest_pack(inner_merge, inner_expand, inner_reduce)), (D, wide, ratio * D)
    )
    inner_weights = prepare(
        (inner_attend_full, small[0], merge_full, small[1], small[2], small[3], expand_full)
        + (small[4], unfold(reduce_full), small[5], small[6], small[7])
    )
    attend_full, merge_full, expand_full, reduce_full = split_cols(
        gather(
            jnp.concatenate(
                [outer_attend, rest_pack(outer_merge, outer_expand, outer_reduce)], axis=1
            )
        ),
        (3 * D, D, wide, ratio * D),
    )
    outer_weights = prepare(
        (attend_full, small[8], merge_full, small[9], small[10], small[11], expand_full)
        + (small[12], unfold(reduce_full), small[13], small[14], small[15])
    )
    docs = counts.shape[0]
    keep_mask = jnp.arange(SLOTS)[None, :] < counts[:, None]
    segment_mask = keep_mask.reshape(docs * SEGS, SEG)
    keep_float = segment_mask.astype(jnp.float32)[:, :, None]
    token_groups = tokens.reshape(docs * SEGS, SEG, D)
    inner_out, inner_saved = block_forward(
        token_groups, token_groups.astype(jnp.float32), segment_mask, inner_weights
    )
    inner_rows = inner_out.reshape(docs * SEGS, SEG, D)
    heads_in = (
        inner_rows[:, 0, :].reshape(docs, SEGS, D) + jnp.transpose(place_table)[None]
    ).astype(jnp.bfloat16)
    outer_out, outer_saved = block_forward(
        heads_in, heads_in.astype(jnp.float32), None, outer_weights
    )
    joined = (
        jnp.concatenate([outer_out.reshape(docs * SEGS, 1, D), inner_rows[:, 1:]], axis=1)
        * keep_float
    )
    mixed = joined.reshape(docs * SLOTS, D).astype(jnp.bfloat16)
    grad_joined = cotangent.astype(jnp.float32).reshape(docs * SEGS, SEG, D) * keep_float
    grad_heads, outer_factors, outer_sums = block_backward(grad_joined[:, 0, :], outer_saved, outer_weights, True)
    grad_place = jnp.transpose(jnp.sum(grad_heads.reshape(docs, SEGS, D), axis=0))
    grad_inner_rows = jnp.concatenate(
        [grad_heads.reshape(docs * SEGS, 1, D), grad_joined[:, 1:]], axis=1
    )
    tokens_grad, inner_grads = block_backward(
        grad_inner_rows.reshape(docs * SLOTS, D), inner_saved, inner_weights, False
    )
    left_pack = jnp.concatenate(
        [factor.reshape(factor.shape[0], devices, -1) for factor in outer_factors[0]], axis=2
    )
    left_pack = jnp.transpose(left_pack, (1, 0, 2))
    left_all = lax.all_to_all(left_pack, AXES, split_axis=0, concat_axis=0, tiled=True)
    left_all = left_all.reshape(-1, left_all.shape[-1])
    right_all = gather(jnp.concatenate(outer_factors[1], axis=1))
    left_pieces = split_cols(left_all, (parts, parts, parts, parts * ratio))
    right_pieces = split_cols(right_all, (3 * D, D, wide, D))
    outer_big = [cross_rows(left, right) for left, right in zip(left_pieces, right_pieces)]
    outer_bias = [
        lax.dynamic_slice_in_dim(
            jnp.sum(right.astype(jnp.float32), axis=0), here * width, width, axis=0
        )
        for right, width in zip(
            right_pieces, (3 * parts, parts, wide // devices, parts)
        )
    ]
    (
        grad_attend,
        grad_attend_bias,
        grad_merge,
        grad_merge_bias,
        grad_gain,
        grad_shift,
        grad_expand,
        grad_expand_bias,
        grad_reduce,
        grad_reduce_bias,
        grad_final_gain,
        grad_final_shift,
    ) = inner_grads
    tall_pack = scatter(
        jnp.concatenate([grad_expand, refold(grad_reduce)], axis=1).astype(jnp.bfloat16)
    ).astype(jnp.float32)
    head_pack = scatter(
        jnp.concatenate([grad_attend, grad_merge], axis=1).astype(jnp.bfloat16)
    ).astype(jnp.float32)
    row_sums = (
        grad_attend_bias,
        grad_merge_bias,
        grad_gain,
        grad_shift,
        grad_expand_bias,
        grad_reduce_bias,
        grad_final_gain,
        grad_final_shift,
    ) + outer_sums + (grad_place,)
    sums = scatter(
        jnp.concatenate([entry.reshape(devices, -1) for entry in row_sums], axis=1)
    ).reshape(-1)
    sums = split_cols(sums, [entry.size // devices for entry in row_sums])
    own_expand, own_reduce = split_cols(tall_pack, (wide, ratio * D))
    own_reduce = jnp.concatenate(jnp.split(own_reduce, ratio, axis=1), axis=0)
    own_attend, own_merge = split_cols(head_pack, (3 * D, D))
    return (
        mixed,
        tokens_grad,
        own_attend,
        sums[0],
        own_merge,
        sums[1],
        sums[2],
        sums[3],
        own_expand,
        sums[4],
        own_reduce,
        sums[5],
        sums[6],
        sums[7],
        outer_big[0],
        outer_bias[0],
        outer_big[1],
        outer_bias[1],
        sums[8],
        sums[9],
        outer_big[2],
        outer_bias[2],
        outer_big[3],
        outer_bias[3],
        sums[10],
        sums[11],
        sums[12].reshape(parts, SEGS),
    )


def solution(mesh):
    return jax.shard_map(
        on_device,
        mesh=mesh,
        in_specs=(
            P(("dp", "fsdp"), None),
            P(("dp", "fsdp")),
            P(("dp", "fsdp"), None),
            P(("dp", "fsdp")),
            P(("dp", "fsdp"), None),
            P(("dp", "fsdp")),
            P(("dp", "fsdp")),
            P(("dp", "fsdp")),
            P(("dp", "fsdp"), None),
            P(("dp", "fsdp")),
            P(("dp", "fsdp"), None),
            P(("dp", "fsdp")),
            P(("dp", "fsdp")),
            P(("dp", "fsdp")),
            P(("dp", "fsdp"), None),
            P(("dp", "fsdp")),
            P(("dp", "fsdp"), None),
            P(("dp", "fsdp")),
            P(("dp", "fsdp")),
            P(("dp", "fsdp")),
            P(("dp", "fsdp"), None),
            P(("dp", "fsdp")),
            P(("dp", "fsdp"), None),
            P(("dp", "fsdp")),
            P(("dp", "fsdp")),
            P(("dp", "fsdp")),
            P(("dp", "fsdp"), None),
            P(("dp", "fsdp"), None),
        ),
        out_specs=(
            P(("dp", "fsdp"), None),
            P(("dp", "fsdp"), None),
            P(("dp", "fsdp"), None),
            P(("dp", "fsdp")),
            P(("dp", "fsdp"), None),
            P(("dp", "fsdp")),
            P(("dp", "fsdp")),
            P(("dp", "fsdp")),
            P(("dp", "fsdp"), None),
            P(("dp", "fsdp")),
            P(("dp", "fsdp"), None),
            P(("dp", "fsdp")),
            P(("dp", "fsdp")),
            P(("dp", "fsdp")),
            P(("dp", "fsdp"), None),
            P(("dp", "fsdp")),
            P(("dp", "fsdp"), None),
            P(("dp", "fsdp")),
            P(("dp", "fsdp")),
            P(("dp", "fsdp")),
            P(("dp", "fsdp"), None),
            P(("dp", "fsdp")),
            P(("dp", "fsdp"), None),
            P(("dp", "fsdp")),
            P(("dp", "fsdp")),
            P(("dp", "fsdp")),
            P(("dp", "fsdp"), None),
        ),
        check_vma=False,
    )
```

```python
from functools import partial

import jax
import jax.numpy as jnp
from jax import lax
from jax.experimental import pallas as pl
from jax.experimental.pallas import tpu as pltpu
from jax.sharding import PartitionSpec as P

D = 768
HEADS = 12
HD = 64
SEG = 128
SLOTS = 1024
SEGS = 8


def norm_apply(rows, norm_gain, norm_shift):
    centre = jnp.mean(rows, axis=-1, keepdims=True)
    centred = rows - centre
    spread = jnp.mean(centred * centred, axis=-1, keepdims=True)
    return centred * lax.rsqrt(spread + 1e-05) * norm_gain + norm_shift


def prepare(group):
    return tuple(
        (
            entry if place_index in (0, 2, 6, 8) else entry.astype(jnp.float32)
            for place_index, entry in enumerate(group)
        )
    )


def cross_rows(left_rows, right_rows):
    return lax.dot_general(
        left_rows, right_rows, (((0,), (0,)), ((), ())), preferred_element_type=jnp.float32
    )


def back_cols(left_rows, right_rows):
    return lax.dot_general(
        left_rows, right_rows, (((1,), (1,)), ((), ())), preferred_element_type=jnp.float32
    )


def block_forward(source, source_float, key_mask, weights):
    (
        attend,
        attend_bias,
        merge,
        merge_bias,
        norm_gain,
        norm_shift,
        expand,
        expand_bias,
        reduce_matrix,
        reduce_bias,
        final_gain,
        final_shift,
    ) = weights
    groups, length, row_width = source.shape
    source_rows = source.reshape(groups * length, row_width)
    projected = (
        jnp.dot(source_rows, attend, preferred_element_type=jnp.float32) + attend_bias
    ).astype(jnp.bfloat16)
    projected = projected.reshape(groups, length, 3, HEADS, HD)
    query_heads = projected[:, :, 0]
    key_heads = projected[:, :, 1]
    value_heads = projected[:, :, 2]
    scores = jnp.einsum(
        "gqhe,gkhe->ghqk", query_heads, key_heads, preferred_element_type=jnp.float32
    ) * HD ** (-0.5)
    if key_mask is not None:
        scores = jnp.where(key_mask[:, None, None, :], scores, -1e30)
    softmax_out = jax.nn.softmax(scores, axis=-1)
    probs_low = softmax_out.astype(jnp.bfloat16)
    context = jnp.einsum(
        "ghqk,gkhe->gqhe", probs_low, value_heads, preferred_element_type=jnp.float32
    )
    context = context.astype(jnp.bfloat16).reshape(groups * length, row_width)
    first_sum = (
        source_float.reshape(groups * length, row_width)
        + jnp.dot(context, merge, preferred_element_type=jnp.float32)
        + merge_bias
    )
    normed = norm_apply(first_sum, norm_gain, norm_shift).astype(jnp.bfloat16)
    hidden = jnp.dot(normed, expand, preferred_element_type=jnp.float32) + expand_bias
    active = jax.nn.gelu(hidden, approximate=False).astype(jnp.bfloat16)
    second_sum = (
        normed.astype(jnp.float32)
        + jnp.dot(active, reduce_matrix, preferred_element_type=jnp.float32)
        + reduce_bias
    )
    result = norm_apply(second_sum, final_gain, final_shift)
    saved = (
        source_rows,
        query_heads,
        key_heads,
        value_heads,
        softmax_out,
        probs_low,
        context,
        first_sum,
        normed,
        hidden,
        active,
        second_sum,
    )
    return (result, saved)


def block_backward(grad_out, saved, weights, factors_only):
    (
        attend,
        attend_bias,
        merge,
        merge_bias,
        norm_gain,
        norm_shift,
        expand,
        expand_bias,
        reduce_matrix,
        reduce_bias,
        final_gain,
        final_shift,
    ) = weights
    (
        source_rows,
        query_heads,
        key_heads,
        value_heads,
        softmax_out,
        probs_low,
        context,
        first_sum,
        normed,
        hidden,
        active,
        second_sum,
    ) = saved
    groups, length = (query_heads.shape[0], query_heads.shape[1])
    row_width = source_rows.shape[1]
    scale = HD ** (-0.5)
    _, pull_final = jax.vjp(norm_apply, second_sum, final_gain, final_shift)
    grad_second, grad_final_gain, grad_final_shift = pull_final(grad_out)
    grad_branch = grad_second.astype(jnp.bfloat16)
    _, pull_gelu = jax.vjp(partial(jax.nn.gelu, approximate=False), hidden)
    grad_hidden = pull_gelu(back_cols(grad_branch, reduce_matrix))[0].astype(jnp.bfloat16)
    grad_normed = grad_second + back_cols(grad_hidden, expand)
    _, pull_first = jax.vjp(norm_apply, first_sum, norm_gain, norm_shift)
    grad_first, grad_gain, grad_shift = pull_first(grad_normed)
    grad_attn = grad_first.astype(jnp.bfloat16)
    grad_context = (
        back_cols(grad_attn, merge).astype(jnp.bfloat16).reshape(groups, length, HEADS, HD)
    )
    grad_values = jnp.einsum(
        "ghqk,gqhe->gkhe", probs_low, grad_context, preferred_element_type=jnp.float32
    )
    grad_probs = jnp.einsum(
        "gqhe,gkhe->ghqk", grad_context, value_heads, preferred_element_type=jnp.float32
    )
    row_total = jnp.sum(grad_probs * softmax_out, axis=-1, keepdims=True)
    grad_scores = (softmax_out * (grad_probs - row_total)).astype(jnp.bfloat16)
    grad_query = (
        jnp.einsum("ghqk,gkhe->gqhe", grad_scores, key_heads, preferred_element_type=jnp.float32)
        * scale
    )
    grad_key = (
        jnp.einsum("ghqk,gqhe->gkhe", grad_scores, query_heads, preferred_element_type=jnp.float32)
        * scale
    )
    grad_projected = jnp.stack([grad_query, grad_key, grad_values], axis=2)
    grad_projected = grad_projected.reshape(groups * length, 3 * row_width).astype(jnp.bfloat16)
    grad_source = grad_first + back_cols(grad_projected, attend)
    if factors_only:
        return (
            grad_source,
            (
                (source_rows, context, normed, active),
                (grad_projected, grad_attn, grad_hidden, grad_branch),
            ),
            (grad_gain, grad_shift, grad_final_gain, grad_final_shift),
        )
    return (
        grad_source,
        (
            cross_rows(source_rows, grad_projected),
            jnp.sum(grad_projected.astype(jnp.float32), axis=0),
            cross_rows(context, grad_attn),
            jnp.sum(grad_attn.astype(jnp.float32), axis=0),
            grad_gain,
            grad_shift,
            cross_rows(normed, grad_hidden),
            jnp.sum(grad_hidden.astype(jnp.float32), axis=0),
            cross_rows(active, grad_branch),
            jnp.sum(grad_branch.astype(jnp.float32), axis=0),
            grad_final_gain,
            grad_final_shift,
        ),
    )


AXES = ("dp", "fsdp")


def gather(rows):
    return lax.all_gather(rows, AXES, axis=0, tiled=True)


def scatter(rows):
    return lax.psum_scatter(rows, AXES, scatter_dimension=0, tiled=True)


def split_cols(packed, widths):
    pieces, start = [], 0
    for width in widths:
        pieces.append(packed[..., start : start + width])
        start += width
    return pieces


def everyone(rows):
    devices = lax.axis_size(AXES)
    padded = jnp.pad(rows, ((0, -rows.shape[0] % 16), (0, 0)))[None]
    sent = jnp.broadcast_to(padded, (devices,) + padded.shape[1:])
    return lax.all_to_all(sent, AXES, split_axis=0, concat_axis=0, tiled=True)


def sum_rows(rows):
    devices, size = rows.shape
    padded = jnp.pad(rows, ((0, 0), (0, -size % 1024))).reshape(devices, -1, 128)
    got = lax.all_to_all(padded, AXES, split_axis=0, concat_axis=0, tiled=True)
    return jnp.sum(got, axis=0).reshape(-1)[:size]


def hop(array, turn):
    return lax.ppermute(array, AXES, [(place, turn(place)) for place in range(32)])


def over_x(array):
    return hop(array, lambda place: place ^ 8)


def over_y(array):
    return hop(array, lambda place: place ^ 16)


def over_core(array):
    return hop(array, lambda place: place ^ 1)


def over_z(array, step):
    return hop(array, lambda place: (place & ~6) | ((((place >> 1) + step) & 3) << 1))


def place_here():
    chip = lax.axis_index("fsdp")
    return lax.axis_index("dp"), chip // 2, chip % 2


def half_cols(array, core):
    width = array.shape[-1] // 2
    return lax.dynamic_slice_in_dim(array, core * width, width, axis=array.ndim - 1)


def fold_rows(array, rows):
    return jnp.concatenate(jnp.split(array, array.shape[0] // rows, axis=0), axis=1)


def unfold_cols(array, width):
    return jnp.concatenate(jnp.split(array, array.shape[1] // width, axis=1), axis=0)


def both_cores(mine, other, core, axis):
    return jnp.concatenate(
        [jnp.where(core == 0, mine, other), jnp.where(core == 0, other, mine)], axis=axis
    )


def assemble_kernel(heights, widths, place_ref, *refs):
    pieces, outs, sems = refs[:10], refs[10:-1], refs[-1]
    plane, depth, core = place_ref[0], place_ref[1], place_ref[2]
    slots = ((0, 0, 4), (1, 0, 4), (2, 0, 4), (3, 0, 2), (3, 2, 2))
    copies = []
    for side in range(2):
        column = core if side == 0 else 1 - core
        for number, (turn, first, count) in enumerate(slots):
            piece = pieces[5 * side + number]
            for slot in range(count):
                chip = (plane ^ turn) * 4 + ((depth + 4 - first - slot) & 3)
                start = 0
                for out, height, width in zip(outs, heights, widths):
                    for group in range(height // 48):
                        row = pl.multiple_of(chip * height + 48 * group, 48)
                        lane = pl.multiple_of(column * width, 128)
                        copies.append(
                            pltpu.make_async_copy(
                                piece.at[slot, :, pl.ds(start, width)],
                                out.at[pl.ds(row, 48), pl.ds(lane, width)],
                                sems.at[len(copies)],
                            )
                        )
                        start += width
    for copy in copies:
        copy.start()
    for copy in copies:
        copy.wait()


def gather_links(shards):
    plane, depth, core = place_here()
    rows = min(shard.shape[0] for shard in shards)
    mine = jnp.concatenate([fold_rows(half_cols(shard, core), rows) for shard in shards], axis=1)
    sent = jnp.concatenate(
        [fold_rows(half_cols(shard, 1 - core), rows) for shard in shards], axis=1
    )
    other = over_core(sent)
    widths = [shard.shape[1] // 2 for shard in shards]
    heights = [2 * shard.shape[0] for shard in shards]
    slab, start = [], 0
    for width, height in zip(widths, heights):
        span = width * (height // (2 * rows))
        pair = [unfold_cols(part[:, start : start + span], width) for part in (mine, other)]
        slab.append(fold_rows(both_cores(pair[0], pair[1], core, 0), 2 * rows))
        start += span
    slab = jnp.concatenate(slab, axis=1)
    line = jnp.stack([slab] + [over_z(slab, step) for step in (1, 2, 3)])
    line_x, line_y = over_x(line), over_y(line)
    pieces = [line, line_x, line_y, over_y(line_x[:2]), over_x(line_y[2:])]
    pieces = pieces + [over_core(piece) for piece in pieces]
    count = 32 * sum(height // 48 for height in heights)
    place = jnp.stack([plane, depth, core]).astype(jnp.int32)
    return pl.pallas_call(
        partial(assemble_kernel, heights, widths),
        out_shape=[
            jax.ShapeDtypeStruct((16 * height, 2 * width), jnp.bfloat16)
            for height, width in zip(heights, widths)
        ],
        in_specs=[pl.BlockSpec(memory_space=pltpu.SMEM)]
        + [pl.BlockSpec(memory_space=pl.ANY)] * 10,
        out_specs=[pl.BlockSpec(memory_space=pltpu.VMEM)] * len(shards),
        scratch_shapes=[pltpu.SemaphoreType.DMA((count,))],
        compiler_params=pltpu.CompilerParams(vmem_limit_bytes=32 << 20),
        name="assemble",
    )(place, *pieces)


def scatter_links(grads):
    plane, depth, core = place_here()
    low = jnp.bfloat16

    def packed(side):
        return jnp.concatenate(
            [
                jnp.transpose(
                    half_cols(grad, side).reshape(16, grad.shape[0] // 768, 48, -1), (0, 2, 1, 3)
                ).reshape(16, 48, -1)
                for grad in grads
            ],
            axis=2,
        )

    kept = (packed(core) + over_core(packed(1 - core))).reshape(4, 4, 48, -1)
    here, next_x, next_y, across = [
        lax.dynamic_index_in_dim(kept, plane ^ turn, axis=0, keepdims=False)
        for turn in range(4)
    ]
    from_y, from_x = over_y(across[:2]), over_x(across[2:])
    next_x = jnp.concatenate([next_x[:2] + from_y, next_x[2:]], axis=0)
    next_y = jnp.concatenate([next_y[:2], next_y[2:] + from_x], axis=0)
    came_x, came_y = over_x(next_x), over_y(next_y)
    here = (
        here.astype(jnp.float32) + came_x.astype(jnp.float32) + came_y.astype(jnp.float32)
    ).astype(low)
    slabs = [
        lax.dynamic_index_in_dim(here, (depth + step) & 3, axis=0, keepdims=False)
        for step in range(4)
    ]
    total = slabs[0].astype(jnp.float32)
    for step in (1, 2, 3):
        total = total + over_z(slabs[step], step).astype(jnp.float32)
    mine, sent, start = [], [], 0
    for grad in grads:
        width = grad.shape[1] // 2
        groups = grad.shape[0] // 768
        rows = unfold_cols(total[:, start : start + groups * width], width)
        start += groups * width
        mine.append(fold_rows(lax.dynamic_slice_in_dim(rows, core * 24 * groups, 24 * groups), 24))
        sent.append(
            fold_rows(lax.dynamic_slice_in_dim(rows, (1 - core) * 24 * groups, 24 * groups), 24)
        )
    other = over_core(jnp.concatenate(sent, axis=1))
    owned, start = [], 0
    for grad, part in zip(grads, mine):
        width = grad.shape[1] // 2
        pair = [unfold_cols(side, width) for side in (part, other[:, start : start + part.shape[1]])]
        owned.append(both_cores(pair[0], pair[1], core, 1))
        start += part.shape[1]
    return owned


def unfold(packed, parts, ratio):
    width = packed.shape[1] // ratio
    return jnp.stack(
        [
            packed[:, width * group : width * (group + 1)].reshape(-1, parts, width)
            for group in range(ratio)
        ],
        axis=1,
    ).reshape(-1, width)


def gather_flat(shards):
    parts = min(shard.shape[0] for shard in shards)
    pieces = split_cols(
        gather(jnp.concatenate([fold_rows(shard, parts) for shard in shards], axis=1)),
        [shard.size // parts for shard in shards],
    )
    return [
        unfold(piece, parts, shard.shape[0] // parts) if shard.shape[0] > parts else piece
        for piece, shard in zip(pieces, shards)
    ]


def scatter_flat(grads):
    devices = lax.axis_size(AXES)
    parts = min(grad.shape[0] for grad in grads) // devices
    packed = jnp.concatenate(
        [
            jnp.transpose(grad.reshape(devices, -1, parts, grad.shape[1]), (0, 2, 1, 3)).reshape(
                devices * parts, -1
            )
            for grad in grads
        ],
        axis=1,
    )
    owned = split_cols(
        scatter(packed).astype(jnp.float32), [grad.size // (devices * parts) for grad in grads]
    )
    return [unfold_cols(piece, grad.shape[1]) for piece, grad in zip(owned, grads)]


def on_device(
    tokens,
    counts,
    inner_attend,
    inner_attend_bias,
    inner_merge,
    inner_merge_bias,
    inner_gain,
    inner_shift,
    inner_expand,
    inner_expand_bias,
    inner_reduce,
    inner_reduce_bias,
    inner_final_gain,
    inner_final_shift,
    outer_attend,
    outer_attend_bias,
    outer_merge,
    outer_merge_bias,
    outer_gain,
    outer_shift,
    outer_expand,
    outer_expand_bias,
    outer_reduce,
    outer_reduce_bias,
    outer_final_gain,
    outer_final_shift,
    segment_place,
    cotangent,
):
    parts = inner_merge.shape[0]
    devices = D // parts
    ratio = inner_reduce.shape[0] // parts
    here = lax.axis_index(AXES)
    small_parts = (
        inner_attend_bias,
        inner_merge_bias,
        inner_gain,
        inner_shift,
        inner_expand_bias,
        inner_reduce_bias,
        inner_final_gain,
        inner_final_shift,
        outer_attend_bias,
        outer_merge_bias,
        outer_gain,
        outer_shift,
        outer_expand_bias,
        outer_reduce_bias,
        outer_final_gain,
        outer_final_shift,
        segment_place.reshape(parts * SEGS),
    )
    small_widths = [part.shape[0] for part in small_parts]
    spread = everyone(
        jnp.concatenate(
            [jnp.pad(part, (0, -part.shape[0] % 128)).reshape(-1, 128) for part in small_parts]
        )
    )
    small, start = [], 0
    for width in small_widths:
        rows = -(-width // 128)
        piece = spread[:, start : start + rows].reshape(devices, -1)[:, :width]
        small.append(piece.reshape(-1))
        start += rows
    place_table = small[16].reshape(D, SEGS).astype(jnp.float32)
    linked = lax.axis_size("dp") == 4 and lax.axis_size("fsdp") == 8
    gather_inner = gather_links if linked else gather_flat
    scatter_inner = scatter_links if linked else scatter_flat
    wide = inner_expand.shape[1]
    (attend_full,) = gather_inner([inner_attend])
    merge_full, expand_full, reduce_full = gather_inner([inner_merge, inner_expand, inner_reduce])
    inner_weights = prepare(
        (attend_full, small[0], merge_full, small[1], small[2], small[3], expand_full)
        + (small[4], reduce_full, small[5], small[6], small[7])
    )
    outer_shards = lax.optimization_barrier(
        (attend_full, outer_attend, outer_merge, outer_expand, outer_reduce)
    )
    attend_full, merge_full, expand_full, reduce_full = gather_flat(outer_shards[1:])
    outer_weights = prepare(
        (attend_full, small[8], merge_full, small[9], small[10], small[11], expand_full)
        + (small[12], reduce_full, small[13], small[14], small[15])
    )
    docs = counts.shape[0]
    keep_mask = jnp.arange(SLOTS)[None, :] < counts[:, None]
    segment_mask = keep_mask.reshape(docs * SEGS, SEG)
    keep_float = segment_mask.astype(jnp.float32)[:, :, None]
    token_groups = tokens.reshape(docs * SEGS, SEG, D)
    inner_out, inner_saved = block_forward(
        token_groups, token_groups.astype(jnp.float32), segment_mask, inner_weights
    )
    inner_rows = inner_out.reshape(docs * SEGS, SEG, D)
    heads_in = (
        inner_rows[:, 0, :].reshape(docs, SEGS, D) + jnp.transpose(place_table)[None]
    ).astype(jnp.bfloat16)
    outer_out, outer_saved = block_forward(
        heads_in, heads_in.astype(jnp.float32), None, outer_weights
    )
    joined = (
        jnp.concatenate([outer_out.reshape(docs * SEGS, 1, D), inner_rows[:, 1:]], axis=1)
        * keep_float
    )
    mixed = joined.reshape(docs * SLOTS, D).astype(jnp.bfloat16)
    grad_joined = cotangent.astype(jnp.float32).reshape(docs * SEGS, SEG, D) * keep_float
    grad_heads, outer_factors, outer_sums = block_backward(grad_joined[:, 0, :], outer_saved, outer_weights, True)
    grad_place = jnp.transpose(jnp.sum(grad_heads.reshape(docs, SEGS, D), axis=0))
    grad_inner_rows = jnp.concatenate(
        [grad_heads.reshape(docs * SEGS, 1, D), grad_joined[:, 1:]], axis=1
    )
    tokens_grad, inner_grads = block_backward(
        grad_inner_rows.reshape(docs * SLOTS, D), inner_saved, inner_weights, False
    )
    left_pack = jnp.concatenate(
        [factor.reshape(factor.shape[0], devices, -1) for factor in outer_factors[0]], axis=2
    )
    left_pack = jnp.transpose(left_pack, (1, 0, 2))
    left_all = lax.all_to_all(left_pack, AXES, split_axis=0, concat_axis=0, tiled=True)
    left_all = left_all.reshape(-1, left_all.shape[-1])
    right_all = gather(jnp.concatenate(outer_factors[1], axis=1))
    left_pieces = split_cols(left_all, (parts, parts, parts, parts * ratio))
    right_pieces = split_cols(right_all, (3 * D, D, wide, D))
    outer_big = [cross_rows(left, right) for left, right in zip(left_pieces, right_pieces)]
    outer_bias = [
        lax.dynamic_slice_in_dim(
            jnp.sum(right.astype(jnp.float32), axis=0), here * width, width, axis=0
        )
        for right, width in zip(
            right_pieces, (3 * parts, parts, wide // devices, parts)
        )
    ]
    (
        grad_attend,
        grad_attend_bias,
        grad_merge,
        grad_merge_bias,
        grad_gain,
        grad_shift,
        grad_expand,
        grad_expand_bias,
        grad_reduce,
        grad_reduce_bias,
        grad_final_gain,
        grad_final_shift,
    ) = inner_grads
    own_expand, own_reduce = scatter_inner(
        [grad_expand.astype(jnp.bfloat16), grad_reduce.astype(jnp.bfloat16)]
    )
    own_attend, own_merge = scatter_inner(
        [grad_attend.astype(jnp.bfloat16), grad_merge.astype(jnp.bfloat16)]
    )
    row_sums = (
        grad_attend_bias,
        grad_merge_bias,
        grad_gain,
        grad_shift,
        grad_expand_bias,
        grad_reduce_bias,
        grad_final_gain,
        grad_final_shift,
    ) + outer_sums + (grad_place,)
    sums = sum_rows(jnp.concatenate([entry.reshape(devices, -1) for entry in row_sums], axis=1))
    sums = split_cols(sums, [entry.size // devices for entry in row_sums])
    return (
        mixed,
        tokens_grad,
        own_attend,
        sums[0],
        own_merge,
        sums[1],
        sums[2],
        sums[3],
        own_expand,
        sums[4],
        own_reduce,
        sums[5],
        sums[6],
        sums[7],
        outer_big[0],
        outer_bias[0],
        outer_big[1],
        outer_bias[1],
        sums[8],
        sums[9],
        outer_big[2],
        outer_bias[2],
        outer_big[3],
        outer_bias[3],
        sums[10],
        sums[11],
        sums[12].reshape(parts, SEGS),
    )


def solution(mesh):
    return jax.shard_map(
        on_device,
        mesh=mesh,
        in_specs=(
            P(("dp", "fsdp"), None),
            P(("dp", "fsdp")),
            P(("dp", "fsdp"), None),
            P(("dp", "fsdp")),
            P(("dp", "fsdp"), None),
            P(("dp", "fsdp")),
            P(("dp", "fsdp")),
            P(("dp", "fsdp")),
            P(("dp", "fsdp"), None),
            P(("dp", "fsdp")),
            P(("dp", "fsdp"), None),
            P(("dp", "fsdp")),
            P(("dp", "fsdp")),
            P(("dp", "fsdp")),
            P(("dp", "fsdp"), None),
            P(("dp", "fsdp")),
            P(("dp", "fsdp"), None),
            P(("dp", "fsdp")),
            P(("dp", "fsdp")),
            P(("dp", "fsdp")),
            P(("dp", "fsdp"), None),
            P(("dp", "fsdp")),
            P(("dp", "fsdp"), None),
            P(("dp", "fsdp")),
            P(("dp", "fsdp")),
            P(("dp", "fsdp")),
            P(("dp", "fsdp"), None),
            P(("dp", "fsdp"), None),
        ),
        out_specs=(
            P(("dp", "fsdp"), None),
            P(("dp", "fsdp"), None),
            P(("dp", "fsdp"), None),
            P(("dp", "fsdp")),
            P(("dp", "fsdp"), None),
            P(("dp", "fsdp")),
            P(("dp", "fsdp")),
            P(("dp", "fsdp")),
            P(("dp", "fsdp"), None),
            P(("dp", "fsdp")),
            P(("dp", "fsdp"), None),
            P(("dp", "fsdp")),
            P(("dp", "fsdp")),
            P(("dp", "fsdp")),
            P(("dp", "fsdp"), None),
            P(("dp", "fsdp")),
            P(("dp", "fsdp"), None),
            P(("dp", "fsdp")),
            P(("dp", "fsdp")),
            P(("dp", "fsdp")),
            P(("dp", "fsdp"), None),
            P(("dp", "fsdp")),
            P(("dp", "fsdp"), None),
            P(("dp", "fsdp")),
            P(("dp", "fsdp")),
            P(("dp", "fsdp")),
            P(("dp", "fsdp"), None),
        ),
        check_vma=False,
    )
```

```python
from functools import partial

import jax
import jax.numpy as jnp
from jax import lax
from jax.experimental import pallas as pl
from jax.experimental.pallas import tpu as pltpu
from jax.sharding import PartitionSpec as P

D = 768
HEADS = 12
HD = 64
SEG = 128
SLOTS = 1024
SEGS = 8


def cross_rows(left_rows, right_rows):
    return lax.dot_general(
        left_rows, right_rows, (((0,), (0,)), ((), ())), preferred_element_type=jnp.float32
    )


def back_cols(left_rows, right_rows):
    return lax.dot_general(
        left_rows, right_rows, (((1,), (1,)), ((), ())), preferred_element_type=jnp.float32
    )


ROWS = 256
PAIR = 2 * HD
PAIRS = HEADS // 2
F32 = jnp.float32
LOW = jnp.bfloat16


def dot_nn(left, right):
    return jnp.dot(left, right, preferred_element_type=F32)


def centre_rows(rows):
    centred = rows - jnp.mean(rows, axis=-1, keepdims=True)
    spread = lax.rsqrt(jnp.mean(centred * centred, axis=-1, keepdims=True) + 1e-05)
    return centred * spread, spread


def norm_back(grad, unit, spread):
    return spread * (
        grad
        - jnp.mean(grad, axis=-1, keepdims=True)
        - unit * jnp.mean(grad * unit, axis=-1, keepdims=True)
    )


def gelu_pair(hidden):
    size = jnp.abs(hidden)
    bell = jnp.exp(hidden * hidden * -0.5)
    t = 1.0 / (1.0 + (0.3275911 * 0.7071067811865476) * size)
    poly = t * (
        0.127414796
        + t * (-0.142248368 + t * (0.7107068705 + t * (-0.7265760135 + t * 0.5307027145)))
    )
    tail = poly * bell
    phi = jnp.where(hidden >= 0, 1.0 - tail, tail)
    return hidden * phi, phi + hidden * bell * 0.3989422804014327


def two_heads(pair, axis):
    first = lax.broadcasted_iota(jnp.int32, pair.shape, 1) < HD
    zero = jnp.zeros_like(pair)
    return jnp.concatenate([jnp.where(first, pair, zero), jnp.where(first, zero, pair)], axis=axis)


def pair_probs(query, key, valid):
    scores = back_cols(two_heads(query, 0), key) * HD ** (-0.5)
    scores = jnp.where(valid, scores, -1e30)
    weight = jnp.exp(scores - jnp.max(scores, axis=-1, keepdims=True))
    return weight / jnp.sum(weight, axis=-1, keepdims=True)


def side_by_side(stacked):
    half = stacked.shape[0] // 2
    return jnp.concatenate([stacked[:half], stacked[half:]], axis=1)


def valid_keys(count_ref, segment):
    position = lax.broadcasted_iota(jnp.int32, (1, SEG), 1)
    return position < count_ref[0] - segment * SEG


def attend_kernel(count_ref, rows_ref, attend_ref, bias_ref, projected_ref, context_ref):
    step = pl.program_id(0)
    projected_ref[...] = (dot_nn(rows_ref[...], attend_ref[...]) + bias_ref[...]).astype(LOW)
    for local in range(ROWS // SEG):
        valid = valid_keys(count_ref, step * (ROWS // SEG) + local)
        span = slice(local * SEG, (local + 1) * SEG)
        for pair in range(PAIRS):
            query, key, value = [
                projected_ref[span, part * D + pair * PAIR : part * D + (pair + 1) * PAIR]
                for part in range(3)
            ]
            probs = pair_probs(query, key, valid).astype(LOW)
            context_ref[span, pair * PAIR : (pair + 1) * PAIR] = dot_nn(
                side_by_side(probs), two_heads(value, 0)
            ).astype(LOW)


def put_row(ref, place, start, row):
    span = slice(start, start + row.shape[1])
    here = lax.broadcasted_iota(jnp.int32, (ref.shape[0], 1), 0) == place
    ref[:, span] = jnp.where(here, row, ref[:, span])


def get_row(ref, place, span):
    here = lax.broadcasted_iota(jnp.int32, (ref.shape[0], 1), 0) == place
    return jnp.sum(jnp.where(here, ref[:, span], 0.0), axis=0, keepdims=True)


def first_row(rows, segment):
    return rows[segment * SEG : segment * SEG + 16, :].astype(F32)[:1]


def feed_kernel(
    count_ref,
    rows_ref,
    context_ref,
    merge_ref,
    expand_ref,
    expand_bias_ref,
    reduce_ref,
    vectors_ref,
    mixed_ref,
    heads_ref,
    wide_heads_ref,
    first_ref,
    normed_ref,
    active_ref,
    slope_ref,
    second_ref,
):
    step = pl.program_id(0)
    merge_bias, gain, shift, reduce_bias, final_gain, final_shift = [
        vectors_ref[row : row + 1, :] for row in range(6)
    ]
    first = rows_ref[...].astype(F32) + dot_nn(context_ref[...], merge_ref[...]) + merge_bias
    first_ref[...] = first
    normed = (centre_rows(first)[0] * gain + shift).astype(LOW)
    normed_ref[...] = normed
    second = normed.astype(F32) + reduce_bias
    chunk, wide = D, expand_ref.shape[1]
    segments = ROWS // SEG
    for start in range(0, wide, chunk):
        span = slice(start, start + chunk)
        active, slope = gelu_pair(dot_nn(normed, expand_ref[:, span]) + expand_bias_ref[:, span])
        active = active.astype(LOW)
        active_ref[:, span] = active
        slope_ref[:, span] = slope.astype(LOW)
        for local in range(segments):
            head = step * segments + local
            put_row(wide_heads_ref, head, start, slope[local * SEG : local * SEG + 1])
            put_row(wide_heads_ref, head, wide + start, first_row(active, local))
        second = second + dot_nn(active, reduce_ref[span, :])
    second_ref[...] = second
    result = centre_rows(second)[0] * final_gain + final_shift
    for local in range(segments):
        for number, rows in enumerate((result, first, second, normed, context_ref)):
            put_row(heads_ref, step * segments + local, number * D, first_row(rows, local))
    place = lax.broadcasted_iota(jnp.int32, (ROWS, 1), 0) + step * ROWS
    mixed_ref[...] = jnp.where(place < count_ref[0], result, 0.0).astype(LOW)


def feed_back_kernel(
    count_ref,
    cotangent_ref,
    second_ref,
    first_ref,
    slope_ref,
    merge_ref,
    expand_ref,
    reduce_ref,
    vectors_ref,
    branch_ref,
    hidden_ref,
    attn_ref,
    context_ref,
    first_grad_ref,
    sums_ref,
    hidden_sums_ref,
):
    step = pl.program_id(0)
    gain, final_gain = vectors_ref[1:2, :], vectors_ref[4:5, :]
    local = lax.broadcasted_iota(jnp.int32, (ROWS, 1), 0)
    plain = (local + step * ROWS < count_ref[0]) & (local % SEG != 0)
    grad = jnp.where(plain, cotangent_ref[...].astype(F32), 0.0)
    unit, spread = centre_rows(second_ref[...])
    sums = [grad * unit, grad]
    second = norm_back(grad * final_gain, unit, spread)
    branch = second.astype(LOW)
    branch_ref[...] = branch
    sums.append(branch.astype(F32))
    normed = second
    chunk = D

    @pl.when(step == 0)
    def _():
        sums_ref[...] = jnp.zeros_like(sums_ref)
        hidden_sums_ref[...] = jnp.zeros_like(hidden_sums_ref)

    for start in range(0, expand_ref.shape[1], chunk):
        span = slice(start, start + chunk)
        hidden = back_cols(branch, reduce_ref[span, :]) * slope_ref[:, span].astype(F32)
        hidden = hidden.astype(LOW)
        hidden_ref[:, span] = hidden
        hidden_sums_ref[:, span] += jnp.sum(hidden.astype(F32), axis=0, keepdims=True)
        normed = normed + back_cols(hidden, expand_ref[:, span])
    unit, spread = centre_rows(first_ref[...])
    sums += [normed * unit, normed]
    first = norm_back(normed * gain, unit, spread)
    first_grad_ref[...] = first
    attn = first.astype(LOW)
    attn_ref[...] = attn
    sums.append(attn.astype(F32))
    context_ref[...] = back_cols(attn, merge_ref[...]).astype(LOW)
    sums_ref[...] += jnp.concatenate(
        [jnp.sum(entry, axis=0, keepdims=True) for entry in sums]
        + [jnp.zeros((2, D), F32)],
        axis=0,
    )


def attend_back_kernel(
    offset,
    count_ref,
    projected_ref,
    context_ref,
    first_ref,
    mixed_in_ref,
    attend_ref,
    head_context_ref,
    head_first_ref,
    head_out_ref,
    *refs,
):
    grad_ref, tokens_ref, mixed_ref, sums_ref = refs[-4:]
    step = pl.program_id(0)
    segments = ROWS // SEG

    @pl.when(step == 0)
    def _():
        sums_ref[...] = jnp.zeros_like(sums_ref)

    is_head = lax.broadcasted_iota(jnp.int32, (SEG, 1), 0) == 0
    scale = HD ** (-0.5)
    for local in range(segments):
        segment = (step + offset) * segments + local
        valid = valid_keys(count_ref, segment)
        span = slice(local * SEG, (local + 1) * SEG)
        for pair in range(PAIRS):
            columns = [
                slice(part * D + pair * PAIR, part * D + (pair + 1) * PAIR) for part in range(3)
            ]
            query, key, value = [projected_ref[span, column] for column in columns]
            grad = jnp.where(
                is_head,
                get_row(head_context_ref, segment, columns[0]),
                context_ref[span, columns[0]].astype(F32),
            ).astype(LOW)
            grad = two_heads(grad, 0)
            probs = pair_probs(query, key, valid)
            grad_probs = back_cols(grad, value)
            total = jnp.sum(grad_probs * probs, axis=-1, keepdims=True)
            scores = (probs * (grad_probs - total)).astype(LOW)
            grad_ref[span, columns[0]] = (
                dot_nn(side_by_side(scores), two_heads(key, 0)) * scale
            ).astype(LOW)
            grad_ref[span, columns[1]] = (
                cross_rows(scores, two_heads(query, 0)) * scale
            ).astype(LOW)
            grad_ref[span, columns[2]] = cross_rows(probs.astype(LOW), grad).astype(LOW)
        first = jnp.where(is_head, get_row(head_first_ref, segment, slice(0, D)), first_ref[span, :])
        tokens_ref[span, :] = first + back_cols(grad_ref[span, :], attend_ref[...])
        mixed_ref[span, :] = jnp.where(
            is_head, get_row(head_out_ref, segment, slice(0, D)), mixed_in_ref[span, :].astype(F32)
        ).astype(LOW)
    sums_ref[...] += jnp.sum(grad_ref[...].astype(F32), axis=0, keepdims=True)


def by_rows(width, offset=0):
    return pl.BlockSpec((ROWS, width), lambda step: (step + offset, 0))


def entire(array):
    return pl.BlockSpec(array.shape, lambda step: (0,) * array.ndim)


def row_call(kernel, name, operands, specs, outs, flops, steps=None, earlier=()):
    rows = next(operand.shape[0] for operand, spec in zip(operands, specs) if spec is not None)
    shapes = [jax.ShapeDtypeStruct(shape, kind) for shape, kind, _ in outs]
    moved = sum(operand.size * operand.dtype.itemsize for operand in operands)
    moved += sum(shape.size * shape.dtype.itemsize for shape in shapes)
    return pl.pallas_call(
        kernel,
        grid=(rows // ROWS if steps is None else steps,),
        in_specs=[pl.BlockSpec(memory_space=pltpu.SMEM)]
        + [entire(operand) if spec is None else spec for operand, spec in zip(operands[1:], specs[1:])]
        + [pl.BlockSpec(memory_space=pl.ANY)] * len(earlier),
        out_specs=[spec for _, _, spec in outs],
        out_shape=shapes,
        input_output_aliases={len(operands) + place: place for place in range(len(earlier))},
        compiler_params=pltpu.CompilerParams(vmem_limit_bytes=60 << 20),
        cost_estimate=pl.CostEstimate(flops=flops, bytes_accessed=moved, transcendentals=0),
        name=name,
    )(*operands, *earlier)


def whole_block(shape):
    return pl.BlockSpec(shape, lambda step: (0,) * len(shape))


def inner_attention(rows, counts, attend, attend_bias):
    size = rows.shape[0]
    return row_call(
        attend_kernel,
        "attend",
        (counts, rows, attend, attend_bias),
        (None, by_rows(D), None, None),
        [((size, 3 * D), LOW, by_rows(3 * D)), ((size, D), LOW, by_rows(D))],
        2 * size * D * (3 * D + 4 * SEG),
    )


def inner_feed(rows, counts, projected, context, weights):
    attend, merge, expand, reduce_matrix, expand_bias, vectors = weights
    size, wide = rows.shape[0], expand.shape[1]
    mixed, heads, wide_heads, *saved = row_call(
        feed_kernel,
        "feed",
        (counts, rows, context, merge, expand, expand_bias, reduce_matrix, vectors),
        (None, by_rows(D), by_rows(D), None, None, None, None, None),
        [
            ((size, D), LOW, by_rows(D)),
            ((size // SEG, 5 * D), F32, whole_block((size // SEG, 5 * D))),
            ((size // SEG, 2 * wide), F32, whole_block((size // SEG, 2 * wide))),
            ((size, D), F32, by_rows(D)),
            ((size, D), LOW, by_rows(D)),
            ((size, wide), LOW, by_rows(wide)),
            ((size, wide), LOW, by_rows(wide)),
            ((size, D), F32, by_rows(D)),
        ],
        2 * size * D * (D + 2 * wide),
    )
    return mixed, heads, wide_heads, saved


def inner_feed_back(cotangent, counts, saved, weights):
    attend, merge, expand, reduce_matrix, expand_bias, vectors = weights
    first, normed, active, slope, second = saved
    size, wide = cotangent.shape[0], expand.shape[1]
    return row_call(
        feed_back_kernel,
        "feed_back",
        (counts, cotangent, second, first, slope, merge, expand, reduce_matrix, vectors),
        (None, by_rows(D), by_rows(D), by_rows(D), by_rows(wide), None, None, None, None),
        [
            ((size, D), LOW, by_rows(D)),
            ((size, wide), LOW, by_rows(wide)),
            ((size, D), LOW, by_rows(D)),
            ((size, D), LOW, by_rows(D)),
            ((size, D), F32, by_rows(D)),
            ((8, D), F32, whole_block((8, D))),
            ((1, wide), F32, whole_block((1, wide))),
        ],
        2 * size * D * (D + 2 * wide),
    )


def inner_attend_back(counts, operands, attend, head_rows, offset, steps, earlier):
    projected, grad_context, grad_first, mixed = operands
    size = projected.shape[0]
    return row_call(
        partial(attend_back_kernel, offset),
        "attend_back",
        (counts, projected, grad_context, grad_first, mixed, attend, *head_rows),
        (None, by_rows(3 * D, offset), by_rows(D, offset), by_rows(D, offset))
        + (by_rows(D, offset), None, None, None, None),
        [
            ((size, 3 * D), LOW, by_rows(3 * D, offset)),
            ((size, D), F32, by_rows(D, offset)),
            ((size, D), LOW, by_rows(D, offset)),
            ((1, 3 * D), F32, whole_block((1, 3 * D))),
        ],
        2 * steps * ROWS * D * (3 * D + 10 * SEG),
        steps,
        earlier,
    )


AXES = ("dp", "fsdp")


def gather(rows):
    return lax.all_gather(rows, AXES, axis=0, tiled=True)


def scatter(rows):
    return lax.psum_scatter(rows, AXES, scatter_dimension=0, tiled=True)


def split_cols(packed, widths):
    pieces, start = [], 0
    for width in widths:
        pieces.append(packed[..., start : start + width])
        start += width
    return pieces


def pack_kernel(*refs):
    vectors, place_ref, out_ref, rows_ref = refs[:16], refs[16], refs[17], refs[18]
    rows_ref[...] = jnp.zeros_like(rows_ref)
    for row, ref in enumerate(vectors):
        rows_ref[row : row + 1, : ref.shape[1]] = ref[...].astype(F32)
    place = jnp.transpose(place_ref[...].astype(F32))
    rows_ref[16 : 16 + SEGS, : place.shape[1]] = place
    packed = rows_ref[...].astype(LOW)
    out_ref[...] = jnp.broadcast_to(packed[None], out_ref.shape)


def spread_row(rows, size, width):
    devices = rows.shape[0]
    lane = lax.broadcasted_iota(jnp.int32, (128, width), 1)
    owner = lane // size
    pick = (lane - owner * size == lax.broadcasted_iota(jnp.int32, (128, width), 0)).astype(LOW)
    spread = dot_nn(rows, pick)
    row = lax.broadcasted_iota(jnp.int32, (devices, width), 0)
    owner = lax.broadcasted_iota(jnp.int32, (devices, width), 1) // size
    return jnp.sum(jnp.where(row == owner, spread, 0.0), axis=0, keepdims=True)


VECTOR_ROWS = (1, 2, 3, 5, 6, 7)


def unpack_kernel(sizes, got_ref, *outs):
    devices = got_ref.shape[0]
    got = got_ref[...].astype(F32)
    for block in range(2):
        attend_ref, expand_ref, vectors_ref = outs[3 * block : 3 * block + 3]
        for kind in range(8):
            row = 8 * block + kind
            size = sizes[row]
            spread = spread_row(got[:, row, :].astype(LOW), size, size * devices)
            if kind == 0:
                attend_ref[...] = spread
            elif kind == 4:
                expand_ref[...] = spread
            else:
                place = VECTOR_ROWS.index(kind)
                vectors_ref[place : place + 1, :] = spread
        vectors_ref[6:8, :] = jnp.zeros((2, vectors_ref.shape[1]), F32)
    place_ref = outs[6]
    for segment in range(SEGS):
        place_ref[segment : segment + 1, :] = spread_row(
            got[:, 16 + segment, :].astype(LOW), sizes[16], sizes[16] * devices
        )


def share_small(vectors, segment_place):
    devices = lax.axis_size(AXES)
    sizes = [vector.shape[0] for vector in vectors] + [segment_place.shape[0]]
    sent = pl.pallas_call(
        pack_kernel,
        out_shape=jax.ShapeDtypeStruct((devices, 32, 128), LOW),
        scratch_shapes=[pltpu.VMEM((32, 128), F32)],
        name="pack",
    )(*[vector[None] for vector in vectors], segment_place)
    got = lax.all_to_all(sent, AXES, split_axis=0, concat_axis=0, tiled=True)
    shapes = []
    for block in range(2):
        for rows, size in ((1, sizes[8 * block]), (1, sizes[8 * block + 4]), (8, sizes[1])):
            shapes.append(jax.ShapeDtypeStruct((rows, size * devices), F32))
    shapes.append(jax.ShapeDtypeStruct((SEGS, sizes[16] * devices), F32))
    return pl.pallas_call(
        partial(unpack_kernel, sizes),
        out_shape=shapes,
        compiler_params=pltpu.CompilerParams(vmem_limit_bytes=60 << 20),
        name="unpack",
    )(got)


def sum_rows(rows):
    devices, size = rows.shape
    padded = jnp.pad(rows, ((0, 0), (0, -size % 1024))).reshape(devices, -1, 128)
    got = lax.all_to_all(padded, AXES, split_axis=0, concat_axis=0, tiled=True)
    return jnp.sum(got, axis=0).reshape(-1)[:size]


def hop(array, turn):
    return lax.ppermute(array, AXES, [(place, turn(place)) for place in range(32)])


def over_x(array):
    return hop(array, lambda place: place ^ 8)


def over_y(array):
    return hop(array, lambda place: place ^ 16)


def over_core(array):
    return hop(array, lambda place: place ^ 1)


def over_z(array, step):
    return hop(array, lambda place: (place & ~6) | ((((place >> 1) + step) & 3) << 1))


def place_here():
    chip = lax.axis_index("fsdp")
    return lax.axis_index("dp"), chip // 2, chip % 2


def half_cols(array, core):
    width = array.shape[-1] // 2
    return lax.dynamic_slice_in_dim(array, core * width, width, axis=array.ndim - 1)


def fold_rows(array, rows):
    return jnp.concatenate(jnp.split(array, array.shape[0] // rows, axis=0), axis=1)


def unfold_cols(array, width):
    return jnp.concatenate(jnp.split(array, array.shape[1] // width, axis=1), axis=0)


def both_cores(mine, other, core, axis):
    return jnp.concatenate(
        [jnp.where(core == 0, mine, other), jnp.where(core == 0, other, mine)], axis=axis
    )


def assemble_kernel(heights, widths, place_ref, *refs):
    pieces, outs, sems = refs[:10], refs[10:-1], refs[-1]
    plane, depth, core = place_ref[0], place_ref[1], place_ref[2]
    slots = ((0, 0, 4), (1, 0, 4), (2, 0, 4), (3, 0, 2), (3, 2, 2))
    copies = []
    for side in range(2):
        column = core if side == 0 else 1 - core
        for number, (turn, first, count) in enumerate(slots):
            piece = pieces[5 * side + number]
            for slot in range(count):
                chip = (plane ^ turn) * 4 + ((depth + 4 - first - slot) & 3)
                start = 0
                for out, height, width in zip(outs, heights, widths):
                    for group in range(height // 48):
                        row = pl.multiple_of(chip * height + 48 * group, 48)
                        lane = pl.multiple_of(column * width, 128)
                        copies.append(
                            pltpu.make_async_copy(
                                piece.at[slot, :, pl.ds(start, width)],
                                out.at[pl.ds(row, 48), pl.ds(lane, width)],
                                sems.at[len(copies)],
                            )
                        )
                        start += width
    for copy in copies:
        copy.start()
    for copy in copies:
        copy.wait()


def gather_links(shards, gate, gates):
    plane, depth, core = place_here()
    rows = min(shard.shape[0] for shard in shards)
    mine = jnp.concatenate([fold_rows(half_cols(shard, core), rows) for shard in shards], axis=1)
    sent = jnp.concatenate(
        [fold_rows(half_cols(shard, 1 - core), rows) for shard in shards], axis=1
    )
    other = over_core(sent)
    widths = [shard.shape[1] // 2 for shard in shards]
    heights = [2 * shard.shape[0] for shard in shards]
    slab, start = [], 0
    for width, height in zip(widths, heights):
        span = width * (height // (2 * rows))
        pair = [unfold_cols(part[:, start : start + span], width) for part in (mine, other)]
        slab.append(fold_rows(both_cores(pair[0], pair[1], core, 0), 2 * rows))
        start += span
    slab = jnp.concatenate(slab, axis=1)
    line = jnp.stack([slab] + [over_z(slab, step) for step in (1, 2, 3)])
    gates.append(slab)
    line = after(gate, line)
    line_x, line_y = over_x(line), over_y(line)
    pieces = [line, line_x, line_y, over_y(line_x[:2]), over_x(line_y[2:])]
    pieces = pieces + [over_core(piece) for piece in pieces]
    count = 32 * sum(height // 48 for height in heights)
    place = jnp.stack([plane, depth, core]).astype(jnp.int32)
    return pl.pallas_call(
        partial(assemble_kernel, heights, widths),
        out_shape=[
            jax.ShapeDtypeStruct((16 * height, 2 * width), jnp.bfloat16)
            for height, width in zip(heights, widths)
        ],
        in_specs=[pl.BlockSpec(memory_space=pltpu.SMEM)]
        + [pl.BlockSpec(memory_space=pl.ANY)] * 10,
        out_specs=[pl.BlockSpec(memory_space=pltpu.VMEM)] * len(shards),
        scratch_shapes=[pltpu.SemaphoreType.DMA((count,))],
        compiler_params=pltpu.CompilerParams(vmem_limit_bytes=60 << 20),
        name="assemble",
    )(place, *pieces)


def after(first, *later):
    tied = lax.optimization_barrier((first, later))[1]
    return tied[0] if len(tied) == 1 else tied


def first_hops(line, gate):
    core = place_here()[2]
    half = line.shape[0] // 2
    mine = after(gate, lax.dynamic_slice_in_dim(line, core * half, half, axis=0))
    return line, over_x(mine), over_y(mine)


def last_hops(hops, gate):
    line, from_x, from_y = hops
    half = from_x.shape[0] // 2
    sent_y, sent_x = after(gate, from_x[:half], from_y[half:])
    pieces = [from_x, from_y, over_y(sent_y), over_x(sent_x)]
    return [line] + pieces + [over_core(piece) for piece in pieces]


def late_pieces(shard):
    half = shard.shape[0] // 2
    from_x, from_y = over_x(shard), over_y(shard)
    across = jnp.concatenate([over_y(from_x[:half]), over_x(from_y[half:])], axis=0)
    rows = jnp.concatenate([shard, from_x, from_y, across], axis=0)
    return [lax.all_gather(rows, "fsdp", axis=0, tiled=True)]


def join_kernel(all_moves, all_widths, counts, place_ref, *refs):
    total = sum(counts)
    pieces, outs, sems = refs[:total], refs[total:-1], refs[-1]
    waits, first, start, number = [], 0, 0, 0
    for moves, widths, count in zip(all_moves, all_widths, counts):
        targets = outs[number : number + len(widths)]
        waits += start_moves(
            pieces[start : start + count], targets, widths, moves, place_ref, sems, first
        )
        first += len(moves) * len(widths)
        start += count
        number += len(widths)
    for copies in waits:
        wait_all(copies)


def join_pieces(groups, all_widths):
    plane, depth, core = place_here()
    place = jnp.stack([plane, depth, core]).astype(jnp.int32)
    all_moves = [mid_moves_of(pieces) for pieces in groups]
    shapes = [
        jax.ShapeDtypeStruct((4 * pieces[0].shape[0], width), jnp.bfloat16)
        for pieces, widths in zip(groups, all_widths)
        for width in widths
    ]
    sems = sum(len(moves) * len(widths) for moves, widths in zip(all_moves, all_widths))
    pieces = [piece for group in groups for piece in group]
    joined = pl.pallas_call(
        partial(join_kernel, all_moves, all_widths, [len(group) for group in groups]),
        out_shape=shapes,
        in_specs=[pl.BlockSpec(memory_space=pltpu.SMEM)]
        + [pl.BlockSpec(memory_space=pl.ANY)] * len(pieces),
        out_specs=[pl.BlockSpec(memory_space=pltpu.VMEM)] * len(shapes),
        scratch_shapes=[pltpu.SemaphoreType.DMA((sems,))],
        compiler_params=pltpu.CompilerParams(vmem_limit_bytes=60 << 20),
        name="join",
    )(place, *pieces)
    return list(joined)


def along_z(shards):
    return lax.all_gather(jnp.concatenate(shards, axis=1), "fsdp", axis=0, tiled=True)


def start_moves(pieces, outs, widths, moves, place_ref, sems, first):
    plane, core = place_ref[0], place_ref[2]
    groups, start = [], 0
    for out, width in zip(outs, widths):
        copies = []
        for piece, source, rows, turn, quarter, side, offset in moves:
            row = (plane ^ turn) * quarter + offset
            if side is not None:
                row = row + (core if side == 0 else 1 - core) * (quarter // 2)
            copies.append(
                pltpu.make_async_copy(
                    pieces[piece].at[source : source + rows, start : start + width],
                    out.at[pl.ds(pl.multiple_of(row, 48), rows), :],
                    sems.at[first],
                )
            )
            first += 1
        start += width
        groups.append(copies)
    for copies in groups:
        for copy in copies:
            copy.start()
    return groups


def wait_all(copies):
    for copy in copies:
        copy.wait()


def column_sums(rows):
    return jnp.sum(rows, axis=0, keepdims=True)


def feed_rows_back(grad, unit, spread, slope_of, reduce_ref, expand_ref, final_gain):
    second = norm_back(grad * final_gain, unit, spread)
    branch = second.astype(LOW)
    normed, hidden = second, []
    for start in range(0, expand_ref.shape[1], D):
        span = slice(start, start + D)
        part = (back_cols(branch, reduce_ref[span, :]) * slope_of(span)).astype(LOW)
        hidden.append(part)
        normed = normed + back_cols(part, expand_ref[:, span])
    return branch, hidden, normed


def heads_kernel(
    counts,
    mid_moves,
    end_moves,
    place_ref,
    count_ref,
    heads_ref,
    wide_heads_ref,
    table_ref,
    cotangent_ref,
    attend_bias_ref,
    expand_bias_ref,
    vectors_ref,
    inner_vectors_ref,
    *refs,
):
    mid_count, end_count = counts
    mid, refs = refs[:mid_count], refs[mid_count:]
    end, refs = refs[:end_count], refs[end_count:]
    inner_hbm, refs = refs[:3], refs[3:]
    out_ref, grad_ref, left_ref, right_ref, sums_ref = refs[:5]
    branch_ref, hidden_ref, attn_ref, context_ref, first_ref, inner_sums_ref, hidden_sums_ref = refs[5:12]
    attend_ref, merge_ref, expand_ref, reduce_ref = refs[12:16]
    inner_refs, sems = refs[16:19], refs[19]
    wide = expand_ref.shape[1]
    waits = start_moves(
        mid, (attend_ref, merge_ref, expand_ref), (3 * D, D, wide), mid_moves, place_ref, sems, 0
    )
    first_free = 3 * len(mid_moves)
    waits += start_moves(end, (reduce_ref,), (D,), end_moves, place_ref, sems, first_free)
    first_free += len(end_moves)
    inner_waits = [
        pltpu.make_async_copy(source, target, sems.at[first_free + number])
        for number, (source, target) in enumerate(zip(inner_hbm, inner_refs))
    ]
    for copy in inner_waits:
        copy.start()
    merge_bias, gain, shift, reduce_bias, final_gain, final_shift = [
        vectors_ref[row : row + 1, :] for row in range(6)
    ]
    scale = HD ** (-0.5)
    stacked = HEADS * SEGS
    own = (
        lax.broadcasted_iota(jnp.int32, (stacked, D), 1) // HD
        == lax.broadcasted_iota(jnp.int32, (stacked, D), 0) // SEGS
    )

    def by_head(rows):
        return jnp.where(own, jnp.concatenate([rows] * HEADS, axis=0), 0.0).astype(LOW)

    def join_heads(rows):
        rows = jnp.where(own, rows, 0.0)
        return sum(rows[SEGS * head : SEGS * (head + 1)] for head in range(HEADS))

    keep = (
        lax.broadcasted_iota(jnp.int32, (SEGS, 1), 0) * SEG < count_ref[0]
    ).astype(F32)
    source = (heads_ref[:, :D] + table_ref[...]).astype(LOW)
    wait_all(waits[0])
    projected = (dot_nn(source, attend_ref[...]) + attend_bias_ref[...]).astype(LOW)
    query, key, value = projected[:, :D], projected[:, D : 2 * D], projected[:, 2 * D :]
    queries = by_head(query.astype(F32))
    scores = back_cols(queries, key) * scale
    weight = jnp.exp(scores - jnp.max(scores, axis=-1, keepdims=True))
    probs = weight / jnp.sum(weight, axis=-1, keepdims=True)
    probs_low = probs.astype(LOW)
    context = join_heads(dot_nn(probs_low, value)).astype(LOW)
    wait_all(waits[1])
    first = source.astype(F32) + dot_nn(context, merge_ref[...]) + merge_bias
    first_unit, first_spread = centre_rows(first)
    normed = (first_unit * gain + shift).astype(LOW)
    left_ref[:, :D] = source
    left_ref[:, D : 2 * D] = context
    left_ref[:, 2 * D : 3 * D] = normed
    second = normed.astype(F32) + reduce_bias
    slopes = {}
    wait_all(waits[2])
    wait_all(waits[3])
    for start in range(0, wide, D):
        span = slice(start, start + D)
        active, slopes[start] = gelu_pair(
            dot_nn(normed, expand_ref[:, span]) + expand_bias_ref[:, span]
        )
        active = active.astype(LOW)
        left_ref[:, 3 * D + start : 4 * D + start] = active
        second = second + dot_nn(active, reduce_ref[span, :])
    unit, spread = centre_rows(second)
    out_ref[...] = (unit * final_gain + final_shift) * keep
    grad = cotangent_ref[...].astype(F32) * keep
    sums = [column_sums(grad * unit), column_sums(grad)]
    branch, hidden, grad_normed = feed_rows_back(
        grad, unit, spread, lambda span: slopes[span.start], reduce_ref, expand_ref, final_gain
    )
    sums += [column_sums(grad_normed * first_unit), column_sums(grad_normed)]
    grad_first = norm_back(grad_normed * gain, first_unit, first_spread)
    attn = grad_first.astype(LOW)
    grads = by_head(back_cols(attn, merge_ref[...]).astype(LOW).astype(F32))
    grad_probs = back_cols(grads, value)
    total = jnp.sum(grad_probs * probs, axis=-1, keepdims=True)
    grad_scores = (probs * (grad_probs - total)).astype(LOW)
    grad_query = (join_heads(dot_nn(grad_scores, key)) * scale).astype(LOW)
    grad_key = (cross_rows(grad_scores, queries) * scale).astype(LOW)
    grad_value = cross_rows(probs_low, grads).astype(LOW)
    grad_projected = jnp.concatenate([grad_query, grad_key, grad_value], axis=1)
    right_ref[:, : 3 * D] = grad_projected
    right_ref[:, 3 * D : 4 * D] = attn
    for number, part in enumerate(hidden):
        right_ref[:, (4 + number) * D : (5 + number) * D] = part
    right_ref[:, 4 * D + wide :] = branch
    sums_ref[...] = jnp.concatenate(sums + [jnp.zeros((4, D), F32)], axis=0)
    grad = grad_first + back_cols(grad_projected, attend_ref[...])
    grad_ref[...] = grad

    wait_all(inner_waits)
    inner_merge_ref, inner_expand_ref, inner_reduce_ref = inner_refs
    gain, final_gain = inner_vectors_ref[1:2, :], inner_vectors_ref[4:5, :]
    first_unit, first_spread = centre_rows(heads_ref[:, D : 2 * D])
    unit, spread = centre_rows(heads_ref[:, 2 * D : 3 * D])
    sums = [column_sums(grad * unit), column_sums(grad)]
    branch, hidden, grad_normed = feed_rows_back(
        grad,
        unit,
        spread,
        lambda span: wide_heads_ref[:, span],
        inner_reduce_ref,
        inner_expand_ref,
        final_gain,
    )
    branch_ref[...] = branch
    sums.append(column_sums(branch.astype(F32)))
    for number, part in enumerate(hidden):
        span = slice(number * D, (number + 1) * D)
        hidden_ref[:, span] = part
        hidden_sums_ref[:, span] = column_sums(part.astype(F32))
    sums += [column_sums(grad_normed * first_unit), column_sums(grad_normed)]
    grad_first = norm_back(grad_normed * gain, first_unit, first_spread)
    first_ref[...] = grad_first
    attn = grad_first.astype(LOW)
    attn_ref[...] = attn
    sums.append(column_sums(attn.astype(F32)))
    context_ref[...] = back_cols(attn, inner_merge_ref[...]).astype(LOW).astype(F32)
    inner_sums_ref[...] = jnp.concatenate(sums + [jnp.zeros((2, D), F32)], axis=0)


def mid_moves_of(pieces):
    if len(pieces) == 1:
        return [(0, 0, pieces[0].shape[0], 0, 0, None, 0)]
    quarter = pieces[0].shape[0]
    half = quarter // 2
    moves = [(0, 0, quarter, 0, quarter, None, 0)]
    for side in range(2):
        moves += [
            (1 + 4 * side, 0, half, 1, quarter, side, 0),
            (2 + 4 * side, 0, half, 2, quarter, side, 0),
            (3 + 4 * side, 0, half // 2, 3, quarter, side, 0),
            (4 + 4 * side, 0, half // 2, 3, quarter, side, half // 2),
        ]
    return moves


def late_moves_of(piece, linked):
    if not linked:
        return [(0, 0, piece.shape[0], 0, 0, None, 0)]
    rows = piece.shape[0] // 32
    return [
        (0, (4 * slot + turn) * rows, rows, turn, 8 * rows, None, slot * rows)
        for slot in range(8)
        for turn in range(4)
    ]


def heads_step(counts, heads, wide_heads, table, cotangent, small, mid, late, inner, linked):
    attend_bias, expand_bias, vectors, inner_vectors = small
    wide = expand_bias.shape[1]
    mid_moves, end_moves = mid_moves_of(mid), late_moves_of(late, linked)
    plane, depth, core = place_here()
    place = jnp.stack([plane, depth, core]).astype(jnp.int32)
    vmem = pl.BlockSpec(memory_space=pltpu.VMEM)
    smem = pl.BlockSpec(memory_space=pltpu.SMEM)
    outs = [
        ((SEGS, D), F32),
        ((SEGS, D), F32),
        ((SEGS, 3 * D + wide), LOW),
        ((SEGS, 5 * D + wide), LOW),
        ((8, D), F32),
        ((SEGS, D), LOW),
        ((SEGS, wide), LOW),
        ((SEGS, D), LOW),
        ((SEGS, D), F32),
        ((SEGS, D), F32),
        ((8, D), F32),
        ((1, wide), F32),
    ]
    flops = 6 * SEGS * D * (5 * D + 4 * wide)
    moved = 2 * D * (6 * D + 4 * wide)
    return pl.pallas_call(
        partial(heads_kernel, (len(mid), 1), mid_moves, end_moves),
        out_shape=[jax.ShapeDtypeStruct(shape, kind) for shape, kind in outs],
        in_specs=[smem, smem] + [vmem] * 8 + [pl.BlockSpec(memory_space=pl.ANY)] * (len(mid) + 4),
        out_specs=[vmem] * len(outs),
        scratch_shapes=[
            pltpu.VMEM((D, 3 * D), LOW),
            pltpu.VMEM((D, D), LOW),
            pltpu.VMEM((D, wide), LOW),
            pltpu.VMEM((wide, D), LOW),
            pltpu.VMEM((D, D), LOW),
            pltpu.VMEM((D, wide), LOW),
            pltpu.VMEM((wide, D), LOW),
            pltpu.SemaphoreType.DMA((3 * len(mid_moves) + len(end_moves) + 3,)),
        ],
        compiler_params=pltpu.CompilerParams(vmem_limit_bytes=60 << 20),
        cost_estimate=pl.CostEstimate(flops=flops, bytes_accessed=moved, transcendentals=0),
        name="heads",
    )(
        place,
        counts,
        heads,
        wide_heads,
        table,
        cotangent,
        attend_bias,
        expand_bias,
        vectors,
        inner_vectors,
        *mid,
        late,
        *inner,
    )


def scatter_pack(grads):
    core = place_here()[2]

    def packed(side):
        return jnp.concatenate(
            [
                jnp.transpose(
                    half_cols(grad, side).reshape(16, grad.shape[0] // 768, 48, -1), (0, 2, 1, 3)
                ).reshape(16, 48, -1)
                for grad in grads
            ],
            axis=2,
        )

    return packed(core), packed(1 - core)


def scatter_core(kept, sent):
    plane = place_here()[0]
    kept = (kept + over_core(sent)).reshape(4, 4, 48, -1)
    return [
        lax.dynamic_index_in_dim(kept, plane ^ turn, axis=0, keepdims=False)
        for turn in range(4)
    ]


def scatter_across(planes):
    here, next_x, next_y, across = planes
    from_y, from_x = over_y(across[:2]), over_x(across[2:])
    next_x = jnp.concatenate([next_x[:2] + from_y, next_x[2:]], axis=0)
    next_y = jnp.concatenate([next_y[:2], next_y[2:] + from_x], axis=0)
    return here, next_x, next_y


def scatter_next(here, next_x, next_y):
    came_x, came_y = over_x(next_x), over_y(next_y)
    return (
        here.astype(jnp.float32) + came_x.astype(jnp.float32) + came_y.astype(jnp.float32)
    ).astype(jnp.bfloat16)


def scatter_line(here):
    depth = place_here()[1]
    slabs = [
        lax.dynamic_index_in_dim(here, (depth + step) & 3, axis=0, keepdims=False)
        for step in range(4)
    ]
    total = slabs[0].astype(jnp.float32)
    for step in (1, 2, 3):
        total = total + over_z(slabs[step], step).astype(jnp.float32)
    return total


def scatter_end(total, shapes):
    core = place_here()[2]
    mine, sent, start = [], [], 0
    for height, width in shapes:
        width = width // 2
        groups = height // 768
        rows = unfold_cols(total[:, start : start + groups * width], width)
        start += groups * width
        mine.append(fold_rows(lax.dynamic_slice_in_dim(rows, core * 24 * groups, 24 * groups), 24))
        sent.append(
            fold_rows(lax.dynamic_slice_in_dim(rows, (1 - core) * 24 * groups, 24 * groups), 24)
        )
    other = over_core(jnp.concatenate(sent, axis=1))
    owned, start = [], 0
    for (height, width), part in zip(shapes, mine):
        width = width // 2
        pair = [unfold_cols(side, width) for side in (part, other[:, start : start + part.shape[1]])]
        owned.append(both_cores(pair[0], pair[1], core, 1))
        start += part.shape[1]
    return owned


def unfold(packed, parts, ratio):
    width = packed.shape[1] // ratio
    return jnp.stack(
        [
            packed[:, width * group : width * (group + 1)].reshape(-1, parts, width)
            for group in range(ratio)
        ],
        axis=1,
    ).reshape(-1, width)


def gather_flat(shards):
    parts = min(shard.shape[0] for shard in shards)
    pieces = split_cols(
        gather(jnp.concatenate([fold_rows(shard, parts) for shard in shards], axis=1)),
        [shard.size // parts for shard in shards],
    )
    return [
        unfold(piece, parts, shard.shape[0] // parts) if shard.shape[0] > parts else piece
        for piece, shard in zip(pieces, shards)
    ]


def scatter_flat(grads):
    devices = lax.axis_size(AXES)
    parts = min(grad.shape[0] for grad in grads) // devices
    packed = jnp.concatenate(
        [
            jnp.transpose(grad.reshape(devices, -1, parts, grad.shape[1]), (0, 2, 1, 3)).reshape(
                devices * parts, -1
            )
            for grad in grads
        ],
        axis=1,
    )
    owned = split_cols(
        scatter(packed).astype(jnp.float32), [grad.size // (devices * parts) for grad in grads]
    )
    return [unfold_cols(piece, grad.shape[1]) for piece, grad in zip(owned, grads)]


def on_device(
    tokens,
    counts,
    inner_attend,
    inner_attend_bias,
    inner_merge,
    inner_merge_bias,
    inner_gain,
    inner_shift,
    inner_expand,
    inner_expand_bias,
    inner_reduce,
    inner_reduce_bias,
    inner_final_gain,
    inner_final_shift,
    outer_attend,
    outer_attend_bias,
    outer_merge,
    outer_merge_bias,
    outer_gain,
    outer_shift,
    outer_expand,
    outer_expand_bias,
    outer_reduce,
    outer_reduce_bias,
    outer_final_gain,
    outer_final_shift,
    segment_place,
    cotangent,
):
    parts = inner_merge.shape[0]
    devices = D // parts
    ratio = inner_reduce.shape[0] // parts
    here = lax.axis_index(AXES)
    (
        attend_bias,
        expand_bias,
        vectors,
        outer_attend_bias_full,
        outer_expand_bias_full,
        outer_vectors,
        place_rows,
    ) = share_small(
        (
            inner_attend_bias,
            inner_merge_bias,
            inner_gain,
            inner_shift,
            inner_expand_bias,
            inner_reduce_bias,
            inner_final_gain,
            inner_final_shift,
            outer_attend_bias,
            outer_merge_bias,
            outer_gain,
            outer_shift,
            outer_expand_bias,
            outer_reduce_bias,
            outer_final_gain,
            outer_final_shift,
        ),
        segment_place,
    )
    linked = lax.axis_size("dp") == 4 and lax.axis_size("fsdp") == 8
    wide = inner_expand.shape[1]
    inner_rest = [inner_merge, inner_expand, inner_reduce]
    outer_all = [outer_attend, outer_merge, outer_expand, outer_reduce]
    docs = counts.shape[0]
    head_cotangent = cotangent.reshape(docs * SEGS, SEG, D)[:, 0, :]
    if linked:
        gates = []
        inner_full = list(gather_links([inner_attend], place_rows, gates))
        mid_line = along_z(after(gates[0], *inner_rest[:2]))
        end_line = along_z([after(gates[0], inner_rest[2])])
        outer_line = along_z(after(gates[0], *outer_all[:3]))
        projected, context = inner_attention(tokens, counts, inner_full[0], attend_bias)
        mid = first_hops(mid_line, inner_full[0])
        end = first_hops(end_line, (context, mid[1], mid[2]))
        mid = last_hops(mid, context)
        end = last_hops(end, (mid[3], mid[4]))
        outer = first_hops(outer_line, (mid[3], mid[4], end[1], end[2]))
        late = late_pieces(after(context, outer_reduce))
        inner_full += join_pieces([mid, end], [[D, wide], [D]])
    else:
        inner_full = gather_flat([inner_attend]) + gather_flat(inner_rest)
        projected, context = inner_attention(tokens, counts, inner_full[0], attend_bias)
    inner_weights = (*inner_full, expand_bias, vectors)
    mixed, heads, wide_heads, saved = inner_feed(tokens, counts, projected, context, inner_weights)
    if linked:
        outer = last_hops(outer, heads)
    else:
        outer_full = gather_flat(outer_all)
        outer, late = [jnp.concatenate(outer_full[:3], axis=1)], outer_full[3:]
    branch, grad_hidden, grad_attn, grad_context, grad_first, inner_sums, hidden_sums = (
        inner_feed_back(cotangent, counts, saved, inner_weights)
    )
    first, normed, active, slope, second = saved
    low = jnp.bfloat16
    plain_grads = lax.optimization_barrier(
        (
            cross_rows(active, branch).astype(low),
            cross_rows(normed, grad_hidden).astype(low),
            cross_rows(context, grad_attn).astype(low),
        )
    )
    (
        head_out,
        grad_heads,
        left_pack,
        right_pack,
        outer_sums,
        head_branch,
        head_hidden,
        head_attn,
        head_context,
        head_first,
        head_sums,
        head_hidden_sums,
    ) = heads_step(
        counts,
        heads,
        wide_heads,
        place_rows,
        head_cotangent,
        (outer_attend_bias_full, outer_expand_bias_full, outer_vectors, vectors),
        outer,
        late[0],
        inner_full[1:],
        linked,
    )
    grad_place = jnp.transpose(jnp.sum(grad_heads.reshape(docs, SEGS, D), axis=0))
    inner_sums = inner_sums + head_sums
    hidden_sums = hidden_sums + head_hidden_sums
    grad_reduce, grad_expand, grad_merge = [
        (plain.astype(jnp.float32) + cross_rows(left.astype(low), right)).astype(low)
        for plain, left, right in zip(
            plain_grads,
            (wide_heads[:, wide:], heads[:, 3 * D : 4 * D], heads[:, 4 * D :]),
            (head_branch, head_hidden, head_attn),
        )
    ]
    operands = (projected, grad_context, grad_first, mixed)
    head_rows = (head_context, head_first, head_out)
    steps = tokens.shape[0] // ROWS
    if linked:
        kept, sent = scatter_pack([grad_expand, grad_reduce])
        operands = after(sent, *operands)
        part = inner_attend_back(counts, operands, inner_full[0], head_rows, 0, steps // 2, ())
        planes = scatter_core(kept, sent)
        operands = after(planes, *operands)
        rest = inner_attend_back(
            counts, operands, inner_full[0], head_rows, steps // 2, steps - steps // 2, part[:3]
        )
        grad_projected, tokens_grad, mixed = rest[:3]
        attend_sums = part[3] + rest[3]
        tall = scatter_across(planes)
        tall = scatter_next(*tall)
        grad_attend = cross_rows(tokens, grad_projected).astype(low)
        planes = scatter_core(*scatter_pack([grad_attend, grad_merge]))
        tall = scatter_line(tall)
        short = scatter_next(*scatter_across(planes))
        short = scatter_line(short)
        own_expand, own_reduce = scatter_end(tall, [grad_expand.shape, grad_reduce.shape])
        own_attend, own_merge = scatter_end(short, [grad_attend.shape, grad_merge.shape])
    else:
        grad_projected, tokens_grad, mixed, attend_sums = inner_attend_back(
            counts, operands, inner_full[0], head_rows, 0, steps, ()
        )
        grad_attend = cross_rows(tokens, grad_projected).astype(low)
        own_expand, own_reduce = scatter_flat([grad_expand, grad_reduce])
        own_attend, own_merge = scatter_flat([grad_attend, grad_merge])
    left_pack = jnp.concatenate(
        [
            factor.reshape(factor.shape[0], devices, -1)
            for factor in split_cols(left_pack, (D, D, D, wide))
        ],
        axis=2,
    )
    left_pack = jnp.transpose(left_pack, (1, 0, 2))
    left_all = lax.all_to_all(left_pack, AXES, split_axis=0, concat_axis=0, tiled=True)
    left_all = left_all.reshape(-1, left_all.shape[-1])
    right_all = gather(right_pack)
    left_pieces = split_cols(left_all, (parts, parts, parts, parts * ratio))
    right_pieces = split_cols(right_all, (3 * D, D, wide, D))
    outer_big = [cross_rows(left, right) for left, right in zip(left_pieces, right_pieces)]
    outer_bias = [
        lax.dynamic_slice_in_dim(
            jnp.sum(right.astype(jnp.float32), axis=0), here * width, width, axis=0
        )
        for right, width in zip(
            right_pieces, (3 * parts, parts, wide // devices, parts)
        )
    ]
    row_sums = (
        attend_sums,
        inner_sums[5],
        inner_sums[3],
        inner_sums[4],
        hidden_sums,
        inner_sums[2],
        inner_sums[0],
        inner_sums[1],
        outer_sums[2],
        outer_sums[3],
        outer_sums[0],
        outer_sums[1],
        grad_place,
    )
    sums = sum_rows(jnp.concatenate([entry.reshape(devices, -1) for entry in row_sums], axis=1))
    sums = split_cols(sums, [entry.size // devices for entry in row_sums])
    return (
        mixed,
        tokens_grad,
        own_attend,
        sums[0],
        own_merge,
        sums[1],
        sums[2],
        sums[3],
        own_expand,
        sums[4],
        own_reduce,
        sums[5],
        sums[6],
        sums[7],
        outer_big[0],
        outer_bias[0],
        outer_big[1],
        outer_bias[1],
        sums[8],
        sums[9],
        outer_big[2],
        outer_bias[2],
        outer_big[3],
        outer_bias[3],
        sums[10],
        sums[11],
        sums[12].reshape(parts, SEGS),
    )


def solution(mesh):
    return jax.shard_map(
        on_device,
        mesh=mesh,
        in_specs=(
            P(("dp", "fsdp"), None),
            P(("dp", "fsdp")),
            P(("dp", "fsdp"), None),
            P(("dp", "fsdp")),
            P(("dp", "fsdp"), None),
            P(("dp", "fsdp")),
            P(("dp", "fsdp")),
            P(("dp", "fsdp")),
            P(("dp", "fsdp"), None),
            P(("dp", "fsdp")),
            P(("dp", "fsdp"), None),
            P(("dp", "fsdp")),
            P(("dp", "fsdp")),
            P(("dp", "fsdp")),
            P(("dp", "fsdp"), None),
            P(("dp", "fsdp")),
            P(("dp", "fsdp"), None),
            P(("dp", "fsdp")),
            P(("dp", "fsdp")),
            P(("dp", "fsdp")),
            P(("dp", "fsdp"), None),
            P(("dp", "fsdp")),
            P(("dp", "fsdp"), None),
            P(("dp", "fsdp")),
            P(("dp", "fsdp")),
            P(("dp", "fsdp")),
            P(("dp", "fsdp"), None),
            P(("dp", "fsdp"), None),
        ),
        out_specs=(
            P(("dp", "fsdp"), None),
            P(("dp", "fsdp"), None),
            P(("dp", "fsdp"), None),
            P(("dp", "fsdp")),
            P(("dp", "fsdp"), None),
            P(("dp", "fsdp")),
            P(("dp", "fsdp")),
            P(("dp", "fsdp")),
            P(("dp", "fsdp"), None),
            P(("dp", "fsdp")),
            P(("dp", "fsdp"), None),
            P(("dp", "fsdp")),
            P(("dp", "fsdp")),
            P(("dp", "fsdp")),
            P(("dp", "fsdp"), None),
            P(("dp", "fsdp")),
            P(("dp", "fsdp"), None),
            P(("dp", "fsdp")),
            P(("dp", "fsdp")),
            P(("dp", "fsdp")),
            P(("dp", "fsdp"), None),
            P(("dp", "fsdp")),
            P(("dp", "fsdp"), None),
            P(("dp", "fsdp")),
            P(("dp", "fsdp")),
            P(("dp", "fsdp")),
            P(("dp", "fsdp"), None),
        ),
        check_vma=False,
    )
```

```python
from functools import partial

import jax
import jax.numpy as jnp
from jax import lax
from jax.experimental import pallas as pl
from jax.experimental.pallas import tpu as pltpu
from jax.sharding import PartitionSpec as P

D = 768
HEADS = 12
HD = 64
SEG = 128
SLOTS = 1024
SEGS = 8


def cross_rows(left_rows, right_rows):
    return lax.dot_general(
        left_rows, right_rows, (((0,), (0,)), ((), ())), preferred_element_type=jnp.float32
    )


def back_cols(left_rows, right_rows):
    return lax.dot_general(
        left_rows, right_rows, (((1,), (1,)), ((), ())), preferred_element_type=jnp.float32
    )


ROWS = 256
PAIR = 2 * HD
PAIRS = HEADS // 2
F32 = jnp.float32
LOW = jnp.bfloat16


def dot_nn(left, right):
    return jnp.dot(left, right, preferred_element_type=F32)


def centre_rows(rows):
    centred = rows - jnp.mean(rows, axis=-1, keepdims=True)
    spread = lax.rsqrt(jnp.mean(centred * centred, axis=-1, keepdims=True) + 1e-05)
    return centred * spread, spread


def norm_back(grad, unit, spread):
    return spread * (
        grad
        - jnp.mean(grad, axis=-1, keepdims=True)
        - unit * jnp.mean(grad * unit, axis=-1, keepdims=True)
    )


def gelu_pair(hidden):
    size = jnp.abs(hidden)
    bell = jnp.exp(hidden * hidden * -0.5)
    t = 1.0 / (1.0 + (0.3275911 * 0.7071067811865476) * size)
    poly = t * (
        0.127414796
        + t * (-0.142248368 + t * (0.7107068705 + t * (-0.7265760135 + t * 0.5307027145)))
    )
    tail = poly * bell
    phi = jnp.where(hidden >= 0, 1.0 - tail, tail)
    return hidden * phi, phi + hidden * bell * 0.3989422804014327


def two_heads(pair, axis):
    first = lax.broadcasted_iota(jnp.int32, pair.shape, 1) < HD
    zero = jnp.zeros_like(pair)
    return jnp.concatenate([jnp.where(first, pair, zero), jnp.where(first, zero, pair)], axis=axis)


def pair_probs(query, key, valid):
    scores = back_cols(two_heads(query, 0), key) * HD ** (-0.5)
    scores = jnp.where(valid, scores, -1e30)
    weight = jnp.exp(scores - jnp.max(scores, axis=-1, keepdims=True))
    return weight / jnp.sum(weight, axis=-1, keepdims=True)


def side_by_side(stacked):
    half = stacked.shape[0] // 2
    return jnp.concatenate([stacked[:half], stacked[half:]], axis=1)


def valid_keys(count_ref, segment):
    position = lax.broadcasted_iota(jnp.int32, (1, SEG), 1)
    return position < count_ref[0] - segment * SEG


def attend_copies(pieces, target, place_ref, sems):
    if len(pieces) == 1:
        return [pltpu.make_async_copy(pieces[0], target, sems.at[0])]
    plane, depth, core = place_ref[0], place_ref[1], place_ref[2]
    height, width = pieces[0].shape[1], target.shape[1] // 2
    slots = ((0, 0, 4), (1, 0, 4), (2, 0, 4), (3, 0, 2), (3, 2, 2))
    copies = []
    for side in range(2):
        lane = pl.multiple_of((core if side == 0 else 1 - core) * width, 128)
        for number, (turn, first, count) in enumerate(slots):
            for slot in range(count):
                chip = (plane ^ turn) * 4 + ((depth + 4 - first - slot) & 3)
                row = pl.multiple_of(chip * height, 48)
                copies.append(
                    pltpu.make_async_copy(
                        pieces[5 * side + number].at[slot, :, :width],
                        target.at[pl.ds(row, height), pl.ds(lane, width)],
                        sems.at[len(copies)],
                    )
                )
    return copies


def attend_kernel(count, count_ref, rows_ref, place_ref, bias_ref, *refs):
    pieces, (projected_ref, context_ref, joined_ref), (attend_ref, sems, out_sem) = (
        refs[:count],
        refs[count : count + 3],
        refs[count + 3 :],
    )
    step = pl.program_id(0)
    kept = pltpu.make_async_copy(attend_ref, joined_ref, out_sem)

    @pl.when(step == 0)
    def _():
        copies = attend_copies(pieces, attend_ref, place_ref, sems)
        for copy in copies:
            copy.start()
        for copy in copies:
            copy.wait()
        kept.start()

    projected_ref[...] = (dot_nn(rows_ref[...], attend_ref[...]) + bias_ref[...]).astype(LOW)
    for local in range(ROWS // SEG):
        valid = valid_keys(count_ref, step * (ROWS // SEG) + local)
        span = slice(local * SEG, (local + 1) * SEG)
        for pair in range(PAIRS):
            query, key, value = [
                projected_ref[span, part * D + pair * PAIR : part * D + (pair + 1) * PAIR]
                for part in range(3)
            ]
            probs = pair_probs(query, key, valid).astype(LOW)
            context_ref[span, pair * PAIR : (pair + 1) * PAIR] = dot_nn(
                side_by_side(probs), two_heads(value, 0)
            ).astype(LOW)

    @pl.when(step == pl.num_programs(0) - 1)
    def _():
        kept.wait()


def put_row(ref, place, start, row):
    span = slice(start, start + row.shape[1])
    here = lax.broadcasted_iota(jnp.int32, (ref.shape[0], 1), 0) == place
    ref[:, span] = jnp.where(here, row, ref[:, span])


def get_row(ref, place, span):
    here = lax.broadcasted_iota(jnp.int32, (ref.shape[0], 1), 0) == place
    return jnp.sum(jnp.where(here, ref[:, span], 0.0), axis=0, keepdims=True)


def first_row(rows, segment):
    return rows[segment * SEG : segment * SEG + 16, :].astype(F32)[:1]


def feed_kernel(
    mid_moves,
    end_moves,
    counts,
    count_ref,
    rows_ref,
    context_ref,
    place_ref,
    expand_bias_ref,
    vectors_ref,
    *refs,
):
    mid, end, refs = refs[: counts[0]], refs[counts[0] : sum(counts)], refs[sum(counts) :]
    joined, weights, sems, out_sems = refs[8:11], refs[11:14], refs[14], refs[15]
    merge_ref, expand_ref, reduce_ref = weights
    kept = [
        pltpu.make_async_copy(weight, out, out_sems.at[number])
        for number, (weight, out) in enumerate(zip(weights, joined))
    ]

    @pl.when(pl.program_id(0) == 0)
    def _():
        widths = (D, expand_ref.shape[1])
        waits = start_moves(mid, weights[:2], widths, mid_moves, place_ref, sems, 0)
        waits += start_moves(
            end, weights[2:], (D,), end_moves, place_ref, sems, 2 * len(mid_moves)
        )
        for copies, copy in zip(waits, kept):
            wait_all(copies)
            copy.start()

    feed_rows(count_ref, rows_ref, context_ref, *weights, expand_bias_ref, vectors_ref, *refs[:8])

    @pl.when(pl.program_id(0) == pl.num_programs(0) - 1)
    def _():
        wait_all(kept)


def feed_rows(
    count_ref,
    rows_ref,
    context_ref,
    merge_ref,
    expand_ref,
    reduce_ref,
    expand_bias_ref,
    vectors_ref,
    mixed_ref,
    heads_ref,
    wide_heads_ref,
    first_ref,
    normed_ref,
    active_ref,
    slope_ref,
    second_ref,
):
    step = pl.program_id(0)
    merge_bias, gain, shift, reduce_bias, final_gain, final_shift = [
        vectors_ref[row : row + 1, :] for row in range(6)
    ]
    first = rows_ref[...].astype(F32) + dot_nn(context_ref[...], merge_ref[...]) + merge_bias
    first_ref[...] = first
    normed = (centre_rows(first)[0] * gain + shift).astype(LOW)
    normed_ref[...] = normed
    second = normed.astype(F32) + reduce_bias
    chunk, wide = D, expand_ref.shape[1]
    segments = ROWS // SEG
    for start in range(0, wide, chunk):
        span = slice(start, start + chunk)
        active, slope = gelu_pair(dot_nn(normed, expand_ref[:, span]) + expand_bias_ref[:, span])
        active = active.astype(LOW)
        active_ref[:, span] = active
        slope_ref[:, span] = slope.astype(LOW)
        for local in range(segments):
            head = step * segments + local
            put_row(wide_heads_ref, head, start, slope[local * SEG : local * SEG + 1])
            put_row(wide_heads_ref, head, wide + start, first_row(active, local))
        second = second + dot_nn(active, reduce_ref[span, :])
    second_ref[...] = second
    result = centre_rows(second)[0] * final_gain + final_shift
    for local in range(segments):
        for number, rows in enumerate((result, first, second, normed, context_ref)):
            put_row(heads_ref, step * segments + local, number * D, first_row(rows, local))
    place = lax.broadcasted_iota(jnp.int32, (ROWS, 1), 0) + step * ROWS
    mixed_ref[...] = jnp.where(place < count_ref[0], result, 0.0).astype(LOW)


def feed_back_kernel(
    count_ref,
    cotangent_ref,
    second_ref,
    first_ref,
    slope_ref,
    merge_ref,
    expand_ref,
    reduce_ref,
    vectors_ref,
    branch_ref,
    hidden_ref,
    attn_ref,
    context_ref,
    first_grad_ref,
    sums_ref,
    hidden_sums_ref,
):
    step = pl.program_id(0)
    gain, final_gain = vectors_ref[1:2, :], vectors_ref[4:5, :]
    local = lax.broadcasted_iota(jnp.int32, (ROWS, 1), 0)
    plain = (local + step * ROWS < count_ref[0]) & (local % SEG != 0)
    grad = jnp.where(plain, cotangent_ref[...].astype(F32), 0.0)
    unit, spread = centre_rows(second_ref[...])
    sums = [grad * unit, grad]
    second = norm_back(grad * final_gain, unit, spread)
    branch = second.astype(LOW)
    branch_ref[...] = branch
    sums.append(branch.astype(F32))
    normed = second
    chunk = D

    @pl.when(step == 0)
    def _():
        sums_ref[...] = jnp.zeros_like(sums_ref)
        hidden_sums_ref[...] = jnp.zeros_like(hidden_sums_ref)

    for start in range(0, expand_ref.shape[1], chunk):
        span = slice(start, start + chunk)
        hidden = back_cols(branch, reduce_ref[span, :]) * slope_ref[:, span].astype(F32)
        hidden = hidden.astype(LOW)
        hidden_ref[:, span] = hidden
        hidden_sums_ref[:, span] += jnp.sum(hidden.astype(F32), axis=0, keepdims=True)
        normed = normed + back_cols(hidden, expand_ref[:, span])
    unit, spread = centre_rows(first_ref[...])
    sums += [normed * unit, normed]
    first = norm_back(normed * gain, unit, spread)
    first_grad_ref[...] = first
    attn = first.astype(LOW)
    attn_ref[...] = attn
    sums.append(attn.astype(F32))
    context_ref[...] = back_cols(attn, merge_ref[...]).astype(LOW)
    sums_ref[...] += jnp.concatenate(
        [jnp.sum(entry, axis=0, keepdims=True) for entry in sums]
        + [jnp.zeros((2, D), F32)],
        axis=0,
    )


def attend_back_kernel(
    offset,
    count_ref,
    projected_ref,
    context_ref,
    first_ref,
    mixed_in_ref,
    attend_ref,
    head_context_ref,
    head_first_ref,
    head_out_ref,
    *refs,
):
    grad_ref, tokens_ref, mixed_ref, sums_ref = refs[-4:]
    step = pl.program_id(0)
    segments = ROWS // SEG

    @pl.when(step == 0)
    def _():
        sums_ref[...] = jnp.zeros_like(sums_ref)

    is_head = lax.broadcasted_iota(jnp.int32, (16, 1), 0) == 0
    scale = HD ** (-0.5)
    for local in range(segments):
        segment = (step + offset) * segments + local
        valid = valid_keys(count_ref, segment)
        span = slice(local * SEG, (local + 1) * SEG)
        for pair in range(PAIRS):
            columns = [
                slice(part * D + pair * PAIR, part * D + (pair + 1) * PAIR) for part in range(3)
            ]
            query, key, value = [projected_ref[span, column] for column in columns]
            top = slice(local * SEG, local * SEG + 16)
            rest = slice(local * SEG + 16, (local + 1) * SEG)
            replaced = jnp.where(
                is_head,
                get_row(head_context_ref, segment, columns[0]),
                context_ref[top, columns[0]].astype(F32),
            ).astype(LOW)
            grad = jnp.concatenate([replaced, context_ref[rest, columns[0]]], axis=0)
            grad = two_heads(grad, 0)
            probs = pair_probs(query, key, valid)
            grad_probs = back_cols(grad, value)
            total = jnp.sum(grad_probs * probs, axis=-1, keepdims=True)
            scores = (probs * (grad_probs - total)).astype(LOW)
            grad_ref[span, columns[0]] = (
                dot_nn(side_by_side(scores), two_heads(key, 0)) * scale
            ).astype(LOW)
            grad_ref[span, columns[1]] = (
                cross_rows(scores, two_heads(query, 0)) * scale
            ).astype(LOW)
            grad_ref[span, columns[2]] = cross_rows(probs.astype(LOW), grad).astype(LOW)
    tokens_ref[...] = first_ref[...] + back_cols(grad_ref[...], attend_ref[...])
    mixed_ref[...] = mixed_in_ref[...]
    for local in range(segments):
        segment = (step + offset) * segments + local
        top = slice(local * SEG, local * SEG + 16)
        missing = jnp.where(is_head, get_row(head_first_ref, segment, slice(0, D)), 0.0)
        tokens_ref[top, :] += missing
        mixed_ref[top, :] = jnp.where(
            is_head,
            get_row(head_out_ref, segment, slice(0, D)),
            mixed_in_ref[top, :].astype(F32),
        ).astype(LOW)
    sums_ref[...] += jnp.sum(grad_ref[...].astype(F32), axis=0, keepdims=True)


def by_rows(width, offset=0):
    return pl.BlockSpec((ROWS, width), lambda step: (step + offset, 0))


def entire(array):
    return pl.BlockSpec(array.shape, lambda step: (0,) * array.ndim)


def row_call(kernel, name, operands, specs, outs, flops, steps=None, earlier=(), scratch=()):
    rows = next(operand.shape[0] for operand, spec in zip(operands, specs) if spec is not None)
    shapes = [jax.ShapeDtypeStruct(shape, kind) for shape, kind, _ in outs]
    moved = sum(operand.size * operand.dtype.itemsize for operand in operands)
    moved += sum(shape.size * shape.dtype.itemsize for shape in shapes)
    return pl.pallas_call(
        kernel,
        grid=(rows // ROWS if steps is None else steps,),
        in_specs=[pl.BlockSpec(memory_space=pltpu.SMEM)]
        + [entire(operand) if spec is None else spec for operand, spec in zip(operands[1:], specs[1:])]
        + [pl.BlockSpec(memory_space=pl.ANY)] * len(earlier),
        out_specs=[spec for _, _, spec in outs],
        out_shape=shapes,
        input_output_aliases={len(operands) + place: place for place in range(len(earlier))},
        scratch_shapes=scratch,
        compiler_params=pltpu.CompilerParams(vmem_limit_bytes=60 << 20),
        cost_estimate=pl.CostEstimate(flops=flops, bytes_accessed=moved, transcendentals=0),
        name=name,
    )(*operands, *earlier)


def whole_block(shape):
    return pl.BlockSpec(shape, lambda step: (0,) * len(shape))


def place_array():
    return jnp.stack(place_here()).astype(jnp.int32)


def inner_attention(rows, counts, pieces, attend_bias):
    size = rows.shape[0]
    smem, anywhere = pl.BlockSpec(memory_space=pltpu.SMEM), pl.BlockSpec(memory_space=pl.ANY)
    return row_call(
        partial(attend_kernel, len(pieces)),
        "attend",
        (counts, rows, place_array(), attend_bias, *pieces),
        (None, by_rows(D), smem, None) + (anywhere,) * len(pieces),
        [
            ((size, 3 * D), LOW, by_rows(3 * D)),
            ((size, D), LOW, by_rows(D)),
            ((D, 3 * D), LOW, anywhere),
        ],
        2 * size * D * (3 * D + 4 * SEG),
        scratch=[
            pltpu.VMEM((D, 3 * D), LOW),
            pltpu.SemaphoreType.DMA((32,)),
            pltpu.SemaphoreType.DMA,
        ],
    )


def inner_feed(rows, counts, projected, context, mid, end, expand_bias, vectors):
    size, wide = rows.shape[0], expand_bias.shape[1]
    mid_moves, end_moves = mid_moves_of(mid), mid_moves_of(end)
    smem, anywhere = pl.BlockSpec(memory_space=pltpu.SMEM), pl.BlockSpec(memory_space=pl.ANY)
    mixed, heads, wide_heads, *saved = row_call(
        partial(feed_kernel, mid_moves, end_moves, (len(mid), len(end))),
        "feed",
        (counts, rows, context, place_array(), expand_bias, vectors, *mid, *end),
        (None, by_rows(D), by_rows(D), smem, None, None) + (anywhere,) * (len(mid) + len(end)),
        [
            ((size, D), LOW, by_rows(D)),
            ((size // SEG, 5 * D), F32, whole_block((size // SEG, 5 * D))),
            ((size // SEG, 2 * wide), F32, whole_block((size // SEG, 2 * wide))),
            ((size, D), F32, by_rows(D)),
            ((size, D), LOW, by_rows(D)),
            ((size, wide), LOW, by_rows(wide)),
            ((size, wide), LOW, by_rows(wide)),
            ((size, D), F32, by_rows(D)),
            ((D, D), LOW, anywhere),
            ((D, wide), LOW, anywhere),
            ((wide, D), LOW, anywhere),
        ],
        2 * size * D * (D + 2 * wide),
        scratch=[
            pltpu.VMEM((D, D), LOW),
            pltpu.VMEM((D, wide), LOW),
            pltpu.VMEM((wide, D), LOW),
            pltpu.SemaphoreType.DMA((2 * len(mid_moves) + len(end_moves),)),
            pltpu.SemaphoreType.DMA((3,)),
        ],
    )
    return mixed, heads, wide_heads, saved[:5], saved[5:]


def inner_feed_back(cotangent, counts, saved, weights):
    merge, expand, reduce_matrix, vectors = weights
    first, normed, active, slope, second = saved
    size, wide = cotangent.shape[0], expand.shape[1]
    return row_call(
        feed_back_kernel,
        "feed_back",
        (counts, cotangent, second, first, slope, merge, expand, reduce_matrix, vectors),
        (None, by_rows(D), by_rows(D), by_rows(D), by_rows(wide), None, None, None, None),
        [
            ((size, D), LOW, by_rows(D)),
            ((size, wide), LOW, by_rows(wide)),
            ((size, D), LOW, by_rows(D)),
            ((size, D), LOW, by_rows(D)),
            ((size, D), F32, by_rows(D)),
            ((8, D), F32, whole_block((8, D))),
            ((1, wide), F32, whole_block((1, wide))),
        ],
        2 * size * D * (D + 2 * wide),
    )


def inner_attend_back(counts, operands, attend, head_rows, offset, steps, earlier):
    projected, grad_context, grad_first, mixed = operands
    size = projected.shape[0]
    return row_call(
        partial(attend_back_kernel, offset),
        "attend_back",
        (counts, projected, grad_context, grad_first, mixed, attend, *head_rows),
        (None, by_rows(3 * D, offset), by_rows(D, offset), by_rows(D, offset))
        + (by_rows(D, offset), None, None, None, None),
        [
            ((size, 3 * D), LOW, by_rows(3 * D, offset)),
            ((size, D), F32, by_rows(D, offset)),
            ((size, D), LOW, by_rows(D, offset)),
            ((1, 3 * D), F32, whole_block((1, 3 * D))),
        ],
        2 * steps * ROWS * D * (3 * D + 10 * SEG),
        steps,
        earlier,
    )


AXES = ("dp", "fsdp")


def gather(rows):
    return lax.all_gather(rows, AXES, axis=0, tiled=True)


def scatter(rows):
    return lax.psum_scatter(rows, AXES, scatter_dimension=0, tiled=True)


def split_cols(packed, widths):
    pieces, start = [], 0
    for width in widths:
        pieces.append(packed[..., start : start + width])
        start += width
    return pieces


def pack_kernel(*refs):
    vectors, place_ref, out_ref, rows_ref = refs[:16], refs[16], refs[17], refs[18]
    rows_ref[...] = jnp.zeros_like(rows_ref)
    for row, ref in enumerate(vectors):
        rows_ref[row : row + 1, : ref.shape[1]] = ref[...].astype(F32)
    place = jnp.transpose(place_ref[...].astype(F32))
    rows_ref[16 : 16 + SEGS, : place.shape[1]] = place
    out_ref[...] = rows_ref[...].astype(LOW)


def pack_small(vectors, segment_place):
    return pl.pallas_call(
        pack_kernel,
        out_shape=jax.ShapeDtypeStruct((16 + SEGS, 128), LOW),
        scratch_shapes=[pltpu.VMEM((16 + SEGS, 128), F32)],
        name="pack",
    )(*[vector[None] for vector in vectors], segment_place)


def spread_row(rows, size, width):
    devices = rows.shape[0]
    lane = lax.broadcasted_iota(jnp.int32, (128, width), 1)
    owner = lane // size
    pick = (lane - owner * size == lax.broadcasted_iota(jnp.int32, (128, width), 0)).astype(LOW)
    spread = dot_nn(rows, pick)
    row = lax.broadcasted_iota(jnp.int32, (devices, width), 0)
    owner = lax.broadcasted_iota(jnp.int32, (devices, width), 1) // size
    return jnp.sum(jnp.where(row == owner, spread, 0.0), axis=0, keepdims=True)


VECTOR_ROWS = (1, 2, 3, 5, 6, 7)


def unpack_kernel(sizes, place_ref, *refs):
    outs, got_ref, sems = refs[-9:-2], refs[-2], refs[-1]
    pieces = refs[:-9]
    plane, depth = place_ref[0], place_ref[1]
    if len(pieces) == 1:
        copies = [pltpu.make_async_copy(pieces[0], got_ref, sems.at[0])]
    else:
        copies = []
        slots = ((0, 0, 4), (1, 0, 4), (2, 0, 4), (3, 0, 2), (3, 2, 2))
        first_lane = pieces[0].shape[2] - 128
        for piece, (turn, first, count) in zip(pieces, slots):
            for slot in range(count):
                chip = (plane ^ turn) * 4 + ((depth + 4 - first - slot) & 3)
                copies.append(
                    pltpu.make_async_copy(
                        piece.at[slot, :, first_lane : first_lane + 128],
                        got_ref.at[pl.ds(pl.multiple_of(48 * chip, 48), 48), :],
                        sems.at[len(copies)],
                    )
                )
    for copy in copies:
        copy.start()
    for copy in copies:
        copy.wait()
    got = got_ref[...].astype(F32).reshape(-1, 16 + SEGS, 128)
    devices = got.shape[0]
    for block in range(2):
        attend_ref, expand_ref, vectors_ref = outs[3 * block : 3 * block + 3]
        for kind in range(8):
            row = 8 * block + kind
            size = sizes[row]
            spread = spread_row(got[:, row, :].astype(LOW), size, size * devices)
            if kind == 0:
                attend_ref[...] = spread
            elif kind == 4:
                expand_ref[...] = spread
            else:
                place = VECTOR_ROWS.index(kind)
                vectors_ref[place : place + 1, :] = spread
        vectors_ref[6:8, :] = jnp.zeros((2, vectors_ref.shape[1]), F32)
    for segment in range(SEGS):
        outs[6][segment : segment + 1, :] = spread_row(
            got[:, 16 + segment, :].astype(LOW), sizes[16], sizes[16] * devices
        )


def unpack_small(sizes, devices, pieces):
    shapes = []
    for block in range(2):
        for rows, size in ((1, sizes[8 * block]), (1, sizes[8 * block + 4]), (8, sizes[1])):
            shapes.append(jax.ShapeDtypeStruct((rows, size * devices), F32))
    shapes.append(jax.ShapeDtypeStruct((SEGS, sizes[16] * devices), F32))
    return pl.pallas_call(
        partial(unpack_kernel, sizes),
        out_shape=shapes,
        in_specs=[pl.BlockSpec(memory_space=pltpu.SMEM)]
        + [pl.BlockSpec(memory_space=pl.ANY)] * len(pieces),
        scratch_shapes=[
            pltpu.VMEM((devices * (16 + SEGS), 128), LOW),
            pltpu.SemaphoreType.DMA((16,)),
        ],
        compiler_params=pltpu.CompilerParams(vmem_limit_bytes=60 << 20),
        name="unpack",
    )(place_array(), *pieces)


def sum_rows(rows, gate):
    devices, size = rows.shape
    padded = jnp.pad(rows, ((0, 0), (0, -size % 1024))).reshape(devices, -1, 128)
    got = lax.all_to_all(padded, AXES, split_axis=0, concat_axis=0, tiled=True)
    return jnp.sum(after(gate, got), axis=0).reshape(-1)[:size]


def hop(array, turn):
    return lax.ppermute(array, AXES, [(place, turn(place)) for place in range(32)])


def over_x(array):
    return hop(array, lambda place: place ^ 8)


def over_y(array):
    return hop(array, lambda place: place ^ 16)


def over_core(array):
    return hop(array, lambda place: place ^ 1)


def over_z(array, step):
    return hop(array, lambda place: (place & ~6) | ((((place >> 1) + step) & 3) << 1))


def place_here():
    chip = lax.axis_index("fsdp")
    return lax.axis_index("dp"), chip // 2, chip % 2


def half_cols(array, core):
    width = array.shape[-1] // 2
    return lax.dynamic_slice_in_dim(array, core * width, width, axis=array.ndim - 1)


def fold_rows(array, rows):
    return jnp.concatenate(jnp.split(array, array.shape[0] // rows, axis=0), axis=1)


def unfold_cols(array, width):
    return jnp.concatenate(jnp.split(array, array.shape[1] // width, axis=1), axis=0)


def both_cores(mine, other, core, axis):
    return jnp.concatenate(
        [jnp.where(core == 0, mine, other), jnp.where(core == 0, other, mine)], axis=axis
    )


def attend_line(shard, small):
    core = place_here()[2]
    mine = jnp.concatenate([half_cols(shard, core), small], axis=1)
    sent = jnp.concatenate([half_cols(shard, 1 - core), small], axis=1)
    slab = both_cores(mine, over_core(sent), core, 0)
    hops = [over_z(slab, step) for step in (1, 2, 3)]
    return slab, jnp.stack([slab] + hops)


def attend_pieces(line):
    line_x, line_y = over_x(line), over_y(line)
    pieces = [line, line_x, line_y, over_y(line_x[:2]), over_x(line_y[2:])]
    return pieces + [over_core(piece) for piece in pieces]


def after(first, *later):
    tied = lax.optimization_barrier((first, later))[1]
    return tied[0] if len(tied) == 1 else tied


def half_rows(line):
    half = line.shape[0] // 2
    return lax.dynamic_slice_in_dim(line, place_here()[2] * half, half, axis=0)


def first_hops(line, mine):
    return line, over_x(mine), over_y(mine)


def last_hops(hops, gate, late_gate=()):
    line, from_x, from_y = hops
    half = from_x.shape[0] // 2
    sent_y, sent_x = after(gate, from_x[:half], from_y[half:])
    pieces = [from_x, from_y, over_y(sent_y), over_x(sent_x)]
    return [line] + pieces + [over_core(piece) for piece in after(late_gate, *pieces)]


def late_hops(shard):
    return shard, over_x(shard), over_y(shard)


def late_pieces(hops, gate):
    shard, from_x, from_y = hops
    half = shard.shape[0] // 2
    sent_y, sent_x = after(gate, from_x[:half], from_y[half:])
    across = jnp.concatenate([over_y(sent_y), over_x(sent_x)], axis=0)
    rows = jnp.concatenate([shard, from_x, from_y, across], axis=0)
    return [lax.all_gather(rows, "fsdp", axis=0, tiled=True)]


def along_z(shards):
    return lax.all_gather(jnp.concatenate(shards, axis=1), "fsdp", axis=0, tiled=True)


def start_moves(pieces, outs, widths, moves, place_ref, sems, first):
    plane, core = place_ref[0], place_ref[2]
    groups, start = [], 0
    for out, width in zip(outs, widths):
        copies = []
        for piece, source, rows, turn, quarter, side, offset in moves:
            row = (plane ^ turn) * quarter + offset
            if side is not None:
                row = row + (core if side == 0 else 1 - core) * (quarter // 2)
            copies.append(
                pltpu.make_async_copy(
                    pieces[piece].at[source : source + rows, start : start + width],
                    out.at[pl.ds(pl.multiple_of(row, 48), rows), :],
                    sems.at[first],
                )
            )
            first += 1
        start += width
        groups.append(copies)
    for copies in groups:
        for copy in copies:
            copy.start()
    return groups


def wait_all(copies):
    for copy in copies:
        copy.wait()


def column_sums(rows):
    return jnp.sum(rows, axis=0, keepdims=True)


def feed_rows_back(grad, unit, spread, slope_of, reduce_ref, expand_ref, final_gain):
    second = norm_back(grad * final_gain, unit, spread)
    branch = second.astype(LOW)
    normed, hidden = second, []
    for start in range(0, expand_ref.shape[1], D):
        span = slice(start, start + D)
        part = (back_cols(branch, reduce_ref[span, :]) * slope_of(span)).astype(LOW)
        hidden.append(part)
        normed = normed + back_cols(part, expand_ref[:, span])
    return branch, hidden, normed


def heads_kernel(
    counts,
    mid_moves,
    end_moves,
    place_ref,
    count_ref,
    heads_ref,
    wide_heads_ref,
    table_ref,
    cotangent_ref,
    attend_bias_ref,
    expand_bias_ref,
    vectors_ref,
    inner_vectors_ref,
    *refs,
):
    mid_count, end_count = counts
    mid, refs = refs[:mid_count], refs[mid_count:]
    end, refs = refs[:end_count], refs[end_count:]
    inner_hbm, refs = refs[:3], refs[3:]
    out_ref, grad_ref, left_ref, right_ref, sums_ref = refs[:5]
    branch_ref, hidden_ref, attn_ref, context_ref, first_ref, inner_sums_ref, hidden_sums_ref = refs[5:12]
    attend_ref, merge_ref, expand_ref, reduce_ref = refs[12:16]
    inner_refs, sems = refs[16:19], refs[19]
    wide = expand_ref.shape[1]
    waits = start_moves(
        mid, (attend_ref, merge_ref, expand_ref), (3 * D, D, wide), mid_moves, place_ref, sems, 0
    )
    first_free = 3 * len(mid_moves)
    waits += start_moves(end, (reduce_ref,), (D,), end_moves, place_ref, sems, first_free)
    first_free += len(end_moves)
    inner_waits = [
        pltpu.make_async_copy(source, target, sems.at[first_free + number])
        for number, (source, target) in enumerate(zip(inner_hbm, inner_refs))
    ]
    for copy in inner_waits:
        copy.start()
    merge_bias, gain, shift, reduce_bias, final_gain, final_shift = [
        vectors_ref[row : row + 1, :] for row in range(6)
    ]
    scale = HD ** (-0.5)
    stacked = HEADS * SEGS
    own = (
        lax.broadcasted_iota(jnp.int32, (stacked, D), 1) // HD
        == lax.broadcasted_iota(jnp.int32, (stacked, D), 0) // SEGS
    )

    def by_head(rows):
        return jnp.where(own, jnp.concatenate([rows] * HEADS, axis=0), 0.0).astype(LOW)

    def join_heads(rows):
        rows = jnp.where(own, rows, 0.0)
        return sum(rows[SEGS * head : SEGS * (head + 1)] for head in range(HEADS))

    keep = (
        lax.broadcasted_iota(jnp.int32, (SEGS, 1), 0) * SEG < count_ref[0]
    ).astype(F32)
    source = (heads_ref[:, :D] + table_ref[...]).astype(LOW)
    wait_all(waits[0])
    projected = (dot_nn(source, attend_ref[...]) + attend_bias_ref[...]).astype(LOW)
    query, key, value = projected[:, :D], projected[:, D : 2 * D], projected[:, 2 * D :]
    queries = by_head(query.astype(F32))
    scores = back_cols(queries, key) * scale
    weight = jnp.exp(scores - jnp.max(scores, axis=-1, keepdims=True))
    probs = weight / jnp.sum(weight, axis=-1, keepdims=True)
    probs_low = probs.astype(LOW)
    context = join_heads(dot_nn(probs_low, value)).astype(LOW)
    wait_all(waits[1])
    first = source.astype(F32) + dot_nn(context, merge_ref[...]) + merge_bias
    first_unit, first_spread = centre_rows(first)
    normed = (first_unit * gain + shift).astype(LOW)
    left_ref[:, :D] = source
    left_ref[:, D : 2 * D] = context
    left_ref[:, 2 * D : 3 * D] = normed
    second = normed.astype(F32) + reduce_bias
    slopes = {}
    wait_all(waits[2])
    wait_all(waits[3])
    for start in range(0, wide, D):
        span = slice(start, start + D)
        active, slopes[start] = gelu_pair(
            dot_nn(normed, expand_ref[:, span]) + expand_bias_ref[:, span]
        )
        active = active.astype(LOW)
        left_ref[:, 3 * D + start : 4 * D + start] = active
        second = second + dot_nn(active, reduce_ref[span, :])
    unit, spread = centre_rows(second)
    out_ref[...] = (unit * final_gain + final_shift) * keep
    grad = cotangent_ref[...].astype(F32) * keep
    sums = [column_sums(grad * unit), column_sums(grad)]
    branch, hidden, grad_normed = feed_rows_back(
        grad, unit, spread, lambda span: slopes[span.start], reduce_ref, expand_ref, final_gain
    )
    sums += [column_sums(grad_normed * first_unit), column_sums(grad_normed)]
    grad_first = norm_back(grad_normed * gain, first_unit, first_spread)
    attn = grad_first.astype(LOW)
    grads = by_head(back_cols(attn, merge_ref[...]).astype(LOW).astype(F32))
    grad_probs = back_cols(grads, value)
    total = jnp.sum(grad_probs * probs, axis=-1, keepdims=True)
    grad_scores = (probs * (grad_probs - total)).astype(LOW)
    grad_query = (join_heads(dot_nn(grad_scores, key)) * scale).astype(LOW)
    grad_key = (cross_rows(grad_scores, queries) * scale).astype(LOW)
    grad_value = cross_rows(probs_low, grads).astype(LOW)
    grad_projected = jnp.concatenate([grad_query, grad_key, grad_value], axis=1)
    right_ref[:, : 3 * D] = grad_projected
    right_ref[:, 3 * D : 4 * D] = attn
    for number, part in enumerate(hidden):
        right_ref[:, (4 + number) * D : (5 + number) * D] = part
    right_ref[:, 4 * D + wide :] = branch
    sums_ref[...] = jnp.concatenate(sums + [jnp.zeros((4, D), F32)], axis=0)
    grad = grad_first + back_cols(grad_projected, attend_ref[...])
    grad_ref[...] = grad

    wait_all(inner_waits)
    inner_merge_ref, inner_expand_ref, inner_reduce_ref = inner_refs
    gain, final_gain = inner_vectors_ref[1:2, :], inner_vectors_ref[4:5, :]
    first_unit, first_spread = centre_rows(heads_ref[:, D : 2 * D])
    unit, spread = centre_rows(heads_ref[:, 2 * D : 3 * D])
    sums = [column_sums(grad * unit), column_sums(grad)]
    branch, hidden, grad_normed = feed_rows_back(
        grad,
        unit,
        spread,
        lambda span: wide_heads_ref[:, span],
        inner_reduce_ref,
        inner_expand_ref,
        final_gain,
    )
    branch_ref[...] = branch
    sums.append(column_sums(branch.astype(F32)))
    for number, part in enumerate(hidden):
        span = slice(number * D, (number + 1) * D)
        hidden_ref[:, span] = part
        hidden_sums_ref[:, span] = column_sums(part.astype(F32))
    sums += [column_sums(grad_normed * first_unit), column_sums(grad_normed)]
    grad_first = norm_back(grad_normed * gain, first_unit, first_spread)
    first_ref[...] = grad_first
    attn = grad_first.astype(LOW)
    attn_ref[...] = attn
    sums.append(column_sums(attn.astype(F32)))
    context_ref[...] = back_cols(attn, inner_merge_ref[...]).astype(LOW).astype(F32)
    inner_sums_ref[...] = jnp.concatenate(sums + [jnp.zeros((2, D), F32)], axis=0)


def mid_moves_of(pieces):
    if len(pieces) == 1:
        return [(0, 0, pieces[0].shape[0], 0, 0, None, 0)]
    quarter = pieces[0].shape[0]
    half = quarter // 2
    moves = [(0, 0, quarter, 0, quarter, None, 0)]
    for side in range(2):
        moves += [
            (1 + 4 * side, 0, half, 1, quarter, side, 0),
            (2 + 4 * side, 0, half, 2, quarter, side, 0),
            (3 + 4 * side, 0, half // 2, 3, quarter, side, 0),
            (4 + 4 * side, 0, half // 2, 3, quarter, side, half // 2),
        ]
    return moves


def late_moves_of(piece, linked):
    if not linked:
        return [(0, 0, piece.shape[0], 0, 0, None, 0)]
    rows = piece.shape[0] // 32
    return [
        (0, (4 * slot + turn) * rows, rows, turn, 8 * rows, None, slot * rows)
        for slot in range(8)
        for turn in range(4)
    ]


def heads_step(counts, heads, wide_heads, table, cotangent, small, mid, late, inner, linked):
    attend_bias, expand_bias, vectors, inner_vectors = small
    wide = expand_bias.shape[1]
    mid_moves, end_moves = mid_moves_of(mid), late_moves_of(late, linked)
    plane, depth, core = place_here()
    place = jnp.stack([plane, depth, core]).astype(jnp.int32)
    vmem = pl.BlockSpec(memory_space=pltpu.VMEM)
    smem = pl.BlockSpec(memory_space=pltpu.SMEM)
    outs = [
        ((SEGS, D), F32),
        ((SEGS, D), F32),
        ((SEGS, 3 * D + wide), LOW),
        ((SEGS, 5 * D + wide), LOW),
        ((8, D), F32),
        ((SEGS, D), LOW),
        ((SEGS, wide), LOW),
        ((SEGS, D), LOW),
        ((SEGS, D), F32),
        ((SEGS, D), F32),
        ((8, D), F32),
        ((1, wide), F32),
    ]
    flops = 6 * SEGS * D * (5 * D + 4 * wide)
    moved = 2 * D * (6 * D + 4 * wide)
    return pl.pallas_call(
        partial(heads_kernel, (len(mid), 1), mid_moves, end_moves),
        out_shape=[jax.ShapeDtypeStruct(shape, kind) for shape, kind in outs],
        in_specs=[smem, smem] + [vmem] * 8 + [pl.BlockSpec(memory_space=pl.ANY)] * (len(mid) + 4),
        out_specs=[vmem] * len(outs),
        scratch_shapes=[
            pltpu.VMEM((D, 3 * D), LOW),
            pltpu.VMEM((D, D), LOW),
            pltpu.VMEM((D, wide), LOW),
            pltpu.VMEM((wide, D), LOW),
            pltpu.VMEM((D, D), LOW),
            pltpu.VMEM((D, wide), LOW),
            pltpu.VMEM((wide, D), LOW),
            pltpu.SemaphoreType.DMA((3 * len(mid_moves) + len(end_moves) + 3,)),
        ],
        compiler_params=pltpu.CompilerParams(vmem_limit_bytes=60 << 20),
        cost_estimate=pl.CostEstimate(flops=flops, bytes_accessed=moved, transcendentals=0),
        name="heads",
    )(
        place,
        counts,
        heads,
        wide_heads,
        table,
        cotangent,
        attend_bias,
        expand_bias,
        vectors,
        inner_vectors,
        *mid,
        late,
        *inner,
    )


UNIT = 384


def grads_kernel(jobs, adds, side_ref, *refs):
    refs, came_ref, out_ref = refs[: -1 - adds], refs[-2], refs[-1]
    unit = pl.program_id(0)

    def put(chips, units, shape, total):
        total = total.reshape(shape)
        if adds:
            total = total + came_ref[chips, units].astype(F32)
        out_ref[chips, units] = total.astype(LOW)

    for folded, first, count, number in jobs:
        (left_ref, right_ref), heads, refs = refs[:2], refs[2:number], refs[number:]

        @pl.when((unit >= first) & (unit < first + count))
        def _(folded=folded, first=first, left_ref=left_ref, right_ref=right_ref, heads=heads):
            total = cross_rows(left_ref[...], right_ref[...])
            if heads:
                total = total + cross_rows(heads[0][...].astype(LOW), heads[1][...])
            if folded:
                chips = pl.ds(4 * (unit - first), 4)
                put(chips, slice(first, first + 4), (4, 4, 48, UNIT), total)
            else:
                put(slice(None), pl.ds(unit, 1), (16, 1, 48, UNIT), total)


def half_grads(jobs, side, came=None):
    rules, operands, specs, first = [], [], [], 0
    for left, right, head_left, column, head_right in jobs:
        folded = left.shape[1] > D
        count = left.shape[1] // D if folded else right.shape[1] // (2 * UNIT)
        start = first

        def place(unit, start=start, count=count):
            return lax.min(lax.max(unit - start, 0), count - 1)

        def left_index(unit, side, place=place, folded=folded):
            return (0, place(unit) if folded else 0)

        def right_index(unit, side, place=place, folded=folded, count=count):
            return (0, side[0] if folded else side[0] * count + place(unit))

        def head_index(unit, side, place=place, folded=folded, column=column):
            return (0, column + (place(unit) if folded else 0))

        operands += [left, right]
        specs += [
            pl.BlockSpec((left.shape[0], D), left_index),
            pl.BlockSpec((right.shape[0], UNIT), right_index),
        ]
        if head_left is not None:
            operands += [head_left, head_right]
            specs += [
                pl.BlockSpec((SEGS, D), head_index),
                pl.BlockSpec((SEGS, UNIT), right_index),
            ]
        rules.append((folded, first, count, 2 if head_left is None else 4))
        first += count
    shape = (16, first, 48, UNIT)
    whole = pl.BlockSpec(shape, lambda unit, side: (0, 0, 0, 0))
    if came is not None:
        operands.append(came)
        specs.append(whole)
    size = operands[0].shape[0]
    return pl.pallas_call(
        partial(grads_kernel, rules, int(came is not None)),
        grid_spec=pltpu.PrefetchScalarGridSpec(
            num_scalar_prefetch=1, grid=(first,), in_specs=specs, out_specs=whole
        ),
        out_shape=jax.ShapeDtypeStruct(shape, LOW),
        compiler_params=pltpu.CompilerParams(vmem_limit_bytes=60 << 20),
        cost_estimate=pl.CostEstimate(
            flops=2 * first * size * D * UNIT, bytes_accessed=30 << 20, transcendentals=0
        ),
        name="half_grads",
    )(side.astype(jnp.int32)[None], *operands)


def scatter_planes(kept):
    plane = place_here()[0]
    kept = kept.reshape(4, 4, *kept.shape[1:])
    return [
        lax.dynamic_index_in_dim(kept, plane ^ turn, axis=0, keepdims=False)
        for turn in range(4)
    ]


def scatter_across(planes, gate):
    here, next_x, next_y, across = planes
    from_y, from_x = over_y(across[:2]), over_x(across[2:])
    next_x, next_y = after(gate, next_x, next_y)
    next_x = jnp.concatenate([next_x[:2] + from_y, next_x[2:]], axis=0)
    next_y = jnp.concatenate([next_y[:2], next_y[2:] + from_x], axis=0)
    return here, next_x, next_y


def scatter_next(here, next_x, next_y, gate):
    came_x, came_y = after(gate, over_x(next_x), over_y(next_y))
    return (
        here.astype(jnp.float32) + came_x.astype(jnp.float32) + came_y.astype(jnp.float32)
    ).astype(jnp.bfloat16)


def scatter_line(here):
    depth = place_here()[1]
    slabs = [
        lax.dynamic_index_in_dim(here, (depth + step) & 3, axis=0, keepdims=False)
        for step in range(4)
    ]
    total = slabs[0].astype(jnp.float32)
    for step in (1, 2, 3):
        total = total + over_z(slabs[step], step).astype(jnp.float32)
    return total


def scatter_along(here):
    chips = here.shape[0]
    groups = [[2 * chip + core for chip in range(chips)] for core in range(2)]
    total = lax.psum_scatter(
        here.reshape(-1, here.shape[-1]),
        "fsdp",
        scatter_dimension=0,
        axis_index_groups=groups,
        tiled=True,
    )
    return total.reshape(here.shape[1:]).astype(jnp.float32)


def scatter_end(total, shapes):
    core = place_here()[2]
    mine, sent, start = [], [], 0
    for height, width in shapes:
        groups = height // 768
        count = groups if groups > 1 else width // (2 * UNIT)
        rows = jnp.concatenate(
            [total[unit] for unit in range(start, start + count)], axis=0 if groups > 1 else 1
        )
        start += count
        mine.append(fold_rows(lax.dynamic_slice_in_dim(rows, core * 24 * groups, 24 * groups), 24))
        sent.append(
            fold_rows(lax.dynamic_slice_in_dim(rows, (1 - core) * 24 * groups, 24 * groups), 24)
        )
    other = over_core(jnp.concatenate(sent, axis=1))
    owned, start = [], 0
    for (height, width), part in zip(shapes, mine):
        width = width // 2
        pair = [unfold_cols(side, width) for side in (part, other[:, start : start + part.shape[1]])]
        owned.append(both_cores(pair[0], pair[1], core, 1))
        start += part.shape[1]
    return owned


def unfold(packed, parts, ratio):
    width = packed.shape[1] // ratio
    return jnp.stack(
        [
            packed[:, width * group : width * (group + 1)].reshape(-1, parts, width)
            for group in range(ratio)
        ],
        axis=1,
    ).reshape(-1, width)


def gather_flat(shards):
    parts = min(shard.shape[0] for shard in shards)
    pieces = split_cols(
        gather(jnp.concatenate([fold_rows(shard, parts) for shard in shards], axis=1)),
        [shard.size // parts for shard in shards],
    )
    return [
        unfold(piece, parts, shard.shape[0] // parts) if shard.shape[0] > parts else piece
        for piece, shard in zip(pieces, shards)
    ]


def scatter_flat(grads):
    devices = lax.axis_size(AXES)
    parts = min(grad.shape[0] for grad in grads) // devices
    packed = jnp.concatenate(
        [
            jnp.transpose(grad.reshape(devices, -1, parts, grad.shape[1]), (0, 2, 1, 3)).reshape(
                devices * parts, -1
            )
            for grad in grads
        ],
        axis=1,
    )
    owned = split_cols(
        scatter(packed).astype(jnp.float32), [grad.size // (devices * parts) for grad in grads]
    )
    return [unfold_cols(piece, grad.shape[1]) for piece, grad in zip(owned, grads)]


def on_device(
    tokens,
    counts,
    inner_attend,
    inner_attend_bias,
    inner_merge,
    inner_merge_bias,
    inner_gain,
    inner_shift,
    inner_expand,
    inner_expand_bias,
    inner_reduce,
    inner_reduce_bias,
    inner_final_gain,
    inner_final_shift,
    outer_attend,
    outer_attend_bias,
    outer_merge,
    outer_merge_bias,
    outer_gain,
    outer_shift,
    outer_expand,
    outer_expand_bias,
    outer_reduce,
    outer_reduce_bias,
    outer_final_gain,
    outer_final_shift,
    segment_place,
    cotangent,
):
    parts = inner_merge.shape[0]
    devices = D // parts
    ratio = inner_reduce.shape[0] // parts
    here = lax.axis_index(AXES)
    linked = lax.axis_size("dp") == 4 and lax.axis_size("fsdp") == 8
    wide = inner_expand.shape[1]
    inner_rest = [inner_merge, inner_expand, inner_reduce]
    outer_all = [outer_attend, outer_merge, outer_expand, outer_reduce]
    docs = counts.shape[0]
    head_cotangent = cotangent.reshape(docs * SEGS, SEG, D)[:, 0, :]
    small_parts = (
        inner_attend_bias,
        inner_merge_bias,
        inner_gain,
        inner_shift,
        inner_expand_bias,
        inner_reduce_bias,
        inner_final_gain,
        inner_final_shift,
        outer_attend_bias,
        outer_merge_bias,
        outer_gain,
        outer_shift,
        outer_expand_bias,
        outer_reduce_bias,
        outer_final_gain,
        outer_final_shift,
    )
    sizes = [part.shape[0] for part in small_parts] + [parts]
    small = pack_small(small_parts, segment_place)
    if linked:
        slab, line = attend_line(inner_attend, small)
        late_first = late_hops(after(slab, outer_reduce))
        line = after(late_first[1:], line)
        pieces = attend_pieces(line)
        late = late_pieces(late_first, (pieces[3], pieces[4]))
        mid_line = along_z(after(line, *inner_rest[:2]))
        end_line = along_z([after(line, inner_rest[2])])
        outer_line = along_z(after(line, *outer_all[:3]))
        small_pieces = pieces[:5]
    else:
        pieces = gather_flat([inner_attend])
        small_pieces = [gather(small)]
    (
        attend_bias,
        expand_bias,
        vectors,
        outer_attend_bias_full,
        outer_expand_bias_full,
        outer_vectors,
        place_rows,
    ) = unpack_small(sizes, devices, small_pieces)
    if linked:
        mid_half = half_rows(after((pieces[3], pieces[4], attend_bias), mid_line))
        attend_bias = after(mid_half, attend_bias)
    projected, context, attend = inner_attention(tokens, counts, pieces, attend_bias)
    if linked:
        mid = first_hops(mid_line, mid_half)
        end = first_hops(end_line, half_rows(after((context, mid[1], mid[2]), end_line)))
        mid = last_hops(mid, context)
        end = last_hops(end, (mid[3], mid[4]))
        outer = first_hops(
            outer_line, half_rows(after((mid[3], mid[4], end[1], end[2]), outer_line))
        )
    else:
        rest = gather_flat(inner_rest)
        mid, end = [jnp.concatenate(rest[:2], axis=1)], rest[2:]
    mixed, heads, wide_heads, saved, inner_full = inner_feed(
        tokens, counts, projected, context, mid, end, expand_bias, vectors
    )
    inner_weights = (*inner_full, vectors)
    branch, grad_hidden, grad_attn, grad_context, grad_first, inner_sums, hidden_sums = (
        inner_feed_back(cotangent, counts, saved, inner_weights)
    )
    if linked:
        outer = last_hops(outer, heads, inner_sums)
    else:
        outer_full = gather_flat(outer_all)
        outer, late = [jnp.concatenate(outer_full[:3], axis=1)], outer_full[3:]
    first, normed, active, slope, second = saved
    low = jnp.bfloat16
    (
        head_out,
        grad_heads,
        left_pack,
        right_pack,
        outer_sums,
        head_branch,
        head_hidden,
        head_attn,
        head_context,
        head_first,
        head_sums,
        head_hidden_sums,
    ) = heads_step(
        counts,
        heads,
        wide_heads,
        place_rows,
        head_cotangent,
        (outer_attend_bias_full, outer_expand_bias_full, outer_vectors, vectors),
        outer,
        late[0],
        inner_full,
        linked,
    )
    grad_place = jnp.transpose(jnp.sum(grad_heads.reshape(docs, SEGS, D), axis=0))
    inner_sums = inner_sums + head_sums
    hidden_sums = hidden_sums + head_hidden_sums
    operands = (projected, grad_context, grad_first, mixed)
    head_rows = (head_context, head_first, head_out)
    steps = tokens.shape[0] // ROWS
    right_all = gather(right_pack)

    def left_factors(left_pack):
        rows = jnp.concatenate(
            [
                factor.reshape(factor.shape[0], devices, -1)
                for factor in split_cols(left_pack, (D, D, D, wide))
            ],
            axis=2,
        )
        return jnp.transpose(rows, (1, 0, 2))

    def exchange(rows):
        return lax.all_to_all(rows, AXES, split_axis=0, concat_axis=0, tiled=True)

    def outer_grads(left_all, right_all):
        left_all = left_all.reshape(-1, left_all.shape[-1])
        left_pieces = split_cols(left_all, (parts, parts, parts, parts * ratio))
        right_pieces = split_cols(right_all, (3 * D, D, wide, D))
        big = [cross_rows(left, right) for left, right in zip(left_pieces, right_pieces)]
        bias = [
            lax.dynamic_slice_in_dim(
                jnp.sum(right.astype(jnp.float32), axis=0), here * width, width, axis=0
            )
            for right, width in zip(right_pieces, (3 * parts, parts, wide // devices, parts))
        ]
        return big, bias

    if linked:
        core = place_here()[2]
        jobs = [
            (normed, grad_hidden, heads, 3, head_hidden),
            (active, branch, wide_heads, wide // D, head_branch),
            (context, grad_attn, heads, 4, head_attn),
        ]
        sent = half_grads(jobs, 1 - core)
        left_all = exchange(left_factors(after(sent, left_pack)))
        part = inner_attend_back(
            counts, after(sent, *operands), attend, head_rows, 0, 1, ()
        )
        kept = half_grads(jobs, after((part[3], left_all), core), over_core(sent))
        planes = scatter_planes(kept)
        middle = inner_attend_back(
            counts, after(planes, *operands), attend, head_rows, 1, 1, part[:3]
        )
        tall = scatter_across(planes, middle[3])
        rest = inner_attend_back(
            counts, after(tall, *operands), attend, head_rows, 2, steps - 2, middle[:3]
        )
        grad_projected, tokens_grad, mixed = rest[:3]
        attend_sums = part[3] + middle[3] + rest[3]
        outer_big, outer_bias = outer_grads(*after(rest[3], left_all, right_all))
        jobs = [(tokens, grad_projected, None, 0, None)]
        tall = scatter_next(*tall, (outer_big, outer_bias))
        sent = half_grads(jobs, after(tall, 1 - core))
        tall = scatter_along(tall)
        kept = half_grads(jobs, core, over_core(sent))
        short = scatter_next(*scatter_across(scatter_planes(kept), ()), ())
        sums_gate = short
        short = scatter_line(short)
        own_expand, own_reduce, own_merge = scatter_end(tall, [(D, wide), (wide, D), (D, D)])
        (own_attend,) = scatter_end(short, [(D, 3 * D)])
    else:
        sums_gate = ()
        left_all = exchange(left_factors(left_pack))
        outer_big, outer_bias = outer_grads(left_all, right_all)
        grad_projected, tokens_grad, mixed, attend_sums = inner_attend_back(
            counts, operands, attend, head_rows, 0, steps, ()
        )
        grad_attend = cross_rows(tokens, grad_projected).astype(low)
        grad_reduce, grad_expand, grad_merge = [
            (cross_rows(left, right) + cross_rows(head_left.astype(low), head_right)).astype(low)
            for left, right, head_left, head_right in (
                (active, branch, wide_heads[:, wide:], head_branch),
                (normed, grad_hidden, heads[:, 3 * D : 4 * D], head_hidden),
                (context, grad_attn, heads[:, 4 * D :], head_attn),
            )
        ]
        own_expand, own_reduce = scatter_flat([grad_expand, grad_reduce])
        own_attend, own_merge = scatter_flat([grad_attend, grad_merge])
    row_sums = (
        attend_sums,
        inner_sums[5],
        inner_sums[3],
        inner_sums[4],
        hidden_sums,
        inner_sums[2],
        inner_sums[0],
        inner_sums[1],
        outer_sums[2],
        outer_sums[3],
        outer_sums[0],
        outer_sums[1],
        grad_place,
    )
    sums = sum_rows(jnp.concatenate([entry.reshape(devices, -1) for entry in row_sums], axis=1), sums_gate)
    sums = split_cols(sums, [entry.size // devices for entry in row_sums])
    return (
        mixed,
        tokens_grad,
        own_attend,
        sums[0],
        own_merge,
        sums[1],
        sums[2],
        sums[3],
        own_expand,
        sums[4],
        own_reduce,
        sums[5],
        sums[6],
        sums[7],
        outer_big[0],
        outer_bias[0],
        outer_big[1],
        outer_bias[1],
        sums[8],
        sums[9],
        outer_big[2],
        outer_bias[2],
        outer_big[3],
        outer_bias[3],
        sums[10],
        sums[11],
        sums[12].reshape(parts, SEGS),
    )


def solution(mesh):
    return jax.shard_map(
        on_device,
        mesh=mesh,
        in_specs=(
            P(("dp", "fsdp"), None),
            P(("dp", "fsdp")),
            P(("dp", "fsdp"), None),
            P(("dp", "fsdp")),
            P(("dp", "fsdp"), None),
            P(("dp", "fsdp")),
            P(("dp", "fsdp")),
            P(("dp", "fsdp")),
            P(("dp", "fsdp"), None),
            P(("dp", "fsdp")),
            P(("dp", "fsdp"), None),
            P(("dp", "fsdp")),
            P(("dp", "fsdp")),
            P(("dp", "fsdp")),
            P(("dp", "fsdp"), None),
            P(("dp", "fsdp")),
            P(("dp", "fsdp"), None),
            P(("dp", "fsdp")),
            P(("dp", "fsdp")),
            P(("dp", "fsdp")),
            P(("dp", "fsdp"), None),
            P(("dp", "fsdp")),
            P(("dp", "fsdp"), None),
            P(("dp", "fsdp")),
            P(("dp", "fsdp")),
            P(("dp", "fsdp")),
            P(("dp", "fsdp"), None),
            P(("dp", "fsdp"), None),
        ),
        out_specs=(
            P(("dp", "fsdp"), None),
            P(("dp", "fsdp"), None),
            P(("dp", "fsdp"), None),
            P(("dp", "fsdp")),
            P(("dp", "fsdp"), None),
            P(("dp", "fsdp")),
            P(("dp", "fsdp")),
            P(("dp", "fsdp")),
            P(("dp", "fsdp"), None),
            P(("dp", "fsdp")),
            P(("dp", "fsdp"), None),
            P(("dp", "fsdp")),
            P(("dp", "fsdp")),
            P(("dp", "fsdp")),
            P(("dp", "fsdp"), None),
            P(("dp", "fsdp")),
            P(("dp", "fsdp"), None),
            P(("dp", "fsdp")),
            P(("dp", "fsdp")),
            P(("dp", "fsdp")),
            P(("dp", "fsdp"), None),
            P(("dp", "fsdp")),
            P(("dp", "fsdp"), None),
            P(("dp", "fsdp")),
            P(("dp", "fsdp")),
            P(("dp", "fsdp")),
            P(("dp", "fsdp"), None),
        ),
        check_vma=False,
    )
```

```python
from functools import partial

import jax
import jax.numpy as jnp
from jax import lax
from jax.experimental import pallas as pl
from jax.experimental.pallas import tpu as pltpu
from jax.sharding import PartitionSpec as P

D = 768
HEADS = 12
HD = 64
SEG = 128
SLOTS = 1024
SEGS = 8


def cross_rows(left_rows, right_rows):
    return lax.dot_general(
        left_rows, right_rows, (((0,), (0,)), ((), ())), preferred_element_type=jnp.float32
    )


def back_cols(left_rows, right_rows):
    return lax.dot_general(
        left_rows, right_rows, (((1,), (1,)), ((), ())), preferred_element_type=jnp.float32
    )


ROWS = 256
PAIR = 2 * HD
PAIRS = HEADS // 2
F32 = jnp.float32
LOW = jnp.bfloat16


def dot_nn(left, right):
    return jnp.dot(left, right, preferred_element_type=F32)


def centre_rows(rows):
    centred = rows - jnp.mean(rows, axis=-1, keepdims=True)
    spread = lax.rsqrt(jnp.mean(centred * centred, axis=-1, keepdims=True) + 1e-05)
    return centred * spread, spread


def norm_back(grad, unit, spread):
    return spread * (
        grad
        - jnp.mean(grad, axis=-1, keepdims=True)
        - unit * jnp.mean(grad * unit, axis=-1, keepdims=True)
    )


def gelu_pair(hidden):
    size = jnp.abs(hidden)
    bell = jnp.exp(hidden * hidden * -0.5)
    t = 1.0 / (1.0 + (0.3275911 * 0.7071067811865476) * size)
    poly = t * (
        0.127414796
        + t * (-0.142248368 + t * (0.7107068705 + t * (-0.7265760135 + t * 0.5307027145)))
    )
    tail = poly * bell
    phi = jnp.where(hidden >= 0, 1.0 - tail, tail)
    return hidden * phi, phi + hidden * bell * 0.3989422804014327


def two_heads(pair, axis):
    first = lax.broadcasted_iota(jnp.int32, pair.shape, 1) < HD
    zero = jnp.zeros_like(pair)
    return jnp.concatenate([jnp.where(first, pair, zero), jnp.where(first, zero, pair)], axis=axis)


def pair_probs(query, key, valid):
    scores = back_cols(two_heads(query, 0), key) * HD ** (-0.5)
    scores = jnp.where(valid, scores, -1e30)
    weight = jnp.exp(scores - jnp.max(scores, axis=-1, keepdims=True))
    return weight / jnp.sum(weight, axis=-1, keepdims=True)


def side_by_side(stacked):
    half = stacked.shape[0] // 2
    return jnp.concatenate([stacked[:half], stacked[half:]], axis=1)


def valid_keys(count_ref, segment):
    position = lax.broadcasted_iota(jnp.int32, (1, SEG), 1)
    return position < count_ref[0] - segment * SEG


def attend_copies(pieces, target, place_ref, sems):
    if len(pieces) == 1:
        return [pltpu.make_async_copy(pieces[0], target, sems.at[0])]
    plane, depth, core = place_ref[0], place_ref[1], place_ref[2]
    height, width = pieces[0].shape[1], target.shape[1] // 2
    slots = ((0, 0, 4), (1, 0, 4), (2, 0, 4), (3, 0, 2), (3, 2, 2))
    copies = []
    for side in range(2):
        lane = pl.multiple_of((core if side == 0 else 1 - core) * width, 128)
        for number, (turn, first, count) in enumerate(slots):
            for slot in range(count):
                chip = (plane ^ turn) * 4 + ((depth + 4 - first - slot) & 3)
                row = pl.multiple_of(chip * height, 48)
                copies.append(
                    pltpu.make_async_copy(
                        pieces[5 * side + number].at[slot, :, :width],
                        target.at[pl.ds(row, height), pl.ds(lane, width)],
                        sems.at[len(copies)],
                    )
                )
    return copies


def attend_kernel(count, small_count, size, count_ref, rows_ref, place_ref, *refs):
    pieces, small, refs = refs[:count], refs[count : count + small_count], refs[count + small_count :]
    projected_ref, context_ref, probs_ref, joined_ref = refs[:4]
    attend_ref, bias_ref, got_ref, sems, small_sems, out_sem = refs[4:]
    step = pl.program_id(0)
    kept = pltpu.make_async_copy(attend_ref, joined_ref, out_sem)

    @pl.when(step == 0)
    def _():
        small_waits = small_copies(small, got_ref, place_ref, small_sems)
        copies = attend_copies(pieces, attend_ref, place_ref, sems)
        for copy in small_waits + copies:
            copy.start()
        wait_all(small_waits)
        first_rows = got_ref[...].astype(F32).reshape(-1, 16 + SEGS, 128)[:, 0, :]
        bias_ref[...] = spread_row(first_rows.astype(LOW), size, bias_ref.shape[1])
        wait_all(copies)
        kept.start()

    projected_ref[...] = (dot_nn(rows_ref[...], attend_ref[...]) + bias_ref[...]).astype(LOW)
    for local in range(ROWS // SEG):
        valid = valid_keys(count_ref, step * (ROWS // SEG) + local)
        span = slice(local * SEG, (local + 1) * SEG)
        for pair in range(PAIRS):
            query, key, value = [
                projected_ref[span, part * D + pair * PAIR : part * D + (pair + 1) * PAIR]
                for part in range(3)
            ]
            probs = side_by_side(pair_probs(query, key, valid).astype(LOW))
            probs_ref[span, pair * 2 * SEG : (pair + 1) * 2 * SEG] = probs
            context_ref[span, pair * PAIR : (pair + 1) * PAIR] = dot_nn(
                probs, two_heads(value, 0)
            ).astype(LOW)

    @pl.when(step == pl.num_programs(0) - 1)
    def _():
        kept.wait()


def put_row(ref, place, start, row):
    span = slice(start, start + row.shape[1])
    here = lax.broadcasted_iota(jnp.int32, (ref.shape[0], 1), 0) == place
    ref[:, span] = jnp.where(here, row, ref[:, span])


def get_row(ref, place, span):
    here = lax.broadcasted_iota(jnp.int32, (ref.shape[0], 1), 0) == place
    return jnp.sum(jnp.where(here, ref[:, span], 0.0), axis=0, keepdims=True)


def first_row(rows, segment):
    return rows[segment * SEG : segment * SEG + 16, :].astype(F32)[:1]


def feed_kernel(
    mid_moves,
    end_moves,
    counts,
    count_ref,
    rows_ref,
    context_ref,
    place_ref,
    expand_bias_ref,
    vectors_ref,
    *refs,
):
    mid, end, refs = refs[: counts[0]], refs[counts[0] : sum(counts)], refs[sum(counts) :]
    joined, weights, sems, out_sems = refs[8:11], refs[11:14], refs[14], refs[15]
    merge_ref, expand_ref, reduce_ref = weights
    kept = [
        pltpu.make_async_copy(weight, out, out_sems.at[number])
        for number, (weight, out) in enumerate(zip(weights, joined))
    ]

    @pl.when(pl.program_id(0) == 0)
    def _():
        widths = (D, expand_ref.shape[1])
        waits = start_moves(mid, weights[:2], widths, mid_moves, place_ref, sems, 0)
        waits += start_moves(
            end, weights[2:], (D,), end_moves, place_ref, sems, 2 * len(mid_moves)
        )
        for copies, copy in zip(waits, kept):
            wait_all(copies)
            copy.start()

    feed_rows(count_ref, rows_ref, context_ref, *weights, expand_bias_ref, vectors_ref, *refs[:8])

    @pl.when(pl.program_id(0) == pl.num_programs(0) - 1)
    def _():
        wait_all(kept)


def feed_rows(
    count_ref,
    rows_ref,
    context_ref,
    merge_ref,
    expand_ref,
    reduce_ref,
    expand_bias_ref,
    vectors_ref,
    mixed_ref,
    heads_ref,
    wide_heads_ref,
    first_ref,
    normed_ref,
    active_ref,
    slope_ref,
    second_ref,
):
    step = pl.program_id(0)
    merge_bias, gain, shift, reduce_bias, final_gain, final_shift = [
        vectors_ref[row : row + 1, :] for row in range(6)
    ]
    first = rows_ref[...].astype(F32) + dot_nn(context_ref[...], merge_ref[...]) + merge_bias
    first_ref[...] = first
    normed = (centre_rows(first)[0] * gain + shift).astype(LOW)
    normed_ref[...] = normed
    second = normed.astype(F32) + reduce_bias
    chunk, wide = D, expand_ref.shape[1]
    segments = ROWS // SEG
    for start in range(0, wide, chunk):
        span = slice(start, start + chunk)
        active, slope = gelu_pair(dot_nn(normed, expand_ref[:, span]) + expand_bias_ref[:, span])
        active = active.astype(LOW)
        active_ref[:, span] = active
        slope_ref[:, span] = slope.astype(LOW)
        for local in range(segments):
            head = step * segments + local
            put_row(wide_heads_ref, head, start, slope[local * SEG : local * SEG + 1])
            put_row(wide_heads_ref, head, wide + start, first_row(active, local))
        second = second + dot_nn(active, reduce_ref[span, :])
    second_ref[...] = second
    result = centre_rows(second)[0] * final_gain + final_shift
    for local in range(segments):
        for number, rows in enumerate((result, first, second, normed, context_ref)):
            put_row(heads_ref, step * segments + local, number * D, first_row(rows, local))
    place = lax.broadcasted_iota(jnp.int32, (ROWS, 1), 0) + step * ROWS
    mixed_ref[...] = jnp.where(place < count_ref[0], result, 0.0).astype(LOW)


def feed_back_kernel(
    count_ref,
    cotangent_ref,
    second_ref,
    first_ref,
    slope_ref,
    merge_ref,
    expand_ref,
    reduce_ref,
    vectors_ref,
    branch_ref,
    hidden_ref,
    attn_ref,
    context_ref,
    first_grad_ref,
    sums_ref,
    hidden_sums_ref,
):
    step = pl.program_id(0)
    gain, final_gain = vectors_ref[1:2, :], vectors_ref[4:5, :]
    local = lax.broadcasted_iota(jnp.int32, (ROWS, 1), 0)
    plain = (local + step * ROWS < count_ref[0]) & (local % SEG != 0)
    grad = jnp.where(plain, cotangent_ref[...].astype(F32), 0.0)
    unit, spread = centre_rows(second_ref[...])
    sums = [grad * unit, grad]
    second = norm_back(grad * final_gain, unit, spread)
    branch = second.astype(LOW)
    branch_ref[...] = branch
    sums.append(branch.astype(F32))
    normed = second
    chunk = D

    @pl.when(step == 0)
    def _():
        sums_ref[...] = jnp.zeros_like(sums_ref)
        hidden_sums_ref[...] = jnp.zeros_like(hidden_sums_ref)

    for start in range(0, expand_ref.shape[1], chunk):
        span = slice(start, start + chunk)
        hidden = back_cols(branch, reduce_ref[span, :]) * slope_ref[:, span].astype(F32)
        hidden = hidden.astype(LOW)
        hidden_ref[:, span] = hidden
        hidden_sums_ref[:, span] += jnp.sum(hidden.astype(F32), axis=0, keepdims=True)
        normed = normed + back_cols(hidden, expand_ref[:, span])
    unit, spread = centre_rows(first_ref[...])
    sums += [normed * unit, normed]
    first = norm_back(normed * gain, unit, spread)
    first_grad_ref[...] = first
    attn = first.astype(LOW)
    attn_ref[...] = attn
    sums.append(attn.astype(F32))
    context_ref[...] = back_cols(attn, merge_ref[...]).astype(LOW)
    sums_ref[...] += jnp.concatenate(
        [jnp.sum(entry, axis=0, keepdims=True) for entry in sums]
        + [jnp.zeros((2, D), F32)],
        axis=0,
    )


def attend_back_kernel(
    offset,
    projected_ref,
    probs_ref,
    context_ref,
    first_ref,
    mixed_in_ref,
    attend_ref,
    head_context_ref,
    head_first_ref,
    head_out_ref,
    *refs,
):
    grad_ref, tokens_ref, mixed_ref, sums_ref = refs[-4:]
    step = pl.program_id(0)
    segments = ROWS // SEG

    @pl.when(step == 0)
    def _():
        sums_ref[...] = jnp.zeros_like(sums_ref)

    is_head = lax.broadcasted_iota(jnp.int32, (16, 1), 0) == 0
    scale = HD ** (-0.5)
    for local in range(segments):
        segment = (step + offset) * segments + local
        span = slice(local * SEG, (local + 1) * SEG)
        for pair in range(PAIRS):
            columns = [
                slice(part * D + pair * PAIR, part * D + (pair + 1) * PAIR) for part in range(3)
            ]
            query, key, value = [projected_ref[span, column] for column in columns]
            top = slice(local * SEG, local * SEG + 16)
            rest = slice(local * SEG + 16, (local + 1) * SEG)
            replaced = jnp.where(
                is_head,
                get_row(head_context_ref, segment, columns[0]),
                context_ref[top, columns[0]].astype(F32),
            ).astype(LOW)
            grad = jnp.concatenate([replaced, context_ref[rest, columns[0]]], axis=0)
            grad = two_heads(grad, 0)
            probs = probs_ref[span, pair * 2 * SEG : (pair + 1) * 2 * SEG]
            probs_low = jnp.concatenate([probs[:, :SEG], probs[:, SEG:]], axis=0)
            probs = probs_low.astype(F32)
            grad_probs = back_cols(grad, value)
            total = jnp.sum(grad_probs * probs, axis=-1, keepdims=True)
            scores = (probs * (grad_probs - total)).astype(LOW)
            grad_ref[span, columns[0]] = (
                dot_nn(side_by_side(scores), two_heads(key, 0)) * scale
            ).astype(LOW)
            grad_ref[span, columns[1]] = (
                cross_rows(scores, two_heads(query, 0)) * scale
            ).astype(LOW)
            grad_ref[span, columns[2]] = cross_rows(probs_low, grad).astype(LOW)
    tokens_ref[...] = first_ref[...] + back_cols(grad_ref[...], attend_ref[...])
    mixed_ref[...] = mixed_in_ref[...]
    for local in range(segments):
        segment = (step + offset) * segments + local
        top = slice(local * SEG, local * SEG + 16)
        missing = jnp.where(is_head, get_row(head_first_ref, segment, slice(0, D)), 0.0)
        tokens_ref[top, :] += missing
        mixed_ref[top, :] = jnp.where(
            is_head,
            get_row(head_out_ref, segment, slice(0, D)),
            mixed_in_ref[top, :].astype(F32),
        ).astype(LOW)
    sums_ref[...] += jnp.sum(grad_ref[...].astype(F32), axis=0, keepdims=True)


def by_rows(width, offset=0):
    return pl.BlockSpec((ROWS, width), lambda step: (step + offset, 0))


def entire(array):
    return pl.BlockSpec(array.shape, lambda step: (0,) * array.ndim)


def row_call(kernel, name, operands, specs, outs, flops, steps=None, earlier=(), scratch=()):
    rows = outs[0][0][0]
    shapes = [jax.ShapeDtypeStruct(shape, kind) for shape, kind, _ in outs]
    moved = sum(operand.size * operand.dtype.itemsize for operand in operands)
    moved += sum(shape.size * shape.dtype.itemsize for shape in shapes)
    return pl.pallas_call(
        kernel,
        grid=(rows // ROWS if steps is None else steps,),
        in_specs=[
            entire(operand) if spec is None else spec for operand, spec in zip(operands, specs)
        ]
        + [pl.BlockSpec(memory_space=pl.ANY)] * len(earlier),
        out_specs=[spec for _, _, spec in outs],
        out_shape=shapes,
        input_output_aliases={len(operands) + place: place for place in range(len(earlier))},
        scratch_shapes=scratch,
        compiler_params=pltpu.CompilerParams(vmem_limit_bytes=60 << 20),
        cost_estimate=pl.CostEstimate(flops=flops, bytes_accessed=moved, transcendentals=0),
        name=name,
    )(*operands, *earlier)


def whole_block(shape):
    return pl.BlockSpec(shape, lambda step: (0,) * len(shape))


def place_array():
    return jnp.stack(place_here()).astype(jnp.int32)


def inner_attention(rows, counts, pieces, small_pieces, bias_size):
    size = rows.shape[0]
    devices = D * 3 // bias_size
    smem, anywhere = pl.BlockSpec(memory_space=pltpu.SMEM), pl.BlockSpec(memory_space=pl.ANY)
    return row_call(
        partial(attend_kernel, len(pieces), len(small_pieces), bias_size),
        "attend",
        (counts, rows, place_array(), *pieces, *small_pieces),
        (smem, by_rows(D), smem) + (anywhere,) * (len(pieces) + len(small_pieces)),
        [
            ((size, 3 * D), LOW, by_rows(3 * D)),
            ((size, D), LOW, by_rows(D)),
            ((size, HEADS * SEG), LOW, by_rows(HEADS * SEG)),
            ((D, 3 * D), LOW, anywhere),
        ],
        2 * size * D * (3 * D + 4 * SEG),
        scratch=[
            pltpu.VMEM((D, 3 * D), LOW),
            pltpu.VMEM((1, 3 * D), F32),
            pltpu.VMEM((devices * (16 + SEGS), 128), LOW),
            pltpu.SemaphoreType.DMA((32,)),
            pltpu.SemaphoreType.DMA((16,)),
            pltpu.SemaphoreType.DMA,
        ],
    )


def inner_feed(rows, counts, projected, context, mid, end, expand_bias, vectors):
    size, wide = rows.shape[0], expand_bias.shape[1]
    mid_moves, end_moves = mid_moves_of(mid), mid_moves_of(end)
    smem, anywhere = pl.BlockSpec(memory_space=pltpu.SMEM), pl.BlockSpec(memory_space=pl.ANY)
    mixed, heads, wide_heads, *saved = row_call(
        partial(feed_kernel, mid_moves, end_moves, (len(mid), len(end))),
        "feed",
        (counts, rows, context, place_array(), expand_bias, vectors, *mid, *end),
        (smem, by_rows(D), by_rows(D), smem, None, None) + (anywhere,) * (len(mid) + len(end)),
        [
            ((size, D), LOW, by_rows(D)),
            ((size // SEG, 5 * D), F32, whole_block((size // SEG, 5 * D))),
            ((size // SEG, 2 * wide), F32, whole_block((size // SEG, 2 * wide))),
            ((size, D), F32, by_rows(D)),
            ((size, D), LOW, by_rows(D)),
            ((size, wide), LOW, by_rows(wide)),
            ((size, wide), LOW, by_rows(wide)),
            ((size, D), F32, by_rows(D)),
            ((D, D), LOW, anywhere),
            ((D, wide), LOW, anywhere),
            ((wide, D), LOW, anywhere),
        ],
        2 * size * D * (D + 2 * wide),
        scratch=[
            pltpu.VMEM((D, D), LOW),
            pltpu.VMEM((D, wide), LOW),
            pltpu.VMEM((wide, D), LOW),
            pltpu.SemaphoreType.DMA((2 * len(mid_moves) + len(end_moves),)),
            pltpu.SemaphoreType.DMA((3,)),
        ],
    )
    return mixed, heads, wide_heads, saved[:5], saved[5:]


def inner_feed_back(cotangent, counts, saved, weights):
    merge, expand, reduce_matrix, vectors = weights
    first, normed, active, slope, second = saved
    size, wide = cotangent.shape[0], expand.shape[1]
    return row_call(
        feed_back_kernel,
        "feed_back",
        (counts, cotangent, second, first, slope, merge, expand, reduce_matrix, vectors),
        (pl.BlockSpec(memory_space=pltpu.SMEM), by_rows(D), by_rows(D), by_rows(D), by_rows(wide))
        + (None,) * 4,
        [
            ((size, D), LOW, by_rows(D)),
            ((size, wide), LOW, by_rows(wide)),
            ((size, D), LOW, by_rows(D)),
            ((size, D), LOW, by_rows(D)),
            ((size, D), F32, by_rows(D)),
            ((8, D), F32, whole_block((8, D))),
            ((1, wide), F32, whole_block((1, wide))),
        ],
        2 * size * D * (D + 2 * wide),
    )


def inner_attend_back(operands, attend, head_rows, offset, steps, earlier):
    projected, probs, grad_context, grad_first, mixed = operands
    size = projected.shape[0]
    return row_call(
        partial(attend_back_kernel, offset),
        "attend_back",
        (projected, probs, grad_context, grad_first, mixed, attend, *head_rows),
        (by_rows(3 * D, offset), by_rows(HEADS * SEG, offset), by_rows(D, offset))
        + (by_rows(D, offset), by_rows(D, offset), None, None, None, None),
        [
            ((size, 3 * D), LOW, by_rows(3 * D, offset)),
            ((size, D), F32, by_rows(D, offset)),
            ((size, D), LOW, by_rows(D, offset)),
            ((1, 3 * D), F32, whole_block((1, 3 * D))),
        ],
        2 * steps * ROWS * D * (3 * D + 10 * SEG),
        steps,
        earlier,
    )


AXES = ("dp", "fsdp")


def gather(rows):
    return lax.all_gather(rows, AXES, axis=0, tiled=True)


def scatter(rows):
    return lax.psum_scatter(rows, AXES, scatter_dimension=0, tiled=True)


def split_cols(packed, widths):
    pieces, start = [], 0
    for width in widths:
        pieces.append(packed[..., start : start + width])
        start += width
    return pieces


def pack_kernel(*refs):
    vectors, place_ref, out_ref, rows_ref = refs[:16], refs[16], refs[17], refs[18]
    rows_ref[...] = jnp.zeros_like(rows_ref)
    for row, ref in enumerate(vectors):
        rows_ref[row : row + 1, : ref.shape[1]] = ref[...].astype(F32)
    place = jnp.transpose(place_ref[...].astype(F32))
    rows_ref[16 : 16 + SEGS, : place.shape[1]] = place
    out_ref[...] = rows_ref[...].astype(LOW)


def pack_small(vectors, segment_place):
    return pl.pallas_call(
        pack_kernel,
        out_shape=jax.ShapeDtypeStruct((16 + SEGS, 128), LOW),
        scratch_shapes=[pltpu.VMEM((16 + SEGS, 128), F32)],
        name="pack",
    )(*[vector[None] for vector in vectors], segment_place)


def spread_row(rows, size, width):
    devices = rows.shape[0]
    lane = lax.broadcasted_iota(jnp.int32, (128, width), 1)
    owner = lane // size
    pick = (lane - owner * size == lax.broadcasted_iota(jnp.int32, (128, width), 0)).astype(LOW)
    spread = dot_nn(rows, pick)
    row = lax.broadcasted_iota(jnp.int32, (devices, width), 0)
    owner = lax.broadcasted_iota(jnp.int32, (devices, width), 1) // size
    return jnp.sum(jnp.where(row == owner, spread, 0.0), axis=0, keepdims=True)


VECTOR_ROWS = (1, 2, 3, 5, 6, 7)


def small_copies(pieces, got_ref, place_ref, sems):
    if len(pieces) == 1:
        return [pltpu.make_async_copy(pieces[0], got_ref, sems.at[0])]
    plane, depth = place_ref[0], place_ref[1]
    copies = []
    slots = ((0, 0, 4), (1, 0, 4), (2, 0, 4), (3, 0, 2), (3, 2, 2))
    first_lane = pieces[0].shape[2] - 128
    for piece, (turn, first, count) in zip(pieces, slots):
        for slot in range(count):
            chip = (plane ^ turn) * 4 + ((depth + 4 - first - slot) & 3)
            copies.append(
                pltpu.make_async_copy(
                    piece.at[slot, :, first_lane : first_lane + 128],
                    got_ref.at[pl.ds(pl.multiple_of(48 * chip, 48), 48), :],
                    sems.at[len(copies)],
                )
            )
    return copies


def unpack_kernel(sizes, place_ref, *refs):
    outs, got_ref, sems = (None, *refs[-8:-2]), refs[-2], refs[-1]
    pieces = refs[:-8]
    copies = small_copies(pieces, got_ref, place_ref, sems)
    for copy in copies:
        copy.start()
    wait_all(copies)
    got = got_ref[...].astype(F32).reshape(-1, 16 + SEGS, 128)
    devices = got.shape[0]
    for block in range(2):
        attend_ref, expand_ref, vectors_ref = outs[3 * block : 3 * block + 3]
        for kind in range(1 - block, 8):
            row = 8 * block + kind
            size = sizes[row]
            spread = spread_row(got[:, row, :].astype(LOW), size, size * devices)
            if kind == 0:
                attend_ref[...] = spread
            elif kind == 4:
                expand_ref[...] = spread
            else:
                place = VECTOR_ROWS.index(kind)
                vectors_ref[place : place + 1, :] = spread
        vectors_ref[6:8, :] = jnp.zeros((2, vectors_ref.shape[1]), F32)
    for segment in range(SEGS):
        outs[6][segment : segment + 1, :] = spread_row(
            got[:, 16 + segment, :].astype(LOW), sizes[16], sizes[16] * devices
        )


def unpack_small(sizes, devices, pieces):
    shapes = []
    for block in range(2):
        for rows, size in ((1, sizes[8 * block]), (1, sizes[8 * block + 4]), (8, sizes[1])):
            shapes.append(jax.ShapeDtypeStruct((rows, size * devices), F32))
    shapes.append(jax.ShapeDtypeStruct((SEGS, sizes[16] * devices), F32))
    return pl.pallas_call(
        partial(unpack_kernel, sizes),
        out_shape=shapes[1:],
        in_specs=[pl.BlockSpec(memory_space=pltpu.SMEM)]
        + [pl.BlockSpec(memory_space=pl.ANY)] * len(pieces),
        scratch_shapes=[
            pltpu.VMEM((devices * (16 + SEGS), 128), LOW),
            pltpu.SemaphoreType.DMA((16,)),
        ],
        compiler_params=pltpu.CompilerParams(vmem_limit_bytes=60 << 20),
        name="unpack",
    )(place_array(), *pieces)


def sum_rows(rows, gate):
    devices, size = rows.shape
    padded = jnp.pad(rows, ((0, 0), (0, -size % 1024))).reshape(devices, -1, 128)
    got = lax.all_to_all(padded, AXES, split_axis=0, concat_axis=0, tiled=True)
    return jnp.sum(after(gate, got), axis=0).reshape(-1)[:size]


def hop(array, turn):
    return lax.ppermute(array, AXES, [(place, turn(place)) for place in range(32)])


def over_x(array):
    return hop(array, lambda place: place ^ 8)


def over_y(array):
    return hop(array, lambda place: place ^ 16)


def over_core(array):
    return hop(array, lambda place: place ^ 1)


def over_z(array, step):
    return hop(array, lambda place: (place & ~6) | ((((place >> 1) + step) & 3) << 1))


def place_here():
    chip = lax.axis_index("fsdp")
    return lax.axis_index("dp"), chip // 2, chip % 2


def half_cols(array, core):
    width = array.shape[-1] // 2
    return lax.dynamic_slice_in_dim(array, core * width, width, axis=array.ndim - 1)


def fold_rows(array, rows):
    return jnp.concatenate(jnp.split(array, array.shape[0] // rows, axis=0), axis=1)


def unfold_cols(array, width):
    return jnp.concatenate(jnp.split(array, array.shape[1] // width, axis=1), axis=0)


def both_cores(mine, other, core, axis):
    return jnp.concatenate(
        [jnp.where(core == 0, mine, other), jnp.where(core == 0, other, mine)], axis=axis
    )


def attend_line(shard, small):
    core = place_here()[2]
    mine = jnp.concatenate([half_cols(shard, core), small], axis=1)
    sent = jnp.concatenate([half_cols(shard, 1 - core), small], axis=1)
    slab = both_cores(mine, over_core(sent), core, 0)
    hops = [over_z(slab, step) for step in (1, 2, 3)]
    return slab, jnp.stack([slab] + hops)


def attend_pieces(line):
    line_x, line_y = over_x(line), over_y(line)
    pieces = [line, line_x, line_y, over_y(line_x[:2]), over_x(line_y[2:])]
    return pieces + [over_core(piece) for piece in pieces]


def after(first, *later):
    tied = lax.optimization_barrier((first, later))[1]
    return tied[0] if len(tied) == 1 else tied


def half_rows(line):
    half = line.shape[0] // 2
    return lax.dynamic_slice_in_dim(line, place_here()[2] * half, half, axis=0)


def first_hops(line, mine):
    return line, over_x(mine), over_y(mine)


def last_hops(hops, gate, late_gate=()):
    line, from_x, from_y = hops
    half = from_x.shape[0] // 2
    sent_y, sent_x = after(gate, from_x[:half], from_y[half:])
    pieces = [from_x, from_y, over_y(sent_y), over_x(sent_x)]
    return [line] + pieces + [over_core(piece) for piece in after(late_gate, *pieces)]


def late_hops(shard):
    return shard, over_x(shard), over_y(shard)


def late_pieces(hops, gate):
    shard, from_x, from_y = hops
    half = shard.shape[0] // 2
    sent_y, sent_x = after(gate, from_x[:half], from_y[half:])
    across = jnp.concatenate([over_y(sent_y), over_x(sent_x)], axis=0)
    rows = jnp.concatenate([shard, from_x, from_y, across], axis=0)
    return [lax.all_gather(rows, "fsdp", axis=0, tiled=True)]


def along_z(shards):
    return lax.all_gather(jnp.concatenate(shards, axis=1), "fsdp", axis=0, tiled=True)


def start_moves(pieces, outs, widths, moves, place_ref, sems, first):
    plane, core = place_ref[0], place_ref[2]
    groups, start = [], 0
    for out, width in zip(outs, widths):
        copies = []
        for piece, source, rows, turn, quarter, side, offset in moves:
            row = (plane ^ turn) * quarter + offset
            if side is not None:
                row = row + (core if side == 0 else 1 - core) * (quarter // 2)
            copies.append(
                pltpu.make_async_copy(
                    pieces[piece].at[source : source + rows, start : start + width],
                    out.at[pl.ds(pl.multiple_of(row, 48), rows), :],
                    sems.at[first],
                )
            )
            first += 1
        start += width
        groups.append(copies)
    for copies in groups:
        for copy in copies:
            copy.start()
    return groups


def wait_all(copies):
    for copy in copies:
        copy.wait()


def column_sums(rows):
    return jnp.sum(rows, axis=0, keepdims=True)


def feed_rows_back(grad, unit, spread, slope_of, reduce_ref, expand_ref, final_gain):
    second = norm_back(grad * final_gain, unit, spread)
    branch = second.astype(LOW)
    normed, hidden = second, []
    for start in range(0, expand_ref.shape[1], D):
        span = slice(start, start + D)
        part = (back_cols(branch, reduce_ref[span, :]) * slope_of(span)).astype(LOW)
        hidden.append(part)
        normed = normed + back_cols(part, expand_ref[:, span])
    return branch, hidden, normed


def heads_kernel(
    counts,
    mid_moves,
    end_moves,
    place_ref,
    count_ref,
    heads_ref,
    wide_heads_ref,
    table_ref,
    cotangent_ref,
    attend_bias_ref,
    expand_bias_ref,
    vectors_ref,
    inner_vectors_ref,
    *refs,
):
    mid_count, end_count = counts
    mid, refs = refs[:mid_count], refs[mid_count:]
    end, refs = refs[:end_count], refs[end_count:]
    inner_hbm, refs = refs[:3], refs[3:]
    out_ref, grad_ref, left_ref, right_ref, sums_ref = refs[:5]
    branch_ref, hidden_ref, attn_ref, context_ref, first_ref, inner_sums_ref, hidden_sums_ref = refs[5:12]
    attend_ref, merge_ref, expand_ref, reduce_ref = refs[12:16]
    inner_refs, sems = refs[16:19], refs[19]
    wide = expand_ref.shape[1]
    waits = start_moves(
        mid, (attend_ref, merge_ref, expand_ref), (3 * D, D, wide), mid_moves, place_ref, sems, 0
    )
    first_free = 3 * len(mid_moves)
    waits += start_moves(end, (reduce_ref,), (D,), end_moves, place_ref, sems, first_free)
    first_free += len(end_moves)
    inner_waits = [
        pltpu.make_async_copy(source, target, sems.at[first_free + number])
        for number, (source, target) in enumerate(zip(inner_hbm, inner_refs))
    ]
    for copy in inner_waits:
        copy.start()
    merge_bias, gain, shift, reduce_bias, final_gain, final_shift = [
        vectors_ref[row : row + 1, :] for row in range(6)
    ]
    scale = HD ** (-0.5)
    stacked = HEADS * SEGS
    own = (
        lax.broadcasted_iota(jnp.int32, (stacked, D), 1) // HD
        == lax.broadcasted_iota(jnp.int32, (stacked, D), 0) // SEGS
    )

    def by_head(rows):
        return jnp.where(own, jnp.concatenate([rows] * HEADS, axis=0), 0.0).astype(LOW)

    def join_heads(rows):
        rows = jnp.where(own, rows, 0.0)
        return sum(rows[SEGS * head : SEGS * (head + 1)] for head in range(HEADS))

    keep = (
        lax.broadcasted_iota(jnp.int32, (SEGS, 1), 0) * SEG < count_ref[0]
    ).astype(F32)
    source = (heads_ref[:, :D] + table_ref[...]).astype(LOW)
    wait_all(waits[0])
    projected = (dot_nn(source, attend_ref[...]) + attend_bias_ref[...]).astype(LOW)
    query, key, value = projected[:, :D], projected[:, D : 2 * D], projected[:, 2 * D :]
    queries = by_head(query.astype(F32))
    scores = back_cols(queries, key) * scale
    weight = jnp.exp(scores - jnp.max(scores, axis=-1, keepdims=True))
    probs = weight / jnp.sum(weight, axis=-1, keepdims=True)
    probs_low = probs.astype(LOW)
    context = join_heads(dot_nn(probs_low, value)).astype(LOW)
    wait_all(waits[1])
    first = source.astype(F32) + dot_nn(context, merge_ref[...]) + merge_bias
    first_unit, first_spread = centre_rows(first)
    normed = (first_unit * gain + shift).astype(LOW)
    left_ref[:, :D] = source
    left_ref[:, D : 2 * D] = context
    left_ref[:, 2 * D : 3 * D] = normed
    second = normed.astype(F32) + reduce_bias
    slopes = {}
    wait_all(waits[2])
    wait_all(waits[3])
    for start in range(0, wide, D):
        span = slice(start, start + D)
        active, slopes[start] = gelu_pair(
            dot_nn(normed, expand_ref[:, span]) + expand_bias_ref[:, span]
        )
        active = active.astype(LOW)
        left_ref[:, 3 * D + start : 4 * D + start] = active
        second = second + dot_nn(active, reduce_ref[span, :])
    unit, spread = centre_rows(second)
    out_ref[...] = (unit * final_gain + final_shift) * keep
    grad = cotangent_ref[...].astype(F32) * keep
    sums = [column_sums(grad * unit), column_sums(grad)]
    branch, hidden, grad_normed = feed_rows_back(
        grad, unit, spread, lambda span: slopes[span.start], reduce_ref, expand_ref, final_gain
    )
    sums += [column_sums(grad_normed * first_unit), column_sums(grad_normed)]
    grad_first = norm_back(grad_normed * gain, first_unit, first_spread)
    attn = grad_first.astype(LOW)
    grads = by_head(back_cols(attn, merge_ref[...]).astype(LOW).astype(F32))
    grad_probs = back_cols(grads, value)
    total = jnp.sum(grad_probs * probs, axis=-1, keepdims=True)
    grad_scores = (probs * (grad_probs - total)).astype(LOW)
    grad_query = (join_heads(dot_nn(grad_scores, key)) * scale).astype(LOW)
    grad_key = (cross_rows(grad_scores, queries) * scale).astype(LOW)
    grad_value = cross_rows(probs_low, grads).astype(LOW)
    grad_projected = jnp.concatenate([grad_query, grad_key, grad_value], axis=1)
    right_ref[:, : 3 * D] = grad_projected
    right_ref[:, 3 * D : 4 * D] = attn
    for number, part in enumerate(hidden):
        right_ref[:, (4 + number) * D : (5 + number) * D] = part
    right_ref[:, 4 * D + wide :] = branch
    sums_ref[...] = jnp.concatenate(sums + [jnp.zeros((4, D), F32)], axis=0)
    grad = grad_first + back_cols(grad_projected, attend_ref[...])
    grad_ref[...] = grad

    wait_all(inner_waits)
    inner_merge_ref, inner_expand_ref, inner_reduce_ref = inner_refs
    gain, final_gain = inner_vectors_ref[1:2, :], inner_vectors_ref[4:5, :]
    first_unit, first_spread = centre_rows(heads_ref[:, D : 2 * D])
    unit, spread = centre_rows(heads_ref[:, 2 * D : 3 * D])
    sums = [column_sums(grad * unit), column_sums(grad)]
    branch, hidden, grad_normed = feed_rows_back(
        grad,
        unit,
        spread,
        lambda span: wide_heads_ref[:, span],
        inner_reduce_ref,
        inner_expand_ref,
        final_gain,
    )
    branch_ref[...] = branch
    sums.append(column_sums(branch.astype(F32)))
    for number, part in enumerate(hidden):
        span = slice(number * D, (number + 1) * D)
        hidden_ref[:, span] = part
        hidden_sums_ref[:, span] = column_sums(part.astype(F32))
    sums += [column_sums(grad_normed * first_unit), column_sums(grad_normed)]
    grad_first = norm_back(grad_normed * gain, first_unit, first_spread)
    first_ref[...] = grad_first
    attn = grad_first.astype(LOW)
    attn_ref[...] = attn
    sums.append(column_sums(attn.astype(F32)))
    context_ref[...] = back_cols(attn, inner_merge_ref[...]).astype(LOW).astype(F32)
    inner_sums_ref[...] = jnp.concatenate(sums + [jnp.zeros((2, D), F32)], axis=0)


def mid_moves_of(pieces):
    if len(pieces) == 1:
        return [(0, 0, pieces[0].shape[0], 0, 0, None, 0)]
    quarter = pieces[0].shape[0]
    half = quarter // 2
    moves = [(0, 0, quarter, 0, quarter, None, 0)]
    for side in range(2):
        moves += [
            (1 + 4 * side, 0, half, 1, quarter, side, 0),
            (2 + 4 * side, 0, half, 2, quarter, side, 0),
            (3 + 4 * side, 0, half // 2, 3, quarter, side, 0),
            (4 + 4 * side, 0, half // 2, 3, quarter, side, half // 2),
        ]
    return moves


def late_moves_of(piece, linked):
    if not linked:
        return [(0, 0, piece.shape[0], 0, 0, None, 0)]
    rows = piece.shape[0] // 32
    return [
        (0, (4 * slot + turn) * rows, rows, turn, 8 * rows, None, slot * rows)
        for slot in range(8)
        for turn in range(4)
    ]


def heads_step(counts, heads, wide_heads, table, cotangent, small, mid, late, inner, linked):
    attend_bias, expand_bias, vectors, inner_vectors = small
    wide = expand_bias.shape[1]
    mid_moves, end_moves = mid_moves_of(mid), late_moves_of(late, linked)
    plane, depth, core = place_here()
    place = jnp.stack([plane, depth, core]).astype(jnp.int32)
    vmem = pl.BlockSpec(memory_space=pltpu.VMEM)
    smem = pl.BlockSpec(memory_space=pltpu.SMEM)
    outs = [
        ((SEGS, D), F32),
        ((SEGS, D), F32),
        ((SEGS, 3 * D + wide), LOW),
        ((SEGS, 5 * D + wide), LOW),
        ((8, D), F32),
        ((SEGS, D), LOW),
        ((SEGS, wide), LOW),
        ((SEGS, D), LOW),
        ((SEGS, D), F32),
        ((SEGS, D), F32),
        ((8, D), F32),
        ((1, wide), F32),
    ]
    flops = 6 * SEGS * D * (5 * D + 4 * wide)
    moved = 2 * D * (6 * D + 4 * wide)
    return pl.pallas_call(
        partial(heads_kernel, (len(mid), 1), mid_moves, end_moves),
        out_shape=[jax.ShapeDtypeStruct(shape, kind) for shape, kind in outs],
        in_specs=[smem, smem] + [vmem] * 8 + [pl.BlockSpec(memory_space=pl.ANY)] * (len(mid) + 4),
        out_specs=[vmem] * len(outs),
        scratch_shapes=[
            pltpu.VMEM((D, 3 * D), LOW),
            pltpu.VMEM((D, D), LOW),
            pltpu.VMEM((D, wide), LOW),
            pltpu.VMEM((wide, D), LOW),
            pltpu.VMEM((D, D), LOW),
            pltpu.VMEM((D, wide), LOW),
            pltpu.VMEM((wide, D), LOW),
            pltpu.SemaphoreType.DMA((3 * len(mid_moves) + len(end_moves) + 3,)),
        ],
        compiler_params=pltpu.CompilerParams(vmem_limit_bytes=60 << 20),
        cost_estimate=pl.CostEstimate(flops=flops, bytes_accessed=moved, transcendentals=0),
        name="heads",
    )(
        place,
        counts,
        heads,
        wide_heads,
        table,
        cotangent,
        attend_bias,
        expand_bias,
        vectors,
        inner_vectors,
        *mid,
        late,
        *inner,
    )


UNIT = 384


def grads_kernel(jobs, adds, side_ref, *refs):
    refs, came_ref, out_ref = refs[: -1 - adds], refs[-2], refs[-1]
    unit = pl.program_id(0)

    def put(chips, units, shape, total):
        total = total.reshape(shape)
        if adds:
            total = total + came_ref[chips, units].astype(F32)
        out_ref[chips, units] = total.astype(LOW)

    for folded, first, count, number in jobs:
        (left_ref, right_ref), heads, refs = refs[:2], refs[2:number], refs[number:]

        @pl.when((unit >= first) & (unit < first + count))
        def _(folded=folded, first=first, left_ref=left_ref, right_ref=right_ref, heads=heads):
            total = cross_rows(left_ref[...], right_ref[...])
            if heads:
                total = total + cross_rows(heads[0][...].astype(LOW), heads[1][...])
            if folded:
                chips = pl.ds(4 * (unit - first), 4)
                put(chips, slice(first, first + 4), (4, 4, 48, UNIT), total)
            else:
                put(slice(None), pl.ds(unit, 1), (16, 1, 48, UNIT), total)


def half_grads(jobs, side, came=None):
    rules, operands, specs, first = [], [], [], 0
    for left, right, head_left, column, head_right in jobs:
        folded = left.shape[1] > D
        count = left.shape[1] // D if folded else right.shape[1] // (2 * UNIT)
        start = first

        def place(unit, start=start, count=count):
            return lax.min(lax.max(unit - start, 0), count - 1)

        def left_index(unit, side, place=place, folded=folded):
            return (0, place(unit) if folded else 0)

        def right_index(unit, side, place=place, folded=folded, count=count):
            return (0, side[0] if folded else side[0] * count + place(unit))

        def head_index(unit, side, place=place, folded=folded, column=column):
            return (0, column + (place(unit) if folded else 0))

        operands += [left, right]
        specs += [
            pl.BlockSpec((left.shape[0], D), left_index),
            pl.BlockSpec((right.shape[0], UNIT), right_index),
        ]
        if head_left is not None:
            operands += [head_left, head_right]
            specs += [
                pl.BlockSpec((SEGS, D), head_index),
                pl.BlockSpec((SEGS, UNIT), right_index),
            ]
        rules.append((folded, first, count, 2 if head_left is None else 4))
        first += count
    shape = (16, first, 48, UNIT)
    whole = pl.BlockSpec(shape, lambda unit, side: (0, 0, 0, 0))
    if came is not None:
        operands.append(came)
        specs.append(whole)
    size = operands[0].shape[0]
    return pl.pallas_call(
        partial(grads_kernel, rules, int(came is not None)),
        grid_spec=pltpu.PrefetchScalarGridSpec(
            num_scalar_prefetch=1, grid=(first,), in_specs=specs, out_specs=whole
        ),
        out_shape=jax.ShapeDtypeStruct(shape, LOW),
        compiler_params=pltpu.CompilerParams(vmem_limit_bytes=60 << 20),
        cost_estimate=pl.CostEstimate(
            flops=2 * first * size * D * UNIT, bytes_accessed=30 << 20, transcendentals=0
        ),
        name="half_grads",
    )(side.astype(jnp.int32)[None], *operands)


def scatter_planes(kept):
    plane = place_here()[0]
    kept = kept.reshape(4, 4, *kept.shape[1:])
    return [
        lax.dynamic_index_in_dim(kept, plane ^ turn, axis=0, keepdims=False)
        for turn in range(4)
    ]


def scatter_across(planes, gate):
    here, next_x, next_y, across = planes
    from_y, from_x = over_y(across[:2]), over_x(across[2:])
    next_x, next_y = after(gate, next_x, next_y)
    next_x = jnp.concatenate([next_x[:2] + from_y, next_x[2:]], axis=0)
    next_y = jnp.concatenate([next_y[:2], next_y[2:] + from_x], axis=0)
    return here, next_x, next_y


def scatter_next(here, next_x, next_y, gate):
    came_x, came_y = after(gate, over_x(next_x), over_y(next_y))
    return (
        here.astype(jnp.float32) + came_x.astype(jnp.float32) + came_y.astype(jnp.float32)
    ).astype(jnp.bfloat16)


def scatter_line(here):
    depth = place_here()[1]
    slabs = [
        lax.dynamic_index_in_dim(here, (depth + step) & 3, axis=0, keepdims=False)
        for step in range(4)
    ]
    total = slabs[0].astype(jnp.float32)
    for step in (1, 2, 3):
        total = total + over_z(slabs[step], step).astype(jnp.float32)
    return total


def scatter_along(here):
    chips = here.shape[0]
    groups = [[2 * chip + core for chip in range(chips)] for core in range(2)]
    total = lax.psum_scatter(
        here.reshape(-1, here.shape[-1]),
        "fsdp",
        scatter_dimension=0,
        axis_index_groups=groups,
        tiled=True,
    )
    return total.reshape(here.shape[1:]).astype(jnp.float32)


def scatter_end(total, shapes):
    core = place_here()[2]
    mine, sent, start = [], [], 0
    for height, width in shapes:
        groups = height // 768
        count = groups if groups > 1 else width // (2 * UNIT)
        rows = jnp.concatenate(
            [total[unit] for unit in range(start, start + count)], axis=0 if groups > 1 else 1
        )
        start += count
        mine.append(fold_rows(lax.dynamic_slice_in_dim(rows, core * 24 * groups, 24 * groups), 24))
        sent.append(
            fold_rows(lax.dynamic_slice_in_dim(rows, (1 - core) * 24 * groups, 24 * groups), 24)
        )
    other = over_core(jnp.concatenate(sent, axis=1))
    owned, start = [], 0
    for (height, width), part in zip(shapes, mine):
        width = width // 2
        pair = [unfold_cols(side, width) for side in (part, other[:, start : start + part.shape[1]])]
        owned.append(both_cores(pair[0], pair[1], core, 1))
        start += part.shape[1]
    return owned


def unfold(packed, parts, ratio):
    width = packed.shape[1] // ratio
    return jnp.stack(
        [
            packed[:, width * group : width * (group + 1)].reshape(-1, parts, width)
            for group in range(ratio)
        ],
        axis=1,
    ).reshape(-1, width)


def gather_flat(shards):
    parts = min(shard.shape[0] for shard in shards)
    pieces = split_cols(
        gather(jnp.concatenate([fold_rows(shard, parts) for shard in shards], axis=1)),
        [shard.size // parts for shard in shards],
    )
    return [
        unfold(piece, parts, shard.shape[0] // parts) if shard.shape[0] > parts else piece
        for piece, shard in zip(pieces, shards)
    ]


def scatter_flat(grads):
    devices = lax.axis_size(AXES)
    parts = min(grad.shape[0] for grad in grads) // devices
    packed = jnp.concatenate(
        [
            jnp.transpose(grad.reshape(devices, -1, parts, grad.shape[1]), (0, 2, 1, 3)).reshape(
                devices * parts, -1
            )
            for grad in grads
        ],
        axis=1,
    )
    owned = split_cols(
        scatter(packed).astype(jnp.float32), [grad.size // (devices * parts) for grad in grads]
    )
    return [unfold_cols(piece, grad.shape[1]) for piece, grad in zip(owned, grads)]


def on_device(
    tokens,
    counts,
    inner_attend,
    inner_attend_bias,
    inner_merge,
    inner_merge_bias,
    inner_gain,
    inner_shift,
    inner_expand,
    inner_expand_bias,
    inner_reduce,
    inner_reduce_bias,
    inner_final_gain,
    inner_final_shift,
    outer_attend,
    outer_attend_bias,
    outer_merge,
    outer_merge_bias,
    outer_gain,
    outer_shift,
    outer_expand,
    outer_expand_bias,
    outer_reduce,
    outer_reduce_bias,
    outer_final_gain,
    outer_final_shift,
    segment_place,
    cotangent,
):
    parts = inner_merge.shape[0]
    devices = D // parts
    ratio = inner_reduce.shape[0] // parts
    here = lax.axis_index(AXES)
    linked = lax.axis_size("dp") == 4 and lax.axis_size("fsdp") == 8
    wide = inner_expand.shape[1]
    inner_rest = [inner_merge, inner_expand, inner_reduce]
    outer_all = [outer_attend, outer_merge, outer_expand, outer_reduce]
    docs = counts.shape[0]
    head_cotangent = cotangent.reshape(docs * SEGS, SEG, D)[:, 0, :]
    small_parts = (
        inner_attend_bias,
        inner_merge_bias,
        inner_gain,
        inner_shift,
        inner_expand_bias,
        inner_reduce_bias,
        inner_final_gain,
        inner_final_shift,
        outer_attend_bias,
        outer_merge_bias,
        outer_gain,
        outer_shift,
        outer_expand_bias,
        outer_reduce_bias,
        outer_final_gain,
        outer_final_shift,
    )
    sizes = [part.shape[0] for part in small_parts] + [parts]
    small = pack_small(small_parts, segment_place)
    if linked:
        slab, line = attend_line(inner_attend, small)
        late_first = late_hops(after(slab, outer_reduce))
        line = after(late_first[1:], line)
        pieces = attend_pieces(line)
        late = late_pieces(late_first, (pieces[3], pieces[4]))
        mid_line = along_z(after(line, *inner_rest[:2]))
        end_line = along_z([after(line, inner_rest[2])])
        outer_line = along_z(after(line, *outer_all[:3]))
        small_pieces = pieces[:5]
    else:
        pieces = gather_flat([inner_attend])
        small_pieces = [gather(small)]
    (
        expand_bias,
        vectors,
        outer_attend_bias_full,
        outer_expand_bias_full,
        outer_vectors,
        place_rows,
    ) = unpack_small(sizes, devices, small_pieces)
    if linked:
        mid_half = half_rows(after((pieces[3], pieces[4]), mid_line))
        attend_tokens = after(mid_half, tokens)
    else:
        attend_tokens = tokens
    projected, context, probs, attend = inner_attention(
        attend_tokens, counts, pieces, small_pieces, sizes[0]
    )
    if linked:
        mid = first_hops(mid_line, mid_half)
        end = first_hops(end_line, half_rows(after((context, mid[1], mid[2]), end_line)))
        mid = last_hops(mid, context)
        end = last_hops(end, (mid[3], mid[4], vectors))
        outer = first_hops(
            outer_line, half_rows(after((mid[3], mid[4], end[1], end[2]), outer_line))
        )
    else:
        rest = gather_flat(inner_rest)
        mid, end = [jnp.concatenate(rest[:2], axis=1)], rest[2:]
    mixed, heads, wide_heads, saved, inner_full = inner_feed(
        tokens, counts, projected, context, mid, end, expand_bias, vectors
    )
    inner_weights = (*inner_full, vectors)
    branch, grad_hidden, grad_attn, grad_context, grad_first, inner_sums, hidden_sums = (
        inner_feed_back(cotangent, counts, saved, inner_weights)
    )
    if linked:
        outer = last_hops(outer, heads, inner_sums)
    else:
        outer_full = gather_flat(outer_all)
        outer, late = [jnp.concatenate(outer_full[:3], axis=1)], outer_full[3:]
    first, normed, active, slope, second = saved
    low = jnp.bfloat16
    (
        head_out,
        grad_heads,
        left_pack,
        right_pack,
        outer_sums,
        head_branch,
        head_hidden,
        head_attn,
        head_context,
        head_first,
        head_sums,
        head_hidden_sums,
    ) = heads_step(
        counts,
        heads,
        wide_heads,
        place_rows,
        head_cotangent,
        (outer_attend_bias_full, outer_expand_bias_full, outer_vectors, vectors),
        outer,
        late[0],
        inner_full,
        linked,
    )
    grad_place = jnp.transpose(jnp.sum(grad_heads.reshape(docs, SEGS, D), axis=0))
    inner_sums = inner_sums + head_sums
    hidden_sums = hidden_sums + head_hidden_sums
    operands = (projected, probs, grad_context, grad_first, mixed)
    head_rows = (head_context, head_first, head_out)
    steps = tokens.shape[0] // ROWS
    right_all = gather(right_pack)

    def left_factors(left_pack):
        rows = jnp.concatenate(
            [
                factor.reshape(factor.shape[0], devices, -1)
                for factor in split_cols(left_pack, (D, D, D, wide))
            ],
            axis=2,
        )
        return jnp.transpose(rows, (1, 0, 2))

    def exchange(rows):
        return lax.all_to_all(rows, AXES, split_axis=0, concat_axis=0, tiled=True)

    def outer_grads(left_all, right_all):
        left_all = left_all.reshape(-1, left_all.shape[-1])
        left_pieces = split_cols(left_all, (parts, parts, parts, parts * ratio))
        right_pieces = split_cols(right_all, (3 * D, D, wide, D))
        big = [cross_rows(left, right) for left, right in zip(left_pieces, right_pieces)]
        bias = [
            lax.dynamic_slice_in_dim(
                jnp.sum(right.astype(jnp.float32), axis=0), here * width, width, axis=0
            )
            for right, width in zip(right_pieces, (3 * parts, parts, wide // devices, parts))
        ]
        return big, bias

    if linked:
        core = place_here()[2]
        jobs = [
            (normed, grad_hidden, heads, 3, head_hidden),
            (active, branch, wide_heads, wide // D, head_branch),
        ]
        sent = half_grads(jobs, 1 - core)
        left_all = exchange(left_factors(after(sent, left_pack)))
        part = inner_attend_back(
            after(sent, *operands), attend, head_rows, 0, 1, ()
        )
        kept = half_grads(jobs, after((part[3], left_all), core), over_core(sent))
        planes = scatter_planes(kept)
        middle = inner_attend_back(
            after(planes, *operands), attend, head_rows, 1, steps - 2, part[:3]
        )
        tall = scatter_across(planes, middle[3])
        rest = inner_attend_back(
            after(tall, *operands), attend, head_rows, steps - 1, 1, middle[:3]
        )
        grad_projected, tokens_grad, mixed = rest[:3]
        attend_sums = part[3] + middle[3] + rest[3]
        outer_big, outer_bias = outer_grads(*after(rest[3], left_all, right_all))
        jobs = [
            (tokens, grad_projected, None, 0, None),
            (context, grad_attn, heads, 4, head_attn),
        ]
        tall = scatter_next(*tall, (outer_big, outer_bias))
        sent = half_grads(jobs, after(tall, 1 - core))
        tall = scatter_along(tall)
        kept = half_grads(jobs, core, over_core(sent))
        short = scatter_next(*scatter_across(scatter_planes(kept), ()), ())
        sums_gate = short
        short = scatter_line(after(tall, short))
        own_expand, own_reduce = scatter_end(tall, [(D, wide), (wide, D)])
        own_attend, own_merge = scatter_end(short, [(D, 3 * D), (D, D)])
    else:
        sums_gate = ()
        left_all = exchange(left_factors(left_pack))
        outer_big, outer_bias = outer_grads(left_all, right_all)
        grad_projected, tokens_grad, mixed, attend_sums = inner_attend_back(
            operands, attend, head_rows, 0, steps, ()
        )
        grad_attend = cross_rows(tokens, grad_projected).astype(low)
        grad_reduce, grad_expand, grad_merge = [
            (cross_rows(left, right) + cross_rows(head_left.astype(low), head_right)).astype(low)
            for left, right, head_left, head_right in (
                (active, branch, wide_heads[:, wide:], head_branch),
                (normed, grad_hidden, heads[:, 3 * D : 4 * D], head_hidden),
                (context, grad_attn, heads[:, 4 * D :], head_attn),
            )
        ]
        own_expand, own_reduce = scatter_flat([grad_expand, grad_reduce])
        own_attend, own_merge = scatter_flat([grad_attend, grad_merge])
    row_sums = (
        attend_sums,
        inner_sums[5],
        inner_sums[3],
        inner_sums[4],
        hidden_sums,
        inner_sums[2],
        inner_sums[0],
        inner_sums[1],
        outer_sums[2],
        outer_sums[3],
        outer_sums[0],
        outer_sums[1],
        grad_place,
    )
    sums = sum_rows(jnp.concatenate([entry.reshape(devices, -1) for entry in row_sums], axis=1), sums_gate)
    sums = split_cols(sums, [entry.size // devices for entry in row_sums])
    return (
        mixed,
        tokens_grad,
        own_attend,
        sums[0],
        own_merge,
        sums[1],
        sums[2],
        sums[3],
        own_expand,
        sums[4],
        own_reduce,
        sums[5],
        sums[6],
        sums[7],
        outer_big[0],
        outer_bias[0],
        outer_big[1],
        outer_bias[1],
        sums[8],
        sums[9],
        outer_big[2],
        outer_bias[2],
        outer_big[3],
        outer_bias[3],
        sums[10],
        sums[11],
        sums[12].reshape(parts, SEGS),
    )


def solution(mesh):
    return jax.shard_map(
        on_device,
        mesh=mesh,
        in_specs=(
            P(("dp", "fsdp"), None),
            P(("dp", "fsdp")),
            P(("dp", "fsdp"), None),
            P(("dp", "fsdp")),
            P(("dp", "fsdp"), None),
            P(("dp", "fsdp")),
            P(("dp", "fsdp")),
            P(("dp", "fsdp")),
            P(("dp", "fsdp"), None),
            P(("dp", "fsdp")),
            P(("dp", "fsdp"), None),
            P(("dp", "fsdp")),
            P(("dp", "fsdp")),
            P(("dp", "fsdp")),
            P(("dp", "fsdp"), None),
            P(("dp", "fsdp")),
            P(("dp", "fsdp"), None),
            P(("dp", "fsdp")),
            P(("dp", "fsdp")),
            P(("dp", "fsdp")),
            P(("dp", "fsdp"), None),
            P(("dp", "fsdp")),
            P(("dp", "fsdp"), None),
            P(("dp", "fsdp")),
            P(("dp", "fsdp")),
            P(("dp", "fsdp")),
            P(("dp", "fsdp"), None),
            P(("dp", "fsdp"), None),
        ),
        out_specs=(
            P(("dp", "fsdp"), None),
            P(("dp", "fsdp"), None),
            P(("dp", "fsdp"), None),
            P(("dp", "fsdp")),
            P(("dp", "fsdp"), None),
            P(("dp", "fsdp")),
            P(("dp", "fsdp")),
            P(("dp", "fsdp")),
            P(("dp", "fsdp"), None),
            P(("dp", "fsdp")),
            P(("dp", "fsdp"), None),
            P(("dp", "fsdp")),
            P(("dp", "fsdp")),
            P(("dp", "fsdp")),
            P(("dp", "fsdp"), None),
            P(("dp", "fsdp")),
            P(("dp", "fsdp"), None),
            P(("dp", "fsdp")),
            P(("dp", "fsdp")),
            P(("dp", "fsdp")),
            P(("dp", "fsdp"), None),
            P(("dp", "fsdp")),
            P(("dp", "fsdp"), None),
            P(("dp", "fsdp")),
            P(("dp", "fsdp")),
            P(("dp", "fsdp")),
            P(("dp", "fsdp"), None),
        ),
        check_vma=False,
    )
```

```python
from functools import partial

import jax
import jax.numpy as jnp
from jax import lax
from jax.experimental import pallas as pl
from jax.experimental.pallas import tpu as pltpu
from jax.sharding import PartitionSpec as P

D = 768
HEADS = 12
HD = 64
SEG = 128
SLOTS = 1024
SEGS = 8


def cross_rows(left_rows, right_rows):
    return lax.dot_general(
        left_rows, right_rows, (((0,), (0,)), ((), ())), preferred_element_type=jnp.float32
    )


def back_cols(left_rows, right_rows):
    return lax.dot_general(
        left_rows, right_rows, (((1,), (1,)), ((), ())), preferred_element_type=jnp.float32
    )


ROWS = 256
PAIR = 2 * HD
PAIRS = HEADS // 2
F32 = jnp.float32
LOW = jnp.bfloat16


def dot_nn(left, right):
    return jnp.dot(left, right, preferred_element_type=F32)


def centre_rows(rows):
    centred = rows - jnp.mean(rows, axis=-1, keepdims=True)
    spread = lax.rsqrt(jnp.mean(centred * centred, axis=-1, keepdims=True) + 1e-05)
    return centred * spread, spread


def norm_back(grad, unit, spread):
    return spread * (
        grad
        - jnp.mean(grad, axis=-1, keepdims=True)
        - unit * jnp.mean(grad * unit, axis=-1, keepdims=True)
    )


def gelu_pair(hidden):
    size = jnp.abs(hidden)
    bell = jnp.exp(hidden * hidden * -0.5)
    t = 1.0 / (1.0 + (0.3275911 * 0.7071067811865476) * size)
    poly = t * (
        0.127414796
        + t * (-0.142248368 + t * (0.7107068705 + t * (-0.7265760135 + t * 0.5307027145)))
    )
    tail = poly * bell
    phi = jnp.where(hidden >= 0, 1.0 - tail, tail)
    return hidden * phi, phi + hidden * bell * 0.3989422804014327


def two_heads(pair, axis):
    first = lax.broadcasted_iota(jnp.int32, pair.shape, 1) < HD
    zero = jnp.zeros_like(pair)
    return jnp.concatenate([jnp.where(first, pair, zero), jnp.where(first, zero, pair)], axis=axis)


def pair_probs(query, key, valid):
    scores = back_cols(two_heads(query, 0), key) * HD ** (-0.5)
    scores = jnp.where(valid, scores, -1e30)
    weight = jnp.exp(scores - jnp.max(scores, axis=-1, keepdims=True))
    return weight / jnp.sum(weight, axis=-1, keepdims=True)


def side_by_side(stacked):
    half = stacked.shape[0] // 2
    return jnp.concatenate([stacked[:half], stacked[half:]], axis=1)


def valid_keys(count_ref, segment):
    position = lax.broadcasted_iota(jnp.int32, (1, SEG), 1)
    return position < count_ref[0] - segment * SEG


def attend_copies(pieces, target, place_ref, sems):
    if len(pieces) == 1:
        return [pltpu.make_async_copy(pieces[0], target, sems.at[0])]
    plane, depth, core = place_ref[0], place_ref[1], place_ref[2]
    height, width = pieces[0].shape[1], target.shape[1] // 2
    slots = ((0, 0, 4), (1, 0, 4), (2, 0, 4), (3, 0, 2), (3, 2, 2))
    copies = []
    for side in range(2):
        lane = pl.multiple_of((core if side == 0 else 1 - core) * width, 128)
        for number, (turn, first, count) in enumerate(slots):
            for slot in range(count):
                chip = (plane ^ turn) * 4 + ((depth + 4 - first - slot) & 3)
                row = pl.multiple_of(chip * height, 48)
                copies.append(
                    pltpu.make_async_copy(
                        pieces[5 * side + number].at[slot, :, :width],
                        target.at[pl.ds(row, height), pl.ds(lane, width)],
                        sems.at[len(copies)],
                    )
                )
    return copies


def attend_kernel(count, small_count, size, count_ref, rows_ref, place_ref, *refs):
    pieces, small, refs = refs[:count], refs[count : count + small_count], refs[count + small_count :]
    projected_ref, context_ref, probs_ref, joined_ref = refs[:4]
    attend_ref, bias_ref, got_ref, sems, small_sems, out_sem = refs[4:]
    step = pl.program_id(0)
    kept = pltpu.make_async_copy(attend_ref, joined_ref, out_sem)

    @pl.when(step == 0)
    def _():
        small_waits = small_copies(small, got_ref, place_ref, small_sems)
        copies = attend_copies(pieces, attend_ref, place_ref, sems)
        for copy in small_waits + copies:
            copy.start()
        wait_all(small_waits)
        first_rows = got_ref[...].astype(F32).reshape(-1, 16 + SEGS, 128)[:, 0, :]
        bias_ref[...] = spread_row(first_rows.astype(LOW), size, bias_ref.shape[1])
        wait_all(copies)
        kept.start()

    projected_ref[...] = (dot_nn(rows_ref[...], attend_ref[...]) + bias_ref[...]).astype(LOW)
    for local in range(ROWS // SEG):
        valid = valid_keys(count_ref, step * (ROWS // SEG) + local)
        span = slice(local * SEG, (local + 1) * SEG)
        for pair in range(PAIRS):
            query, key, value = [
                projected_ref[span, part * D + pair * PAIR : part * D + (pair + 1) * PAIR]
                for part in range(3)
            ]
            probs = side_by_side(pair_probs(query, key, valid).astype(LOW))
            probs_ref[span, pair * 2 * SEG : (pair + 1) * 2 * SEG] = probs
            context_ref[span, pair * PAIR : (pair + 1) * PAIR] = dot_nn(
                probs, two_heads(value, 0)
            ).astype(LOW)

    @pl.when(step == pl.num_programs(0) - 1)
    def _():
        kept.wait()


def put_row(ref, place, start, row):
    span = slice(start, start + row.shape[1])
    here = lax.broadcasted_iota(jnp.int32, (ref.shape[0], 1), 0) == place
    ref[:, span] = jnp.where(here, row, ref[:, span])


def get_row(ref, place, span):
    here = lax.broadcasted_iota(jnp.int32, (ref.shape[0], 1), 0) == place
    return jnp.sum(jnp.where(here, ref[:, span], 0.0), axis=0, keepdims=True)


def first_row(rows, segment):
    return rows[segment * SEG : segment * SEG + 16, :].astype(F32)[:1]


def feed_kernel(
    mid_moves,
    end_moves,
    counts,
    count_ref,
    rows_ref,
    context_ref,
    place_ref,
    expand_bias_ref,
    vectors_ref,
    *refs,
):
    mid, end, refs = refs[: counts[0]], refs[counts[0] : sum(counts)], refs[sum(counts) :]
    joined, weights, sems, out_sems = refs[8:11], refs[11:14], refs[14], refs[15]
    merge_ref, expand_ref, reduce_ref = weights
    kept = [
        pltpu.make_async_copy(weight, out, out_sems.at[number])
        for number, (weight, out) in enumerate(zip(weights, joined))
    ]

    @pl.when(pl.program_id(0) == 0)
    def _():
        widths = (D, expand_ref.shape[1])
        waits = start_moves(mid, weights[:2], widths, mid_moves, place_ref, sems, 0)
        waits += start_moves(
            end, weights[2:], (D,), end_moves, place_ref, sems, 2 * len(mid_moves)
        )
        for copies, copy in zip(waits, kept):
            wait_all(copies)
            copy.start()

    feed_rows(count_ref, rows_ref, context_ref, *weights, expand_bias_ref, vectors_ref, *refs[:8])

    @pl.when(pl.program_id(0) == pl.num_programs(0) - 1)
    def _():
        wait_all(kept)


def feed_rows(
    count_ref,
    rows_ref,
    context_ref,
    merge_ref,
    expand_ref,
    reduce_ref,
    expand_bias_ref,
    vectors_ref,
    mixed_ref,
    heads_ref,
    wide_heads_ref,
    first_ref,
    normed_ref,
    active_ref,
    slope_ref,
    second_ref,
):
    step = pl.program_id(0)
    merge_bias, gain, shift, reduce_bias, final_gain, final_shift = [
        vectors_ref[row : row + 1, :] for row in range(6)
    ]
    first = rows_ref[...].astype(F32) + dot_nn(context_ref[...], merge_ref[...]) + merge_bias
    first_ref[...] = first
    normed = (centre_rows(first)[0] * gain + shift).astype(LOW)
    normed_ref[...] = normed
    second = normed.astype(F32) + reduce_bias
    chunk, wide = D, expand_ref.shape[1]
    segments = ROWS // SEG
    for start in range(0, wide, chunk):
        span = slice(start, start + chunk)
        active, slope = gelu_pair(dot_nn(normed, expand_ref[:, span]) + expand_bias_ref[:, span])
        active = active.astype(LOW)
        active_ref[:, span] = active
        slope_ref[:, span] = slope.astype(LOW)
        for local in range(segments):
            head = step * segments + local
            put_row(wide_heads_ref, head, start, slope[local * SEG : local * SEG + 1])
            put_row(wide_heads_ref, head, wide + start, first_row(active, local))
        second = second + dot_nn(active, reduce_ref[span, :])
    second_ref[...] = second
    result = centre_rows(second)[0] * final_gain + final_shift
    for local in range(segments):
        for number, rows in enumerate((result, first, second, normed, context_ref)):
            put_row(heads_ref, step * segments + local, number * D, first_row(rows, local))
    place = lax.broadcasted_iota(jnp.int32, (ROWS, 1), 0) + step * ROWS
    mixed_ref[...] = jnp.where(place < count_ref[0], result, 0.0).astype(LOW)


def feed_back_kernel(
    count_ref,
    cotangent_ref,
    second_ref,
    first_ref,
    slope_ref,
    merge_ref,
    expand_ref,
    reduce_ref,
    vectors_ref,
    branch_ref,
    hidden_ref,
    attn_ref,
    context_ref,
    first_grad_ref,
    sums_ref,
    hidden_sums_ref,
):
    step = pl.program_id(0)
    gain, final_gain = vectors_ref[1:2, :], vectors_ref[4:5, :]
    local = lax.broadcasted_iota(jnp.int32, (ROWS, 1), 0)
    plain = (local + step * ROWS < count_ref[0]) & (local % SEG != 0)
    grad = jnp.where(plain, cotangent_ref[...].astype(F32), 0.0)
    unit, spread = centre_rows(second_ref[...])
    sums = [grad * unit, grad]
    second = norm_back(grad * final_gain, unit, spread)
    branch = second.astype(LOW)
    branch_ref[...] = branch
    sums.append(branch.astype(F32))
    normed = second
    chunk = D

    @pl.when(step == 0)
    def _():
        sums_ref[...] = jnp.zeros_like(sums_ref)
        hidden_sums_ref[...] = jnp.zeros_like(hidden_sums_ref)

    for start in range(0, expand_ref.shape[1], chunk):
        span = slice(start, start + chunk)
        hidden = back_cols(branch, reduce_ref[span, :]) * slope_ref[:, span].astype(F32)
        hidden = hidden.astype(LOW)
        hidden_ref[:, span] = hidden
        hidden_sums_ref[:, span] += jnp.sum(hidden.astype(F32), axis=0, keepdims=True)
        normed = normed + back_cols(hidden, expand_ref[:, span])
    unit, spread = centre_rows(first_ref[...])
    sums += [normed * unit, normed]
    first = norm_back(normed * gain, unit, spread)
    first_grad_ref[...] = first
    attn = first.astype(LOW)
    attn_ref[...] = attn
    sums.append(attn.astype(F32))
    context_ref[...] = back_cols(attn, merge_ref[...]).astype(LOW)
    sums_ref[...] += jnp.concatenate(
        [jnp.sum(entry, axis=0, keepdims=True) for entry in sums]
        + [jnp.zeros((2, D), F32)],
        axis=0,
    )


def attend_back_kernel(
    offset,
    projected_ref,
    probs_ref,
    context_ref,
    first_ref,
    mixed_in_ref,
    attend_ref,
    head_context_ref,
    head_first_ref,
    head_out_ref,
    *refs,
):
    grad_ref, tokens_ref, mixed_ref, sums_ref = refs[-4:]
    step = pl.program_id(0)
    segments = ROWS // SEG

    @pl.when(step == 0)
    def _():
        sums_ref[...] = jnp.zeros_like(sums_ref)

    is_head = lax.broadcasted_iota(jnp.int32, (16, 1), 0) == 0
    scale = HD ** (-0.5)
    for local in range(segments):
        segment = (step + offset) * segments + local
        span = slice(local * SEG, (local + 1) * SEG)
        for pair in range(PAIRS):
            columns = [
                slice(part * D + pair * PAIR, part * D + (pair + 1) * PAIR) for part in range(3)
            ]
            query, key, value = [projected_ref[span, column] for column in columns]
            top = slice(local * SEG, local * SEG + 16)
            rest = slice(local * SEG + 16, (local + 1) * SEG)
            replaced = jnp.where(
                is_head,
                get_row(head_context_ref, segment, columns[0]),
                context_ref[top, columns[0]].astype(F32),
            ).astype(LOW)
            grad = jnp.concatenate([replaced, context_ref[rest, columns[0]]], axis=0)
            grad = two_heads(grad, 0)
            probs = probs_ref[span, pair * 2 * SEG : (pair + 1) * 2 * SEG]
            probs_low = jnp.concatenate([probs[:, :SEG], probs[:, SEG:]], axis=0)
            probs = probs_low.astype(F32)
            grad_probs = back_cols(grad, value)
            total = jnp.sum(grad_probs * probs, axis=-1, keepdims=True)
            scores = (probs * (grad_probs - total)).astype(LOW)
            grad_ref[span, columns[0]] = (
                dot_nn(side_by_side(scores), two_heads(key, 0)) * scale
            ).astype(LOW)
            grad_ref[span, columns[1]] = (
                cross_rows(scores, two_heads(query, 0)) * scale
            ).astype(LOW)
            grad_ref[span, columns[2]] = cross_rows(probs_low, grad).astype(LOW)
    tokens_ref[...] = first_ref[...] + back_cols(grad_ref[...], attend_ref[...])
    mixed_ref[...] = mixed_in_ref[...]
    for local in range(segments):
        segment = (step + offset) * segments + local
        top = slice(local * SEG, local * SEG + 16)
        missing = jnp.where(is_head, get_row(head_first_ref, segment, slice(0, D)), 0.0)
        tokens_ref[top, :] += missing
        mixed_ref[top, :] = jnp.where(
            is_head,
            get_row(head_out_ref, segment, slice(0, D)),
            mixed_in_ref[top, :].astype(F32),
        ).astype(LOW)
    sums_ref[...] += jnp.sum(grad_ref[...].astype(F32), axis=0, keepdims=True)


def by_rows(width, offset=0):
    return pl.BlockSpec((ROWS, width), lambda step: (step + offset, 0))


def entire(array):
    return pl.BlockSpec(array.shape, lambda step: (0,) * array.ndim)


def row_call(kernel, name, operands, specs, outs, flops, steps=None, earlier=(), scratch=()):
    rows = outs[0][0][0]
    shapes = [jax.ShapeDtypeStruct(shape, kind) for shape, kind, _ in outs]
    moved = sum(operand.size * operand.dtype.itemsize for operand in operands)
    moved += sum(shape.size * shape.dtype.itemsize for shape in shapes)
    return pl.pallas_call(
        kernel,
        grid=(rows // ROWS if steps is None else steps,),
        in_specs=[
            entire(operand) if spec is None else spec for operand, spec in zip(operands, specs)
        ]
        + [pl.BlockSpec(memory_space=pl.ANY)] * len(earlier),
        out_specs=[spec for _, _, spec in outs],
        out_shape=shapes,
        input_output_aliases={len(operands) + place: place for place in range(len(earlier))},
        scratch_shapes=scratch,
        compiler_params=pltpu.CompilerParams(vmem_limit_bytes=60 << 20),
        cost_estimate=pl.CostEstimate(flops=flops, bytes_accessed=moved, transcendentals=0),
        name=name,
    )(*operands, *earlier)


def whole_block(shape):
    return pl.BlockSpec(shape, lambda step: (0,) * len(shape))


def place_array():
    return jnp.stack(place_here()).astype(jnp.int32)


def inner_attention(rows, counts, pieces, small_pieces, bias_size):
    size = rows.shape[0]
    devices = D * 3 // bias_size
    smem, anywhere = pl.BlockSpec(memory_space=pltpu.SMEM), pl.BlockSpec(memory_space=pl.ANY)
    return row_call(
        partial(attend_kernel, len(pieces), len(small_pieces), bias_size),
        "attend",
        (counts, rows, place_array(), *pieces, *small_pieces),
        (smem, by_rows(D), smem) + (anywhere,) * (len(pieces) + len(small_pieces)),
        [
            ((size, 3 * D), LOW, by_rows(3 * D)),
            ((size, D), LOW, by_rows(D)),
            ((size, HEADS * SEG), LOW, by_rows(HEADS * SEG)),
            ((D, 3 * D), LOW, anywhere),
        ],
        2 * size * D * (3 * D + 4 * SEG),
        scratch=[
            pltpu.VMEM((D, 3 * D), LOW),
            pltpu.VMEM((1, 3 * D), F32),
            pltpu.VMEM((devices * (16 + SEGS), 128), LOW),
            pltpu.SemaphoreType.DMA((32,)),
            pltpu.SemaphoreType.DMA((16,)),
            pltpu.SemaphoreType.DMA,
        ],
    )


def inner_feed(rows, counts, projected, context, mid, end, expand_bias, vectors):
    size, wide = rows.shape[0], expand_bias.shape[1]
    mid_moves, end_moves = mid_moves_of(mid), mid_moves_of(end)
    smem, anywhere = pl.BlockSpec(memory_space=pltpu.SMEM), pl.BlockSpec(memory_space=pl.ANY)
    mixed, heads, wide_heads, *saved = row_call(
        partial(feed_kernel, mid_moves, end_moves, (len(mid), len(end))),
        "feed",
        (counts, rows, context, place_array(), expand_bias, vectors, *mid, *end),
        (smem, by_rows(D), by_rows(D), smem, None, None) + (anywhere,) * (len(mid) + len(end)),
        [
            ((size, D), LOW, by_rows(D)),
            ((size // SEG, 5 * D), F32, whole_block((size // SEG, 5 * D))),
            ((size // SEG, 2 * wide), F32, whole_block((size // SEG, 2 * wide))),
            ((size, D), F32, by_rows(D)),
            ((size, D), LOW, by_rows(D)),
            ((size, wide), LOW, by_rows(wide)),
            ((size, wide), LOW, by_rows(wide)),
            ((size, D), F32, by_rows(D)),
            ((D, D), LOW, anywhere),
            ((D, wide), LOW, anywhere),
            ((wide, D), LOW, anywhere),
        ],
        2 * size * D * (D + 2 * wide),
        scratch=[
            pltpu.VMEM((D, D), LOW),
            pltpu.VMEM((D, wide), LOW),
            pltpu.VMEM((wide, D), LOW),
            pltpu.SemaphoreType.DMA((2 * len(mid_moves) + len(end_moves),)),
            pltpu.SemaphoreType.DMA((3,)),
        ],
    )
    return mixed, heads, wide_heads, saved[:5], saved[5:]


def inner_feed_back(cotangent, counts, saved, weights):
    merge, expand, reduce_matrix, vectors = weights
    first, normed, active, slope, second = saved
    size, wide = cotangent.shape[0], expand.shape[1]
    return row_call(
        feed_back_kernel,
        "feed_back",
        (counts, cotangent, second, first, slope, merge, expand, reduce_matrix, vectors),
        (pl.BlockSpec(memory_space=pltpu.SMEM), by_rows(D), by_rows(D), by_rows(D), by_rows(wide))
        + (None,) * 4,
        [
            ((size, D), LOW, by_rows(D)),
            ((size, wide), LOW, by_rows(wide)),
            ((size, D), LOW, by_rows(D)),
            ((size, D), LOW, by_rows(D)),
            ((size, D), F32, by_rows(D)),
            ((8, D), F32, whole_block((8, D))),
            ((1, wide), F32, whole_block((1, wide))),
        ],
        2 * size * D * (D + 2 * wide),
    )


def inner_attend_back(operands, attend, head_rows, offset, steps, earlier):
    projected, probs, grad_context, grad_first, mixed = operands
    size = projected.shape[0]
    return row_call(
        partial(attend_back_kernel, offset),
        "attend_back",
        (projected, probs, grad_context, grad_first, mixed, attend, *head_rows),
        (by_rows(3 * D, offset), by_rows(HEADS * SEG, offset), by_rows(D, offset))
        + (by_rows(D, offset), by_rows(D, offset), None, None, None, None),
        [
            ((size, 3 * D), LOW, by_rows(3 * D, offset)),
            ((size, D), F32, by_rows(D, offset)),
            ((size, D), LOW, by_rows(D, offset)),
            ((1, 3 * D), F32, whole_block((1, 3 * D))),
        ],
        2 * steps * ROWS * D * (3 * D + 10 * SEG),
        steps,
        earlier,
    )


AXES = ("dp", "fsdp")


def gather(rows):
    return lax.all_gather(rows, AXES, axis=0, tiled=True)


def scatter(rows):
    return lax.psum_scatter(rows, AXES, scatter_dimension=0, tiled=True)


def split_cols(packed, widths):
    pieces, start = [], 0
    for width in widths:
        pieces.append(packed[..., start : start + width])
        start += width
    return pieces


def pack_kernel(*refs):
    vectors, place_ref, out_ref, rows_ref = refs[:16], refs[16], refs[17], refs[18]
    rows_ref[...] = jnp.zeros_like(rows_ref)
    for row, ref in enumerate(vectors):
        rows_ref[row : row + 1, : ref.shape[1]] = ref[...].astype(F32)
    place = jnp.transpose(place_ref[...].astype(F32))
    rows_ref[16 : 16 + SEGS, : place.shape[1]] = place
    out_ref[...] = rows_ref[...].astype(LOW)


def pack_small(vectors, segment_place):
    return pl.pallas_call(
        pack_kernel,
        out_shape=jax.ShapeDtypeStruct((16 + SEGS, 128), LOW),
        scratch_shapes=[pltpu.VMEM((16 + SEGS, 128), F32)],
        name="pack",
    )(*[vector[None] for vector in vectors], segment_place)


def spread_row(rows, size, width):
    devices = rows.shape[0]
    lane = lax.broadcasted_iota(jnp.int32, (128, width), 1)
    owner = lane // size
    pick = (lane - owner * size == lax.broadcasted_iota(jnp.int32, (128, width), 0)).astype(LOW)
    spread = dot_nn(rows, pick)
    row = lax.broadcasted_iota(jnp.int32, (devices, width), 0)
    owner = lax.broadcasted_iota(jnp.int32, (devices, width), 1) // size
    return jnp.sum(jnp.where(row == owner, spread, 0.0), axis=0, keepdims=True)


VECTOR_ROWS = (1, 2, 3, 5, 6, 7)


def small_copies(pieces, got_ref, place_ref, sems):
    if len(pieces) == 1:
        return [pltpu.make_async_copy(pieces[0], got_ref, sems.at[0])]
    plane, depth = place_ref[0], place_ref[1]
    copies = []
    slots = ((0, 0, 4), (1, 0, 4), (2, 0, 4), (3, 0, 2), (3, 2, 2))
    first_lane = pieces[0].shape[2] - 128
    for piece, (turn, first, count) in zip(pieces, slots):
        for slot in range(count):
            chip = (plane ^ turn) * 4 + ((depth + 4 - first - slot) & 3)
            copies.append(
                pltpu.make_async_copy(
                    piece.at[slot, :, first_lane : first_lane + 128],
                    got_ref.at[pl.ds(pl.multiple_of(48 * chip, 48), 48), :],
                    sems.at[len(copies)],
                )
            )
    return copies


def unpack_kernel(sizes, place_ref, *refs):
    outs, got_ref, sems = (None, *refs[-8:-2]), refs[-2], refs[-1]
    pieces = refs[:-8]
    copies = small_copies(pieces, got_ref, place_ref, sems)
    for copy in copies:
        copy.start()
    wait_all(copies)
    got = got_ref[...].astype(F32).reshape(-1, 16 + SEGS, 128)
    devices = got.shape[0]
    for block in range(2):
        attend_ref, expand_ref, vectors_ref = outs[3 * block : 3 * block + 3]
        for kind in range(1 - block, 8):
            row = 8 * block + kind
            size = sizes[row]
            spread = spread_row(got[:, row, :].astype(LOW), size, size * devices)
            if kind == 0:
                attend_ref[...] = spread
            elif kind == 4:
                expand_ref[...] = spread
            else:
                place = VECTOR_ROWS.index(kind)
                vectors_ref[place : place + 1, :] = spread
        vectors_ref[6:8, :] = jnp.zeros((2, vectors_ref.shape[1]), F32)
    for segment in range(SEGS):
        outs[6][segment : segment + 1, :] = spread_row(
            got[:, 16 + segment, :].astype(LOW), sizes[16], sizes[16] * devices
        )


def unpack_small(sizes, devices, pieces):
    shapes = []
    for block in range(2):
        for rows, size in ((1, sizes[8 * block]), (1, sizes[8 * block + 4]), (8, sizes[1])):
            shapes.append(jax.ShapeDtypeStruct((rows, size * devices), F32))
    shapes.append(jax.ShapeDtypeStruct((SEGS, sizes[16] * devices), F32))
    return pl.pallas_call(
        partial(unpack_kernel, sizes),
        out_shape=shapes[1:],
        in_specs=[pl.BlockSpec(memory_space=pltpu.SMEM)]
        + [pl.BlockSpec(memory_space=pl.ANY)] * len(pieces),
        scratch_shapes=[
            pltpu.VMEM((devices * (16 + SEGS), 128), LOW),
            pltpu.SemaphoreType.DMA((16,)),
        ],
        compiler_params=pltpu.CompilerParams(vmem_limit_bytes=60 << 20),
        name="unpack",
    )(place_array(), *pieces)


def sum_rows(rows, gate):
    devices, size = rows.shape
    padded = jnp.pad(rows, ((0, 0), (0, -size % 1024))).reshape(devices, -1, 128)
    got = lax.all_to_all(padded, AXES, split_axis=0, concat_axis=0, tiled=True)
    return jnp.sum(after(gate, got), axis=0).reshape(-1)[:size]


def hop(array, turn):
    return lax.ppermute(array, AXES, [(place, turn(place)) for place in range(32)])


def over_x(array):
    return hop(array, lambda place: place ^ 8)


def over_y(array):
    return hop(array, lambda place: place ^ 16)


def over_core(array):
    return hop(array, lambda place: place ^ 1)


def over_z(array, step):
    return hop(array, lambda place: (place & ~6) | ((((place >> 1) + step) & 3) << 1))


def place_here():
    chip = lax.axis_index("fsdp")
    return lax.axis_index("dp"), chip // 2, chip % 2


def half_cols(array, core):
    width = array.shape[-1] // 2
    return lax.dynamic_slice_in_dim(array, core * width, width, axis=array.ndim - 1)


def fold_rows(array, rows):
    return jnp.concatenate(jnp.split(array, array.shape[0] // rows, axis=0), axis=1)


def unfold_cols(array, width):
    return jnp.concatenate(jnp.split(array, array.shape[1] // width, axis=1), axis=0)


def both_cores(mine, other, core, axis):
    return jnp.concatenate(
        [jnp.where(core == 0, mine, other), jnp.where(core == 0, other, mine)], axis=axis
    )


def attend_line(shard, small):
    core = place_here()[2]
    mine = jnp.concatenate([half_cols(shard, core), small], axis=1)
    sent = jnp.concatenate([half_cols(shard, 1 - core), small], axis=1)
    slab = both_cores(mine, over_core(sent), core, 0)
    hops = [over_z(slab, step) for step in (1, 2, 3)]
    return slab, jnp.stack([slab] + hops)


def attend_pieces(line):
    line_x, line_y = over_x(line), over_y(line)
    pieces = [line, line_x, line_y, over_y(line_x[:2]), over_x(line_y[2:])]
    return pieces + [over_core(piece) for piece in pieces]


def held(array, first):
    return array + first.reshape(-1)[:1].reshape((1,) * array.ndim).astype(array.dtype) * 0


def after(first, *later):
    tied = lax.optimization_barrier((first, later))[1]
    return tied[0] if len(tied) == 1 else tied


def half_rows(line):
    half = line.shape[0] // 2
    return lax.dynamic_slice_in_dim(line, place_here()[2] * half, half, axis=0)


def first_hops(line, mine):
    return line, over_x(mine), over_y(mine)


def last_hops(hops, gate, late_gate=()):
    line, from_x, from_y = hops
    half = from_x.shape[0] // 2
    sent_y, sent_x = after(gate, from_x[:half], from_y[half:])
    pieces = [from_x, from_y, over_y(sent_y), over_x(sent_x)]
    return [line] + pieces + [over_core(piece) for piece in after(late_gate, *pieces)]


def late_hops(shard):
    return shard, over_x(shard), over_y(shard)


def late_pieces(hops, gate):
    shard, from_x, from_y = hops
    half = shard.shape[0] // 2
    sent_y, sent_x = after(gate, from_x[:half], from_y[half:])
    across = jnp.concatenate([over_y(sent_y), over_x(sent_x)], axis=0)
    rows = jnp.concatenate([shard, from_x, from_y, across], axis=0)
    return [lax.all_gather(rows, "fsdp", axis=0, tiled=True)]


def along_z(shards):
    return lax.all_gather(jnp.concatenate(shards, axis=1), "fsdp", axis=0, tiled=True)


def start_moves(pieces, outs, widths, moves, place_ref, sems, first):
    plane, core = place_ref[0], place_ref[2]
    groups, start = [], 0
    for out, width in zip(outs, widths):
        copies = []
        for piece, source, rows, turn, quarter, side, offset in moves:
            row = (plane ^ turn) * quarter + offset
            if side is not None:
                row = row + (core if side == 0 else 1 - core) * (quarter // 2)
            copies.append(
                pltpu.make_async_copy(
                    pieces[piece].at[source : source + rows, start : start + width],
                    out.at[pl.ds(pl.multiple_of(row, 48), rows), :],
                    sems.at[first],
                )
            )
            first += 1
        start += width
        groups.append(copies)
    for copies in groups:
        for copy in copies:
            copy.start()
    return groups


def wait_all(copies):
    for copy in copies:
        copy.wait()


def column_sums(rows):
    return jnp.sum(rows, axis=0, keepdims=True)


def feed_rows_back(grad, unit, spread, slope_of, reduce_ref, expand_ref, final_gain):
    second = norm_back(grad * final_gain, unit, spread)
    branch = second.astype(LOW)
    normed, hidden = second, []
    for start in range(0, expand_ref.shape[1], D):
        span = slice(start, start + D)
        part = (back_cols(branch, reduce_ref[span, :]) * slope_of(span)).astype(LOW)
        hidden.append(part)
        normed = normed + back_cols(part, expand_ref[:, span])
    return branch, hidden, normed


def heads_kernel(
    counts,
    mid_moves,
    end_moves,
    place_ref,
    count_ref,
    heads_ref,
    wide_heads_ref,
    table_ref,
    cotangent_ref,
    attend_bias_ref,
    expand_bias_ref,
    vectors_ref,
    inner_vectors_ref,
    *refs,
):
    mid_count, end_count = counts
    mid, refs = refs[:mid_count], refs[mid_count:]
    end, refs = refs[:end_count], refs[end_count:]
    inner_hbm, refs = refs[:3], refs[3:]
    out_ref, grad_ref, left_ref, right_ref, sums_ref = refs[:5]
    branch_ref, hidden_ref, attn_ref, context_ref, first_ref, inner_sums_ref, hidden_sums_ref = refs[5:12]
    attend_ref, merge_ref, expand_ref, reduce_ref = refs[12:16]
    inner_refs, sems = refs[16:19], refs[19]
    wide = expand_ref.shape[1]
    waits = start_moves(
        mid, (attend_ref, merge_ref, expand_ref), (3 * D, D, wide), mid_moves, place_ref, sems, 0
    )
    first_free = 3 * len(mid_moves)
    waits += start_moves(end, (reduce_ref,), (D,), end_moves, place_ref, sems, first_free)
    first_free += len(end_moves)
    inner_waits = [
        pltpu.make_async_copy(source, target, sems.at[first_free + number])
        for number, (source, target) in enumerate(zip(inner_hbm, inner_refs))
    ]
    for copy in inner_waits:
        copy.start()
    merge_bias, gain, shift, reduce_bias, final_gain, final_shift = [
        vectors_ref[row : row + 1, :] for row in range(6)
    ]
    scale = HD ** (-0.5)
    stacked = HEADS * SEGS
    own = (
        lax.broadcasted_iota(jnp.int32, (stacked, D), 1) // HD
        == lax.broadcasted_iota(jnp.int32, (stacked, D), 0) // SEGS
    )

    def by_head(rows):
        return jnp.where(own, jnp.concatenate([rows] * HEADS, axis=0), 0.0).astype(LOW)

    def join_heads(rows):
        rows = jnp.where(own, rows, 0.0)
        return sum(rows[SEGS * head : SEGS * (head + 1)] for head in range(HEADS))

    keep = (
        lax.broadcasted_iota(jnp.int32, (SEGS, 1), 0) * SEG < count_ref[0]
    ).astype(F32)
    source = (heads_ref[:, :D] + table_ref[...]).astype(LOW)
    wait_all(waits[0])
    projected = (dot_nn(source, attend_ref[...]) + attend_bias_ref[...]).astype(LOW)
    query, key, value = projected[:, :D], projected[:, D : 2 * D], projected[:, 2 * D :]
    queries = by_head(query.astype(F32))
    scores = back_cols(queries, key) * scale
    weight = jnp.exp(scores - jnp.max(scores, axis=-1, keepdims=True))
    probs = weight / jnp.sum(weight, axis=-1, keepdims=True)
    probs_low = probs.astype(LOW)
    context = join_heads(dot_nn(probs_low, value)).astype(LOW)
    wait_all(waits[1])
    first = source.astype(F32) + dot_nn(context, merge_ref[...]) + merge_bias
    first_unit, first_spread = centre_rows(first)
    normed = (first_unit * gain + shift).astype(LOW)
    left_ref[:, :D] = source
    left_ref[:, D : 2 * D] = context
    left_ref[:, 2 * D : 3 * D] = normed
    second = normed.astype(F32) + reduce_bias
    slopes = {}
    wait_all(waits[2])
    wait_all(waits[3])
    for start in range(0, wide, D):
        span = slice(start, start + D)
        active, slopes[start] = gelu_pair(
            dot_nn(normed, expand_ref[:, span]) + expand_bias_ref[:, span]
        )
        active = active.astype(LOW)
        left_ref[:, 3 * D + start : 4 * D + start] = active
        second = second + dot_nn(active, reduce_ref[span, :])
    unit, spread = centre_rows(second)
    out_ref[...] = (unit * final_gain + final_shift) * keep
    grad = cotangent_ref[...].astype(F32) * keep
    sums = [column_sums(grad * unit), column_sums(grad)]
    branch, hidden, grad_normed = feed_rows_back(
        grad, unit, spread, lambda span: slopes[span.start], reduce_ref, expand_ref, final_gain
    )
    sums += [column_sums(grad_normed * first_unit), column_sums(grad_normed)]
    grad_first = norm_back(grad_normed * gain, first_unit, first_spread)
    attn = grad_first.astype(LOW)
    grads = by_head(back_cols(attn, merge_ref[...]).astype(LOW).astype(F32))
    grad_probs = back_cols(grads, value)
    total = jnp.sum(grad_probs * probs, axis=-1, keepdims=True)
    grad_scores = (probs * (grad_probs - total)).astype(LOW)
    grad_query = (join_heads(dot_nn(grad_scores, key)) * scale).astype(LOW)
    grad_key = (cross_rows(grad_scores, queries) * scale).astype(LOW)
    grad_value = cross_rows(probs_low, grads).astype(LOW)
    grad_projected = jnp.concatenate([grad_query, grad_key, grad_value], axis=1)
    right_ref[:, : 3 * D] = grad_projected
    right_ref[:, 3 * D : 4 * D] = attn
    for number, part in enumerate(hidden):
        right_ref[:, (4 + number) * D : (5 + number) * D] = part
    right_ref[:, 4 * D + wide :] = branch
    sums_ref[...] = jnp.concatenate(sums + [jnp.zeros((4, D), F32)], axis=0)
    grad = grad_first + back_cols(grad_projected, attend_ref[...])
    grad_ref[...] = grad

    wait_all(inner_waits)
    inner_merge_ref, inner_expand_ref, inner_reduce_ref = inner_refs
    gain, final_gain = inner_vectors_ref[1:2, :], inner_vectors_ref[4:5, :]
    first_unit, first_spread = centre_rows(heads_ref[:, D : 2 * D])
    unit, spread = centre_rows(heads_ref[:, 2 * D : 3 * D])
    sums = [column_sums(grad * unit), column_sums(grad)]
    branch, hidden, grad_normed = feed_rows_back(
        grad,
        unit,
        spread,
        lambda span: wide_heads_ref[:, span],
        inner_reduce_ref,
        inner_expand_ref,
        final_gain,
    )
    branch_ref[...] = branch
    sums.append(column_sums(branch.astype(F32)))
    for number, part in enumerate(hidden):
        span = slice(number * D, (number + 1) * D)
        hidden_ref[:, span] = part
        hidden_sums_ref[:, span] = column_sums(part.astype(F32))
    sums += [column_sums(grad_normed * first_unit), column_sums(grad_normed)]
    grad_first = norm_back(grad_normed * gain, first_unit, first_spread)
    first_ref[...] = grad_first
    attn = grad_first.astype(LOW)
    attn_ref[...] = attn
    sums.append(column_sums(attn.astype(F32)))
    context_ref[...] = back_cols(attn, inner_merge_ref[...]).astype(LOW).astype(F32)
    inner_sums_ref[...] = jnp.concatenate(sums + [jnp.zeros((2, D), F32)], axis=0)


def mid_moves_of(pieces):
    if len(pieces) == 1:
        return [(0, 0, pieces[0].shape[0], 0, 0, None, 0)]
    quarter = pieces[0].shape[0]
    half = quarter // 2
    moves = [(0, 0, quarter, 0, quarter, None, 0)]
    for side in range(2):
        moves += [
            (1 + 4 * side, 0, half, 1, quarter, side, 0),
            (2 + 4 * side, 0, half, 2, quarter, side, 0),
            (3 + 4 * side, 0, half // 2, 3, quarter, side, 0),
            (4 + 4 * side, 0, half // 2, 3, quarter, side, half // 2),
        ]
    return moves


def late_moves_of(piece, linked):
    if not linked:
        return [(0, 0, piece.shape[0], 0, 0, None, 0)]
    rows = piece.shape[0] // 32
    return [
        (0, (4 * slot + turn) * rows, rows, turn, 8 * rows, None, slot * rows)
        for slot in range(8)
        for turn in range(4)
    ]


def heads_step(counts, heads, wide_heads, table, cotangent, small, mid, late, inner, linked):
    attend_bias, expand_bias, vectors, inner_vectors = small
    wide = expand_bias.shape[1]
    mid_moves, end_moves = mid_moves_of(mid), late_moves_of(late, linked)
    plane, depth, core = place_here()
    place = jnp.stack([plane, depth, core]).astype(jnp.int32)
    vmem = pl.BlockSpec(memory_space=pltpu.VMEM)
    smem = pl.BlockSpec(memory_space=pltpu.SMEM)
    outs = [
        ((SEGS, D), F32),
        ((SEGS, D), F32),
        ((SEGS, 3 * D + wide), LOW),
        ((SEGS, 5 * D + wide), LOW),
        ((8, D), F32),
        ((SEGS, D), LOW),
        ((SEGS, wide), LOW),
        ((SEGS, D), LOW),
        ((SEGS, D), F32),
        ((SEGS, D), F32),
        ((8, D), F32),
        ((1, wide), F32),
    ]
    flops = 6 * SEGS * D * (5 * D + 4 * wide)
    moved = 2 * D * (6 * D + 4 * wide)
    return pl.pallas_call(
        partial(heads_kernel, (len(mid), 1), mid_moves, end_moves),
        out_shape=[jax.ShapeDtypeStruct(shape, kind) for shape, kind in outs],
        in_specs=[smem, smem] + [vmem] * 8 + [pl.BlockSpec(memory_space=pl.ANY)] * (len(mid) + 4),
        out_specs=[vmem] * len(outs),
        scratch_shapes=[
            pltpu.VMEM((D, 3 * D), LOW),
            pltpu.VMEM((D, D), LOW),
            pltpu.VMEM((D, wide), LOW),
            pltpu.VMEM((wide, D), LOW),
            pltpu.VMEM((D, D), LOW),
            pltpu.VMEM((D, wide), LOW),
            pltpu.VMEM((wide, D), LOW),
            pltpu.SemaphoreType.DMA((3 * len(mid_moves) + len(end_moves) + 3,)),
        ],
        compiler_params=pltpu.CompilerParams(vmem_limit_bytes=60 << 20),
        cost_estimate=pl.CostEstimate(flops=flops, bytes_accessed=moved, transcendentals=0),
        name="heads",
    )(
        place,
        counts,
        heads,
        wide_heads,
        table,
        cotangent,
        attend_bias,
        expand_bias,
        vectors,
        inner_vectors,
        *mid,
        late,
        *inner,
    )


UNIT = 384


def grads_kernel(jobs, adds, side_ref, *refs):
    refs, came_ref, out_ref = refs[: -1 - adds], refs[-2], refs[-1]
    unit = pl.program_id(0)

    def put(chips, units, shape, total):
        total = total.reshape(shape)
        if adds:
            total = total + came_ref[chips, units].astype(F32)
        out_ref[chips, units] = total.astype(LOW)

    for folded, first, count, number in jobs:
        (left_ref, right_ref), heads, refs = refs[:2], refs[2:number], refs[number:]

        @pl.when((unit >= first) & (unit < first + count))
        def _(folded=folded, first=first, left_ref=left_ref, right_ref=right_ref, heads=heads):
            total = cross_rows(left_ref[...], right_ref[...])
            if heads:
                total = total + cross_rows(heads[0][...].astype(LOW), heads[1][...])
            if folded:
                chips = pl.ds(4 * (unit - first), 4)
                put(chips, slice(first, first + 4), (4, 4, 48, UNIT), total)
            else:
                put(slice(None), pl.ds(unit, 1), (16, 1, 48, UNIT), total)


def half_grads(jobs, side, came=None):
    rules, operands, specs, first = [], [], [], 0
    for left, right, head_left, column, head_right in jobs:
        folded = left.shape[1] > D
        count = left.shape[1] // D if folded else right.shape[1] // (2 * UNIT)
        start = first

        def place(unit, start=start, count=count):
            return lax.min(lax.max(unit - start, 0), count - 1)

        def left_index(unit, side, place=place, folded=folded):
            return (0, place(unit) if folded else 0)

        def right_index(unit, side, place=place, folded=folded, count=count):
            return (0, side[0] if folded else side[0] * count + place(unit))

        def head_index(unit, side, place=place, folded=folded, column=column):
            return (0, column + (place(unit) if folded else 0))

        operands += [left, right]
        specs += [
            pl.BlockSpec((left.shape[0], D), left_index),
            pl.BlockSpec((right.shape[0], UNIT), right_index),
        ]
        if head_left is not None:
            operands += [head_left, head_right]
            specs += [
                pl.BlockSpec((SEGS, D), head_index),
                pl.BlockSpec((SEGS, UNIT), right_index),
            ]
        rules.append((folded, first, count, 2 if head_left is None else 4))
        first += count
    shape = (16, first, 48, UNIT)
    whole = pl.BlockSpec(shape, lambda unit, side: (0, 0, 0, 0))
    if came is not None:
        operands.append(came)
        specs.append(whole)
    size = operands[0].shape[0]
    return pl.pallas_call(
        partial(grads_kernel, rules, int(came is not None)),
        grid_spec=pltpu.PrefetchScalarGridSpec(
            num_scalar_prefetch=1, grid=(first,), in_specs=specs, out_specs=whole
        ),
        out_shape=jax.ShapeDtypeStruct(shape, LOW),
        compiler_params=pltpu.CompilerParams(vmem_limit_bytes=60 << 20),
        cost_estimate=pl.CostEstimate(
            flops=2 * first * size * D * UNIT, bytes_accessed=30 << 20, transcendentals=0
        ),
        name="half_grads",
    )(side.astype(jnp.int32)[None], *operands)


def scatter_planes(kept):
    plane = place_here()[0]
    kept = kept.reshape(4, 4, *kept.shape[1:])
    return [
        lax.dynamic_index_in_dim(kept, plane ^ turn, axis=0, keepdims=False)
        for turn in range(4)
    ]


def scatter_across(planes, gate):
    here, next_x, next_y, across = planes
    from_y, from_x = over_y(across[:2]), over_x(across[2:])
    next_x, next_y = after(gate, next_x, next_y)
    next_x = jnp.concatenate([next_x[:2] + from_y, next_x[2:]], axis=0)
    next_y = jnp.concatenate([next_y[:2], next_y[2:] + from_x], axis=0)
    return here, next_x, next_y


def scatter_next(here, next_x, next_y, gate):
    came_x, came_y = after(gate, over_x(next_x), over_y(next_y))
    return (
        here.astype(jnp.float32) + came_x.astype(jnp.float32) + came_y.astype(jnp.float32)
    ).astype(jnp.bfloat16)


def scatter_line(here):
    depth = place_here()[1]
    slabs = [
        lax.dynamic_index_in_dim(here, (depth + step) & 3, axis=0, keepdims=False)
        for step in range(4)
    ]
    total = slabs[0].astype(jnp.float32)
    for step in (1, 2, 3):
        total = total + over_z(slabs[step], step).astype(jnp.float32)
    return total


def scatter_along(here):
    chips = here.shape[0]
    groups = [[2 * chip + core for chip in range(chips)] for core in range(2)]
    total = lax.psum_scatter(
        here.reshape(-1, here.shape[-1]),
        "fsdp",
        scatter_dimension=0,
        axis_index_groups=groups,
        tiled=True,
    )
    return total.reshape(here.shape[1:]).astype(jnp.float32)


def scatter_end(total, shapes):
    core = place_here()[2]
    mine, sent, start = [], [], 0
    for height, width in shapes:
        groups = height // 768
        count = groups if groups > 1 else width // (2 * UNIT)
        rows = jnp.concatenate(
            [total[unit] for unit in range(start, start + count)], axis=0 if groups > 1 else 1
        )
        start += count
        mine.append(fold_rows(lax.dynamic_slice_in_dim(rows, core * 24 * groups, 24 * groups), 24))
        sent.append(
            fold_rows(lax.dynamic_slice_in_dim(rows, (1 - core) * 24 * groups, 24 * groups), 24)
        )
    other = over_core(jnp.concatenate(sent, axis=1))
    owned, start = [], 0
    for (height, width), part in zip(shapes, mine):
        width = width // 2
        pair = [unfold_cols(side, width) for side in (part, other[:, start : start + part.shape[1]])]
        owned.append(both_cores(pair[0], pair[1], core, 1))
        start += part.shape[1]
    return owned


def unfold(packed, parts, ratio):
    width = packed.shape[1] // ratio
    return jnp.stack(
        [
            packed[:, width * group : width * (group + 1)].reshape(-1, parts, width)
            for group in range(ratio)
        ],
        axis=1,
    ).reshape(-1, width)


def gather_flat(shards):
    parts = min(shard.shape[0] for shard in shards)
    pieces = split_cols(
        gather(jnp.concatenate([fold_rows(shard, parts) for shard in shards], axis=1)),
        [shard.size // parts for shard in shards],
    )
    return [
        unfold(piece, parts, shard.shape[0] // parts) if shard.shape[0] > parts else piece
        for piece, shard in zip(pieces, shards)
    ]


def scatter_flat(grads):
    devices = lax.axis_size(AXES)
    parts = min(grad.shape[0] for grad in grads) // devices
    packed = jnp.concatenate(
        [
            jnp.transpose(grad.reshape(devices, -1, parts, grad.shape[1]), (0, 2, 1, 3)).reshape(
                devices * parts, -1
            )
            for grad in grads
        ],
        axis=1,
    )
    owned = split_cols(
        scatter(packed).astype(jnp.float32), [grad.size // (devices * parts) for grad in grads]
    )
    return [unfold_cols(piece, grad.shape[1]) for piece, grad in zip(owned, grads)]


def on_device(
    tokens,
    counts,
    inner_attend,
    inner_attend_bias,
    inner_merge,
    inner_merge_bias,
    inner_gain,
    inner_shift,
    inner_expand,
    inner_expand_bias,
    inner_reduce,
    inner_reduce_bias,
    inner_final_gain,
    inner_final_shift,
    outer_attend,
    outer_attend_bias,
    outer_merge,
    outer_merge_bias,
    outer_gain,
    outer_shift,
    outer_expand,
    outer_expand_bias,
    outer_reduce,
    outer_reduce_bias,
    outer_final_gain,
    outer_final_shift,
    segment_place,
    cotangent,
):
    parts = inner_merge.shape[0]
    devices = D // parts
    ratio = inner_reduce.shape[0] // parts
    here = lax.axis_index(AXES)
    linked = lax.axis_size("dp") == 4 and lax.axis_size("fsdp") == 8
    wide = inner_expand.shape[1]
    inner_rest = [inner_merge, inner_expand, inner_reduce]
    outer_all = [outer_attend, outer_merge, outer_expand, outer_reduce]
    docs = counts.shape[0]
    head_cotangent = cotangent.reshape(docs * SEGS, SEG, D)[:, 0, :]
    small_parts = (
        inner_attend_bias,
        inner_merge_bias,
        inner_gain,
        inner_shift,
        inner_expand_bias,
        inner_reduce_bias,
        inner_final_gain,
        inner_final_shift,
        outer_attend_bias,
        outer_merge_bias,
        outer_gain,
        outer_shift,
        outer_expand_bias,
        outer_reduce_bias,
        outer_final_gain,
        outer_final_shift,
    )
    sizes = [part.shape[0] for part in small_parts] + [parts]
    small = pack_small(small_parts, segment_place)
    if linked:
        slab, line = attend_line(inner_attend, small)
        late_first = late_hops(after(slab, outer_reduce))
        line = after(late_first[1:], line)
        pieces = attend_pieces(line)
        late = late_pieces(late_first, (pieces[3], pieces[4]))
        mid_line = along_z(after(line, *inner_rest[:2]))
        end_line = along_z([after(line, inner_rest[2])])
        outer_line = along_z(after(line, *outer_all[:3]))
        small_pieces = pieces[:5]
    else:
        pieces = gather_flat([inner_attend])
        small_pieces = [gather(small)]
    (
        expand_bias,
        vectors,
        outer_attend_bias_full,
        outer_expand_bias_full,
        outer_vectors,
        place_rows,
    ) = unpack_small(sizes, devices, small_pieces)
    if linked:
        mid_half = half_rows(after((pieces[3], pieces[4]), mid_line))
        attend_tokens = after(mid_half, tokens)
    else:
        attend_tokens = tokens
    projected, context, probs, attend = inner_attention(
        attend_tokens, counts, pieces, small_pieces, sizes[0]
    )
    if linked:
        mid = first_hops(mid_line, mid_half)
        end = first_hops(end_line, half_rows(after((context, mid[1], mid[2]), end_line)))
        mid = last_hops(mid, context)
        end = last_hops(end, (mid[3], mid[4], vectors))
        outer = first_hops(
            outer_line, half_rows(after((mid[3], mid[4], end[1], end[2]), outer_line))
        )
    else:
        rest = gather_flat(inner_rest)
        mid, end = [jnp.concatenate(rest[:2], axis=1)], rest[2:]
    mixed, heads, wide_heads, saved, inner_full = inner_feed(
        tokens, counts, projected, context, mid, end, expand_bias, vectors
    )
    inner_weights = (*inner_full, vectors)
    branch, grad_hidden, grad_attn, grad_context, grad_first, inner_sums, hidden_sums = (
        inner_feed_back(cotangent, counts, saved, inner_weights)
    )
    if linked:
        outer = last_hops(outer, heads, inner_sums)
    else:
        outer_full = gather_flat(outer_all)
        outer, late = [jnp.concatenate(outer_full[:3], axis=1)], outer_full[3:]
    first, normed, active, slope, second = saved
    low = jnp.bfloat16
    (
        head_out,
        grad_heads,
        left_pack,
        right_pack,
        outer_sums,
        head_branch,
        head_hidden,
        head_attn,
        head_context,
        head_first,
        head_sums,
        head_hidden_sums,
    ) = heads_step(
        counts,
        heads,
        wide_heads,
        place_rows,
        head_cotangent,
        (outer_attend_bias_full, outer_expand_bias_full, outer_vectors, vectors),
        outer,
        late[0],
        inner_full,
        linked,
    )
    grad_place = jnp.transpose(jnp.sum(grad_heads.reshape(docs, SEGS, D), axis=0))
    inner_sums = inner_sums + head_sums
    hidden_sums = hidden_sums + head_hidden_sums
    operands = (projected, probs, grad_context, grad_first, mixed)
    head_rows = (head_context, head_first, head_out)
    steps = tokens.shape[0] // ROWS
    right_all = gather(right_pack)

    def left_factors(left_pack):
        rows = jnp.concatenate(
            [
                factor.reshape(factor.shape[0], devices, -1)
                for factor in split_cols(left_pack, (D, D, D, wide))
            ],
            axis=2,
        )
        return jnp.transpose(rows, (1, 0, 2))

    def exchange(rows):
        return lax.all_to_all(rows, AXES, split_axis=0, concat_axis=0, tiled=True)

    def outer_grads(left_all, right_all):
        left_all = left_all.reshape(-1, left_all.shape[-1])
        left_pieces = split_cols(left_all, (parts, parts, parts, parts * ratio))
        right_pieces = split_cols(right_all, (3 * D, D, wide, D))
        big = [cross_rows(left, right) for left, right in zip(left_pieces, right_pieces)]
        bias = [
            lax.dynamic_slice_in_dim(
                jnp.sum(right.astype(jnp.float32), axis=0), here * width, width, axis=0
            )
            for right, width in zip(right_pieces, (3 * parts, parts, wide // devices, parts))
        ]
        return big, bias

    if linked:
        core = place_here()[2]
        jobs = [
            (normed, grad_hidden, heads, 3, head_hidden),
            (active, branch, wide_heads, wide // D, head_branch),
        ]
        sent = half_grads(jobs, 1 - core)
        left_all = exchange(left_factors(after(sent, left_pack)))
        part = inner_attend_back(
            after(sent, *operands), attend, head_rows, 0, 1, ()
        )
        kept = half_grads(jobs, after((part[3], left_all), core), over_core(sent))
        planes = scatter_planes(kept)
        middle = inner_attend_back(
            after(planes, *operands), attend, head_rows, 1, steps - 2, part[:3]
        )
        tall = scatter_across(planes, middle[3])
        rest = inner_attend_back(
            after(tall, *operands), attend, head_rows, steps - 1, 1, middle[:3]
        )
        grad_projected, tokens_grad, mixed = rest[:3]
        attend_sums = part[3] + middle[3] + rest[3]
        outer_big, outer_bias = outer_grads(*after(rest[3], left_all, right_all))
        jobs = [
            (tokens, grad_projected, None, 0, None),
            (context, grad_attn, heads, 4, head_attn),
        ]
        tall = scatter_next(*tall, (outer_big, outer_bias))
        sent = half_grads(jobs, after(tall, 1 - core))
        tall = scatter_along(tall)
        kept = half_grads(jobs, core, over_core(sent))
        short = scatter_next(*scatter_across(scatter_planes(kept), ()), ())
        sums_gate = short
        tall = held(tall, short)
        short = scatter_line(short)
        own_expand, own_reduce = scatter_end(tall, [(D, wide), (wide, D)])
        own_attend, own_merge = scatter_end(short, [(D, 3 * D), (D, D)])
    else:
        sums_gate = ()
        left_all = exchange(left_factors(left_pack))
        outer_big, outer_bias = outer_grads(left_all, right_all)
        grad_projected, tokens_grad, mixed, attend_sums = inner_attend_back(
            operands, attend, head_rows, 0, steps, ()
        )
        grad_attend = cross_rows(tokens, grad_projected).astype(low)
        grad_reduce, grad_expand, grad_merge = [
            (cross_rows(left, right) + cross_rows(head_left.astype(low), head_right)).astype(low)
            for left, right, head_left, head_right in (
                (active, branch, wide_heads[:, wide:], head_branch),
                (normed, grad_hidden, heads[:, 3 * D : 4 * D], head_hidden),
                (context, grad_attn, heads[:, 4 * D :], head_attn),
            )
        ]
        own_expand, own_reduce = scatter_flat([grad_expand, grad_reduce])
        own_attend, own_merge = scatter_flat([grad_attend, grad_merge])
    row_sums = (
        attend_sums,
        inner_sums[5],
        inner_sums[3],
        inner_sums[4],
        hidden_sums,
        inner_sums[2],
        inner_sums[0],
        inner_sums[1],
        outer_sums[2],
        outer_sums[3],
        outer_sums[0],
        outer_sums[1],
        grad_place,
    )
    sums = sum_rows(jnp.concatenate([entry.reshape(devices, -1) for entry in row_sums], axis=1), sums_gate)
    sums = split_cols(sums, [entry.size // devices for entry in row_sums])
    return (
        mixed,
        tokens_grad,
        own_attend,
        sums[0],
        own_merge,
        sums[1],
        sums[2],
        sums[3],
        own_expand,
        sums[4],
        own_reduce,
        sums[5],
        sums[6],
        sums[7],
        outer_big[0],
        outer_bias[0],
        outer_big[1],
        outer_bias[1],
        sums[8],
        sums[9],
        outer_big[2],
        outer_bias[2],
        outer_big[3],
        outer_bias[3],
        sums[10],
        sums[11],
        sums[12].reshape(parts, SEGS),
    )


def solution(mesh):
    return jax.shard_map(
        on_device,
        mesh=mesh,
        in_specs=(
            P(("dp", "fsdp"), None),
            P(("dp", "fsdp")),
            P(("dp", "fsdp"), None),
            P(("dp", "fsdp")),
            P(("dp", "fsdp"), None),
            P(("dp", "fsdp")),
            P(("dp", "fsdp")),
            P(("dp", "fsdp")),
            P(("dp", "fsdp"), None),
            P(("dp", "fsdp")),
            P(("dp", "fsdp"), None),
            P(("dp", "fsdp")),
            P(("dp", "fsdp")),
            P(("dp", "fsdp")),
            P(("dp", "fsdp"), None),
            P(("dp", "fsdp")),
            P(("dp", "fsdp"), None),
            P(("dp", "fsdp")),
            P(("dp", "fsdp")),
            P(("dp", "fsdp")),
            P(("dp", "fsdp"), None),
            P(("dp", "fsdp")),
            P(("dp", "fsdp"), None),
            P(("dp", "fsdp")),
            P(("dp", "fsdp")),
            P(("dp", "fsdp")),
            P(("dp", "fsdp"), None),
            P(("dp", "fsdp"), None),
        ),
        out_specs=(
            P(("dp", "fsdp"), None),
            P(("dp", "fsdp"), None),
            P(("dp", "fsdp"), None),
            P(("dp", "fsdp")),
            P(("dp", "fsdp"), None),
            P(("dp", "fsdp")),
            P(("dp", "fsdp")),
            P(("dp", "fsdp")),
            P(("dp", "fsdp"), None),
            P(("dp", "fsdp")),
            P(("dp", "fsdp"), None),
            P(("dp", "fsdp")),
            P(("dp", "fsdp")),
            P(("dp", "fsdp")),
            P(("dp", "fsdp"), None),
            P(("dp", "fsdp")),
            P(("dp", "fsdp"), None),
            P(("dp", "fsdp")),
            P(("dp", "fsdp")),
            P(("dp", "fsdp")),
            P(("dp", "fsdp"), None),
            P(("dp", "fsdp")),
            P(("dp", "fsdp"), None),
            P(("dp", "fsdp")),
            P(("dp", "fsdp")),
            P(("dp", "fsdp")),
            P(("dp", "fsdp"), None),
        ),
        check_vma=False,
    )
```

```python
from functools import partial

import jax
import jax.numpy as jnp
from jax import lax
from jax.experimental import pallas as pl
from jax.experimental.pallas import tpu as pltpu
from jax.sharding import PartitionSpec as P

D = 768
HEADS = 12
HD = 64
SEG = 128
SLOTS = 1024
SEGS = 8


def cross_rows(left_rows, right_rows):
    return lax.dot_general(
        left_rows, right_rows, (((0,), (0,)), ((), ())), preferred_element_type=jnp.float32
    )


def back_cols(left_rows, right_rows):
    return lax.dot_general(
        left_rows, right_rows, (((1,), (1,)), ((), ())), preferred_element_type=jnp.float32
    )


ROWS = 256
PAIR = 2 * HD
PAIRS = HEADS // 2
F32 = jnp.float32
LOW = jnp.bfloat16


def dot_nn(left, right):
    return jnp.dot(left, right, preferred_element_type=F32)


def centre_rows(rows):
    centred = rows - jnp.mean(rows, axis=-1, keepdims=True)
    spread = lax.rsqrt(jnp.mean(centred * centred, axis=-1, keepdims=True) + 1e-05)
    return centred * spread, spread


def norm_back(grad, unit, spread):
    return spread * (
        grad
        - jnp.mean(grad, axis=-1, keepdims=True)
        - unit * jnp.mean(grad * unit, axis=-1, keepdims=True)
    )


def gelu_pair(hidden):
    size = jnp.abs(hidden)
    bell = jnp.exp(hidden * hidden * -0.5)
    t = 1.0 / (1.0 + (0.3275911 * 0.7071067811865476) * size)
    poly = t * (
        0.127414796
        + t * (-0.142248368 + t * (0.7107068705 + t * (-0.7265760135 + t * 0.5307027145)))
    )
    tail = poly * bell
    phi = jnp.where(hidden >= 0, 1.0 - tail, tail)
    return hidden * phi, phi + hidden * bell * 0.3989422804014327


def two_heads(pair, axis):
    first = lax.broadcasted_iota(jnp.int32, pair.shape, 1) < HD
    zero = jnp.zeros_like(pair)
    return jnp.concatenate([jnp.where(first, pair, zero), jnp.where(first, zero, pair)], axis=axis)


def pair_probs(query, key, valid):
    scores = back_cols(two_heads(query, 0), key) * HD ** (-0.5)
    scores = jnp.where(valid, scores, -1e30)
    weight = jnp.exp(scores - jnp.max(scores, axis=-1, keepdims=True))
    return weight / jnp.sum(weight, axis=-1, keepdims=True)


def side_by_side(stacked):
    half = stacked.shape[0] // 2
    return jnp.concatenate([stacked[:half], stacked[half:]], axis=1)


def valid_keys(count_ref, segment):
    position = lax.broadcasted_iota(jnp.int32, (1, SEG), 1)
    return position < count_ref[0] - segment * SEG


def attend_copies(pieces, target, place_ref, sems):
    if len(pieces) == 1:
        return [pltpu.make_async_copy(pieces[0], target, sems.at[0])]
    plane, depth, core = place_ref[0], place_ref[1], place_ref[2]
    height, width = pieces[0].shape[1], target.shape[1] // 2
    slots = ((0, 0, 4), (1, 0, 4), (2, 0, 4), (3, 0, 2), (3, 2, 2))
    copies = []
    for side in range(2):
        lane = pl.multiple_of((core if side == 0 else 1 - core) * width, 128)
        for number, (turn, first, count) in enumerate(slots):
            for slot in range(count):
                chip = (plane ^ turn) * 4 + ((depth + 4 - first - slot) & 3)
                row = pl.multiple_of(chip * height, 48)
                copies.append(
                    pltpu.make_async_copy(
                        pieces[5 * side + number].at[slot, :, :width],
                        target.at[pl.ds(row, height), pl.ds(lane, width)],
                        sems.at[len(copies)],
                    )
                )
    return copies


def attend_kernel(count, small_count, size, count_ref, rows_ref, place_ref, *refs):
    pieces, small, refs = refs[:count], refs[count : count + small_count], refs[count + small_count :]
    projected_ref, context_ref, probs_ref, joined_ref = refs[:4]
    attend_ref, bias_ref, got_ref, sems, small_sems, out_sem = refs[4:]
    step = pl.program_id(0)
    kept = pltpu.make_async_copy(attend_ref, joined_ref, out_sem)

    @pl.when(step == 0)
    def _():
        small_waits = small_copies(small, got_ref, place_ref, small_sems)
        copies = attend_copies(pieces, attend_ref, place_ref, sems)
        for copy in small_waits + copies:
            copy.start()
        wait_all(small_waits)
        first_rows = got_ref[...].astype(F32).reshape(-1, 16 + SEGS, 128)[:, 0, :]
        bias_ref[...] = spread_row(first_rows.astype(LOW), size, bias_ref.shape[1])
        wait_all(copies)
        kept.start()

    projected_ref[...] = (dot_nn(rows_ref[...], attend_ref[...]) + bias_ref[...]).astype(LOW)
    for local in range(ROWS // SEG):
        valid = valid_keys(count_ref, step * (ROWS // SEG) + local)
        span = slice(local * SEG, (local + 1) * SEG)
        for pair in range(PAIRS):
            query, key, value = [
                projected_ref[span, part * D + pair * PAIR : part * D + (pair + 1) * PAIR]
                for part in range(3)
            ]
            probs = side_by_side(pair_probs(query, key, valid).astype(LOW))
            probs_ref[span, pair * 2 * SEG : (pair + 1) * 2 * SEG] = probs
            context_ref[span, pair * PAIR : (pair + 1) * PAIR] = dot_nn(
                probs, two_heads(value, 0)
            ).astype(LOW)

    @pl.when(step == pl.num_programs(0) - 1)
    def _():
        kept.wait()


def put_row(ref, place, start, row):
    span = slice(start, start + row.shape[1])
    here = lax.broadcasted_iota(jnp.int32, (ref.shape[0], 1), 0) == place
    ref[:, span] = jnp.where(here, row, ref[:, span])


def get_row(ref, place, span):
    here = lax.broadcasted_iota(jnp.int32, (ref.shape[0], 1), 0) == place
    return jnp.sum(jnp.where(here, ref[:, span], 0.0), axis=0, keepdims=True)


def first_row(rows, segment):
    return rows[segment * SEG : segment * SEG + 16, :].astype(F32)[:1]


def feed_kernel(
    mid_moves,
    end_moves,
    counts,
    count_ref,
    rows_ref,
    context_ref,
    place_ref,
    expand_bias_ref,
    vectors_ref,
    *refs,
):
    mid, end, refs = refs[: counts[0]], refs[counts[0] : sum(counts)], refs[sum(counts) :]
    joined, weights, sems, out_sems = refs[8:11], refs[11:14], refs[14], refs[15]
    merge_ref, expand_ref, reduce_ref = weights
    kept = [
        pltpu.make_async_copy(weight, out, out_sems.at[number])
        for number, (weight, out) in enumerate(zip(weights, joined))
    ]

    @pl.when(pl.program_id(0) == 0)
    def _():
        widths = (D, expand_ref.shape[1])
        waits = start_moves(mid, weights[:2], widths, mid_moves, place_ref, sems, 0)
        waits += start_moves(
            end, weights[2:], (D,), end_moves, place_ref, sems, 2 * len(mid_moves)
        )
        for copies, copy in zip(waits, kept):
            wait_all(copies)
            copy.start()

    feed_rows(count_ref, rows_ref, context_ref, *weights, expand_bias_ref, vectors_ref, *refs[:8])

    @pl.when(pl.program_id(0) == pl.num_programs(0) - 1)
    def _():
        wait_all(kept)


def feed_rows(
    count_ref,
    rows_ref,
    context_ref,
    merge_ref,
    expand_ref,
    reduce_ref,
    expand_bias_ref,
    vectors_ref,
    mixed_ref,
    heads_ref,
    wide_heads_ref,
    first_ref,
    normed_ref,
    active_ref,
    slope_ref,
    second_ref,
):
    step = pl.program_id(0)
    merge_bias, gain, shift, reduce_bias, final_gain, final_shift = [
        vectors_ref[row : row + 1, :] for row in range(6)
    ]
    first = rows_ref[...].astype(F32) + dot_nn(context_ref[...], merge_ref[...]) + merge_bias
    first_ref[...] = first
    normed = (centre_rows(first)[0] * gain + shift).astype(LOW)
    normed_ref[...] = normed
    second = normed.astype(F32) + reduce_bias
    chunk, wide = D, expand_ref.shape[1]
    segments = ROWS // SEG
    for start in range(0, wide, chunk):
        span = slice(start, start + chunk)
        active, slope = gelu_pair(dot_nn(normed, expand_ref[:, span]) + expand_bias_ref[:, span])
        active = active.astype(LOW)
        active_ref[:, span] = active
        slope_ref[:, span] = slope.astype(LOW)
        for local in range(segments):
            head = step * segments + local
            put_row(wide_heads_ref, head, start, slope[local * SEG : local * SEG + 1])
            put_row(wide_heads_ref, head, wide + start, first_row(active, local))
        second = second + dot_nn(active, reduce_ref[span, :])
    second_ref[...] = second
    result = centre_rows(second)[0] * final_gain + final_shift
    for local in range(segments):
        for number, rows in enumerate((result, first, second, normed, context_ref)):
            put_row(heads_ref, step * segments + local, number * D, first_row(rows, local))
    place = lax.broadcasted_iota(jnp.int32, (ROWS, 1), 0) + step * ROWS
    mixed_ref[...] = jnp.where(place < count_ref[0], result, 0.0).astype(LOW)


def feed_back_kernel(
    count_ref,
    cotangent_ref,
    second_ref,
    first_ref,
    slope_ref,
    merge_ref,
    expand_ref,
    reduce_ref,
    vectors_ref,
    branch_ref,
    hidden_ref,
    attn_ref,
    context_ref,
    first_grad_ref,
    sums_ref,
    hidden_sums_ref,
):
    step = pl.program_id(0)
    gain, final_gain = vectors_ref[1:2, :], vectors_ref[4:5, :]
    local = lax.broadcasted_iota(jnp.int32, (ROWS, 1), 0)
    plain = (local + step * ROWS < count_ref[0]) & (local % SEG != 0)
    grad = jnp.where(plain, cotangent_ref[...].astype(F32), 0.0)
    unit, spread = centre_rows(second_ref[...])
    sums = [grad * unit, grad]
    second = norm_back(grad * final_gain, unit, spread)
    branch = second.astype(LOW)
    branch_ref[...] = branch
    sums.append(branch.astype(F32))
    normed = second
    chunk = D

    @pl.when(step == 0)
    def _():
        sums_ref[...] = jnp.zeros_like(sums_ref)
        hidden_sums_ref[...] = jnp.zeros_like(hidden_sums_ref)

    for start in range(0, expand_ref.shape[1], chunk):
        span = slice(start, start + chunk)
        hidden = back_cols(branch, reduce_ref[span, :]) * slope_ref[:, span].astype(F32)
        hidden = hidden.astype(LOW)
        hidden_ref[:, span] = hidden
        hidden_sums_ref[:, span] += jnp.sum(hidden.astype(F32), axis=0, keepdims=True)
        normed = normed + back_cols(hidden, expand_ref[:, span])
    unit, spread = centre_rows(first_ref[...])
    sums += [normed * unit, normed]
    first = norm_back(normed * gain, unit, spread)
    first_grad_ref[...] = first
    attn = first.astype(LOW)
    attn_ref[...] = attn
    sums.append(attn.astype(F32))
    context_ref[...] = back_cols(attn, merge_ref[...]).astype(LOW)
    sums_ref[...] += jnp.concatenate(
        [jnp.sum(entry, axis=0, keepdims=True) for entry in sums]
        + [jnp.zeros((2, D), F32)],
        axis=0,
    )


def attend_back_kernel(
    offset,
    projected_ref,
    probs_ref,
    context_ref,
    first_ref,
    mixed_in_ref,
    attend_ref,
    head_context_ref,
    head_first_ref,
    head_out_ref,
    *refs,
):
    grad_ref, tokens_ref, mixed_ref, sums_ref = refs[-4:]
    step = pl.program_id(0)
    segments = ROWS // SEG

    @pl.when(step == 0)
    def _():
        sums_ref[...] = jnp.zeros_like(sums_ref)

    is_head = lax.broadcasted_iota(jnp.int32, (16, 1), 0) == 0
    scale = HD ** (-0.5)
    for local in range(segments):
        segment = (step + offset) * segments + local
        span = slice(local * SEG, (local + 1) * SEG)
        for pair in range(PAIRS):
            columns = [
                slice(part * D + pair * PAIR, part * D + (pair + 1) * PAIR) for part in range(3)
            ]
            query, key, value = [projected_ref[span, column] for column in columns]
            top = slice(local * SEG, local * SEG + 16)
            rest = slice(local * SEG + 16, (local + 1) * SEG)
            replaced = jnp.where(
                is_head,
                get_row(head_context_ref, segment, columns[0]),
                context_ref[top, columns[0]].astype(F32),
            ).astype(LOW)
            grad = jnp.concatenate([replaced, context_ref[rest, columns[0]]], axis=0)
            grad = two_heads(grad, 0)
            probs = probs_ref[span, pair * 2 * SEG : (pair + 1) * 2 * SEG]
            probs_low = jnp.concatenate([probs[:, :SEG], probs[:, SEG:]], axis=0)
            probs = probs_low.astype(F32)
            grad_probs = back_cols(grad, value)
            total = jnp.sum(grad_probs * probs, axis=-1, keepdims=True)
            scores = (probs * (grad_probs - total)).astype(LOW)
            grad_ref[span, columns[0]] = (
                dot_nn(side_by_side(scores), two_heads(key, 0)) * scale
            ).astype(LOW)
            grad_ref[span, columns[1]] = (
                cross_rows(scores, two_heads(query, 0)) * scale
            ).astype(LOW)
            grad_ref[span, columns[2]] = cross_rows(probs_low, grad).astype(LOW)
    tokens_ref[...] = first_ref[...] + back_cols(grad_ref[...], attend_ref[...])
    mixed_ref[...] = mixed_in_ref[...]
    for local in range(segments):
        segment = (step + offset) * segments + local
        top = slice(local * SEG, local * SEG + 16)
        missing = jnp.where(is_head, get_row(head_first_ref, segment, slice(0, D)), 0.0)
        tokens_ref[top, :] += missing
        mixed_ref[top, :] = jnp.where(
            is_head,
            get_row(head_out_ref, segment, slice(0, D)),
            mixed_in_ref[top, :].astype(F32),
        ).astype(LOW)
    sums_ref[...] += jnp.sum(grad_ref[...].astype(F32), axis=0, keepdims=True)


def by_rows(width, offset=0):
    return pl.BlockSpec((ROWS, width), lambda step: (step + offset, 0))


def entire(array):
    return pl.BlockSpec(array.shape, lambda step: (0,) * array.ndim)


def row_call(kernel, name, operands, specs, outs, flops, steps=None, earlier=(), scratch=()):
    rows = outs[0][0][0]
    shapes = [jax.ShapeDtypeStruct(shape, kind) for shape, kind, _ in outs]
    moved = sum(operand.size * operand.dtype.itemsize for operand in operands)
    moved += sum(shape.size * shape.dtype.itemsize for shape in shapes)
    return pl.pallas_call(
        kernel,
        grid=(rows // ROWS if steps is None else steps,),
        in_specs=[
            entire(operand) if spec is None else spec for operand, spec in zip(operands, specs)
        ]
        + [pl.BlockSpec(memory_space=pl.ANY)] * len(earlier),
        out_specs=[spec for _, _, spec in outs],
        out_shape=shapes,
        input_output_aliases={len(operands) + place: place for place in range(len(earlier))},
        scratch_shapes=scratch,
        compiler_params=pltpu.CompilerParams(vmem_limit_bytes=60 << 20),
        cost_estimate=pl.CostEstimate(flops=flops, bytes_accessed=moved, transcendentals=0),
        name=name,
    )(*operands, *earlier)


def whole_block(shape):
    return pl.BlockSpec(shape, lambda step: (0,) * len(shape))


def place_array():
    return jnp.stack(place_here()).astype(jnp.int32)


def inner_attention(rows, counts, pieces, small_pieces, bias_size):
    size = rows.shape[0]
    devices = D * 3 // bias_size
    smem, anywhere = pl.BlockSpec(memory_space=pltpu.SMEM), pl.BlockSpec(memory_space=pl.ANY)
    return row_call(
        partial(attend_kernel, len(pieces), len(small_pieces), bias_size),
        "attend",
        (counts, rows, place_array(), *pieces, *small_pieces),
        (smem, by_rows(D), smem) + (anywhere,) * (len(pieces) + len(small_pieces)),
        [
            ((size, 3 * D), LOW, by_rows(3 * D)),
            ((size, D), LOW, by_rows(D)),
            ((size, HEADS * SEG), LOW, by_rows(HEADS * SEG)),
            ((D, 3 * D), LOW, anywhere),
        ],
        2 * size * D * (3 * D + 4 * SEG),
        scratch=[
            pltpu.VMEM((D, 3 * D), LOW),
            pltpu.VMEM((1, 3 * D), F32),
            pltpu.VMEM((devices * (16 + SEGS), 128), LOW),
            pltpu.SemaphoreType.DMA((32,)),
            pltpu.SemaphoreType.DMA((16,)),
            pltpu.SemaphoreType.DMA,
        ],
    )


def inner_feed(rows, counts, projected, context, mid, end, expand_bias, vectors):
    size, wide = rows.shape[0], expand_bias.shape[1]
    mid_moves, end_moves = mid_moves_of(mid), mid_moves_of(end)
    smem, anywhere = pl.BlockSpec(memory_space=pltpu.SMEM), pl.BlockSpec(memory_space=pl.ANY)
    mixed, heads, wide_heads, *saved = row_call(
        partial(feed_kernel, mid_moves, end_moves, (len(mid), len(end))),
        "feed",
        (counts, rows, context, place_array(), expand_bias, vectors, *mid, *end),
        (smem, by_rows(D), by_rows(D), smem, None, None) + (anywhere,) * (len(mid) + len(end)),
        [
            ((size, D), LOW, by_rows(D)),
            ((size // SEG, 5 * D), F32, whole_block((size // SEG, 5 * D))),
            ((size // SEG, 2 * wide), F32, whole_block((size // SEG, 2 * wide))),
            ((size, D), F32, by_rows(D)),
            ((size, D), LOW, by_rows(D)),
            ((size, wide), LOW, by_rows(wide)),
            ((size, wide), LOW, by_rows(wide)),
            ((size, D), F32, by_rows(D)),
            ((D, D), LOW, anywhere),
            ((D, wide), LOW, anywhere),
            ((wide, D), LOW, anywhere),
        ],
        2 * size * D * (D + 2 * wide),
        scratch=[
            pltpu.VMEM((D, D), LOW),
            pltpu.VMEM((D, wide), LOW),
            pltpu.VMEM((wide, D), LOW),
            pltpu.SemaphoreType.DMA((2 * len(mid_moves) + len(end_moves),)),
            pltpu.SemaphoreType.DMA((3,)),
        ],
    )
    return mixed, heads, wide_heads, saved[:5], saved[5:]


def inner_feed_back(cotangent, counts, saved, weights):
    merge, expand, reduce_matrix, vectors = weights
    first, normed, active, slope, second = saved
    size, wide = cotangent.shape[0], expand.shape[1]
    return row_call(
        feed_back_kernel,
        "feed_back",
        (counts, cotangent, second, first, slope, merge, expand, reduce_matrix, vectors),
        (pl.BlockSpec(memory_space=pltpu.SMEM), by_rows(D), by_rows(D), by_rows(D), by_rows(wide))
        + (None,) * 4,
        [
            ((size, D), LOW, by_rows(D)),
            ((size, wide), LOW, by_rows(wide)),
            ((size, D), LOW, by_rows(D)),
            ((size, D), LOW, by_rows(D)),
            ((size, D), F32, by_rows(D)),
            ((8, D), F32, whole_block((8, D))),
            ((1, wide), F32, whole_block((1, wide))),
        ],
        2 * size * D * (D + 2 * wide),
    )


def inner_attend_back(operands, attend, head_rows, offset, steps, earlier):
    projected, probs, grad_context, grad_first, mixed = operands
    size = projected.shape[0]
    return row_call(
        partial(attend_back_kernel, offset),
        "attend_back",
        (projected, probs, grad_context, grad_first, mixed, attend, *head_rows),
        (by_rows(3 * D, offset), by_rows(HEADS * SEG, offset), by_rows(D, offset))
        + (by_rows(D, offset), by_rows(D, offset), None, None, None, None),
        [
            ((size, 3 * D), LOW, by_rows(3 * D, offset)),
            ((size, D), F32, by_rows(D, offset)),
            ((size, D), LOW, by_rows(D, offset)),
            ((1, 3 * D), F32, whole_block((1, 3 * D))),
        ],
        2 * steps * ROWS * D * (3 * D + 10 * SEG),
        steps,
        earlier,
    )


AXES = ("dp", "fsdp")


def gather(rows):
    return lax.all_gather(rows, AXES, axis=0, tiled=True)


def scatter(rows):
    return lax.psum_scatter(rows, AXES, scatter_dimension=0, tiled=True)


def split_cols(packed, widths):
    pieces, start = [], 0
    for width in widths:
        pieces.append(packed[..., start : start + width])
        start += width
    return pieces


def pack_kernel(*refs):
    vectors, place_ref, out_ref, rows_ref = refs[:16], refs[16], refs[17], refs[18]
    rows_ref[...] = jnp.zeros_like(rows_ref)
    for row, ref in enumerate(vectors):
        rows_ref[row : row + 1, : ref.shape[1]] = ref[...].astype(F32)
    place = jnp.transpose(place_ref[...].astype(F32))
    rows_ref[16 : 16 + SEGS, : place.shape[1]] = place
    out_ref[...] = rows_ref[...].astype(LOW)


def pack_small(vectors, segment_place):
    return pl.pallas_call(
        pack_kernel,
        out_shape=jax.ShapeDtypeStruct((16 + SEGS, 128), LOW),
        scratch_shapes=[pltpu.VMEM((16 + SEGS, 128), F32)],
        name="pack",
    )(*[vector[None] for vector in vectors], segment_place)


def spread_row(rows, size, width):
    devices = rows.shape[0]
    lane = lax.broadcasted_iota(jnp.int32, (128, width), 1)
    owner = lane // size
    pick = (lane - owner * size == lax.broadcasted_iota(jnp.int32, (128, width), 0)).astype(LOW)
    spread = dot_nn(rows, pick)
    row = lax.broadcasted_iota(jnp.int32, (devices, width), 0)
    owner = lax.broadcasted_iota(jnp.int32, (devices, width), 1) // size
    return jnp.sum(jnp.where(row == owner, spread, 0.0), axis=0, keepdims=True)


VECTOR_ROWS = (1, 2, 3, 5, 6, 7)


def small_copies(pieces, got_ref, place_ref, sems):
    if len(pieces) == 1:
        return [pltpu.make_async_copy(pieces[0], got_ref, sems.at[0])]
    plane, depth = place_ref[0], place_ref[1]
    copies = []
    slots = ((0, 0, 4), (1, 0, 4), (2, 0, 4), (3, 0, 2), (3, 2, 2))
    first_lane = pieces[0].shape[2] - 128
    for piece, (turn, first, count) in zip(pieces, slots):
        for slot in range(count):
            chip = (plane ^ turn) * 4 + ((depth + 4 - first - slot) & 3)
            copies.append(
                pltpu.make_async_copy(
                    piece.at[slot, :, first_lane : first_lane + 128],
                    got_ref.at[pl.ds(pl.multiple_of(48 * chip, 48), 48), :],
                    sems.at[len(copies)],
                )
            )
    return copies


def unpack_kernel(sizes, place_ref, *refs):
    outs, got_ref, sems = (None, *refs[-8:-2]), refs[-2], refs[-1]
    pieces = refs[:-8]
    copies = small_copies(pieces, got_ref, place_ref, sems)
    for copy in copies:
        copy.start()
    wait_all(copies)
    got = got_ref[...].astype(F32).reshape(-1, 16 + SEGS, 128)
    devices = got.shape[0]
    for block in range(2):
        attend_ref, expand_ref, vectors_ref = outs[3 * block : 3 * block + 3]
        for kind in range(1 - block, 8):
            row = 8 * block + kind
            size = sizes[row]
            spread = spread_row(got[:, row, :].astype(LOW), size, size * devices)
            if kind == 0:
                attend_ref[...] = spread
            elif kind == 4:
                expand_ref[...] = spread
            else:
                place = VECTOR_ROWS.index(kind)
                vectors_ref[place : place + 1, :] = spread
        vectors_ref[6:8, :] = jnp.zeros((2, vectors_ref.shape[1]), F32)
    for segment in range(SEGS):
        outs[6][segment : segment + 1, :] = spread_row(
            got[:, 16 + segment, :].astype(LOW), sizes[16], sizes[16] * devices
        )


def unpack_small(sizes, devices, pieces):
    shapes = []
    for block in range(2):
        for rows, size in ((1, sizes[8 * block]), (1, sizes[8 * block + 4]), (8, sizes[1])):
            shapes.append(jax.ShapeDtypeStruct((rows, size * devices), F32))
    shapes.append(jax.ShapeDtypeStruct((SEGS, sizes[16] * devices), F32))
    return pl.pallas_call(
        partial(unpack_kernel, sizes),
        out_shape=shapes[1:],
        in_specs=[pl.BlockSpec(memory_space=pltpu.SMEM)]
        + [pl.BlockSpec(memory_space=pl.ANY)] * len(pieces),
        scratch_shapes=[
            pltpu.VMEM((devices * (16 + SEGS), 128), LOW),
            pltpu.SemaphoreType.DMA((16,)),
        ],
        compiler_params=pltpu.CompilerParams(vmem_limit_bytes=60 << 20),
        name="unpack",
    )(place_array(), *pieces)


def sum_rows(rows, gate):
    devices, size = rows.shape
    padded = jnp.pad(rows, ((0, 0), (0, -size % 1024))).reshape(devices, -1, 128)
    got = lax.all_to_all(padded, AXES, split_axis=0, concat_axis=0, tiled=True)
    return jnp.sum(after(gate, got), axis=0).reshape(-1)[:size]


def hop(array, turn):
    return lax.ppermute(array, AXES, [(place, turn(place)) for place in range(32)])


def over_x(array):
    return hop(array, lambda place: place ^ 8)


def over_y(array):
    return hop(array, lambda place: place ^ 16)


def over_core(array):
    return hop(array, lambda place: place ^ 1)


def over_z(array, step):
    return hop(array, lambda place: (place & ~6) | ((((place >> 1) + step) & 3) << 1))


def place_here():
    chip = lax.axis_index("fsdp")
    return lax.axis_index("dp"), chip // 2, chip % 2


def half_cols(array, core):
    width = array.shape[-1] // 2
    return lax.dynamic_slice_in_dim(array, core * width, width, axis=array.ndim - 1)


def fold_rows(array, rows):
    return jnp.concatenate(jnp.split(array, array.shape[0] // rows, axis=0), axis=1)


def unfold_cols(array, width):
    return jnp.concatenate(jnp.split(array, array.shape[1] // width, axis=1), axis=0)


def both_cores(mine, other, core, axis):
    return jnp.concatenate(
        [jnp.where(core == 0, mine, other), jnp.where(core == 0, other, mine)], axis=axis
    )


def attend_line(shard, small):
    core = place_here()[2]
    mine = jnp.concatenate([half_cols(shard, core), small], axis=1)
    sent = jnp.concatenate([half_cols(shard, 1 - core), small], axis=1)
    slab = both_cores(mine, over_core(sent), core, 0)
    hops = [over_z(slab, step) for step in (1, 2, 3)]
    return slab, jnp.stack([slab] + hops)


def attend_pieces(line):
    line_x, line_y = over_x(line), over_y(line)
    pieces = [line, line_x, line_y, over_y(line_x[:2]), over_x(line_y[2:])]
    return pieces + [over_core(piece) for piece in pieces]


def held(array, first):
    return array + first.reshape(-1)[:1].reshape((1,) * array.ndim).astype(array.dtype) * 0


def after(first, *later):
    tied = lax.optimization_barrier((first, later))[1]
    return tied[0] if len(tied) == 1 else tied


def half_rows(line):
    half = line.shape[0] // 2
    return lax.dynamic_slice_in_dim(line, place_here()[2] * half, half, axis=0)


def first_hops(line, mine):
    return line, over_x(mine), over_y(mine)


def last_hops(hops, gate, late_gate=()):
    line, from_x, from_y = hops
    half = from_x.shape[0] // 2
    sent_y, sent_x = after(gate, from_x[:half], from_y[half:])
    pieces = [from_x, from_y, over_y(sent_y), over_x(sent_x)]
    return [line] + pieces + [over_core(piece) for piece in after(late_gate, *pieces)]


def late_hops(shard):
    return shard, over_x(shard), over_y(shard)


def late_pieces(hops, gate):
    shard, from_x, from_y = hops
    half = shard.shape[0] // 2
    sent_y, sent_x = held(from_x[:half], gate), held(from_y[half:], gate)
    across = jnp.concatenate([over_y(sent_y), over_x(sent_x)], axis=0)
    rows = jnp.concatenate([shard, from_x, from_y, across], axis=0)
    return [lax.all_gather(rows, "fsdp", axis=0, tiled=True)]


def along_z(shards):
    return lax.all_gather(jnp.concatenate(shards, axis=1), "fsdp", axis=0, tiled=True)


def start_moves(pieces, outs, widths, moves, place_ref, sems, first):
    plane, core = place_ref[0], place_ref[2]
    groups, start = [], 0
    for out, width in zip(outs, widths):
        copies = []
        for piece, source, rows, turn, quarter, side, offset in moves:
            row = (plane ^ turn) * quarter + offset
            if side is not None:
                row = row + (core if side == 0 else 1 - core) * (quarter // 2)
            copies.append(
                pltpu.make_async_copy(
                    pieces[piece].at[source : source + rows, start : start + width],
                    out.at[pl.ds(pl.multiple_of(row, 48), rows), :],
                    sems.at[first],
                )
            )
            first += 1
        start += width
        groups.append(copies)
    for copies in groups:
        for copy in copies:
            copy.start()
    return groups


def wait_all(copies):
    for copy in copies:
        copy.wait()


def column_sums(rows):
    return jnp.sum(rows, axis=0, keepdims=True)


def feed_rows_back(grad, unit, spread, slope_of, reduce_ref, expand_ref, final_gain):
    second = norm_back(grad * final_gain, unit, spread)
    branch = second.astype(LOW)
    normed, hidden = second, []
    for start in range(0, expand_ref.shape[1], D):
        span = slice(start, start + D)
        part = (back_cols(branch, reduce_ref[span, :]) * slope_of(span)).astype(LOW)
        hidden.append(part)
        normed = normed + back_cols(part, expand_ref[:, span])
    return branch, hidden, normed


def heads_kernel(
    counts,
    mid_moves,
    end_moves,
    place_ref,
    count_ref,
    heads_ref,
    wide_heads_ref,
    table_ref,
    cotangent_ref,
    attend_bias_ref,
    expand_bias_ref,
    vectors_ref,
    inner_vectors_ref,
    *refs,
):
    mid_count, end_count = counts
    mid, refs = refs[:mid_count], refs[mid_count:]
    end, refs = refs[:end_count], refs[end_count:]
    inner_hbm, refs = refs[:3], refs[3:]
    out_ref, grad_ref, left_ref, right_ref, sums_ref = refs[:5]
    branch_ref, hidden_ref, attn_ref, context_ref, first_ref, inner_sums_ref, hidden_sums_ref = refs[5:12]
    attend_ref, merge_ref, expand_ref, reduce_ref = refs[12:16]
    inner_refs, sems = refs[16:19], refs[19]
    wide = expand_ref.shape[1]
    waits = start_moves(
        mid, (attend_ref, merge_ref, expand_ref), (3 * D, D, wide), mid_moves, place_ref, sems, 0
    )
    first_free = 3 * len(mid_moves)
    waits += start_moves(end, (reduce_ref,), (D,), end_moves, place_ref, sems, first_free)
    first_free += len(end_moves)
    inner_waits = [
        pltpu.make_async_copy(source, target, sems.at[first_free + number])
        for number, (source, target) in enumerate(zip(inner_hbm, inner_refs))
    ]
    for copy in inner_waits:
        copy.start()
    merge_bias, gain, shift, reduce_bias, final_gain, final_shift = [
        vectors_ref[row : row + 1, :] for row in range(6)
    ]
    scale = HD ** (-0.5)
    stacked = HEADS * SEGS
    own = (
        lax.broadcasted_iota(jnp.int32, (stacked, D), 1) // HD
        == lax.broadcasted_iota(jnp.int32, (stacked, D), 0) // SEGS
    )

    def by_head(rows):
        return jnp.where(own, jnp.concatenate([rows] * HEADS, axis=0), 0.0).astype(LOW)

    def join_heads(rows):
        rows = jnp.where(own, rows, 0.0)
        return sum(rows[SEGS * head : SEGS * (head + 1)] for head in range(HEADS))

    keep = (
        lax.broadcasted_iota(jnp.int32, (SEGS, 1), 0) * SEG < count_ref[0]
    ).astype(F32)
    source = (heads_ref[:, :D] + table_ref[...]).astype(LOW)
    wait_all(waits[0])
    projected = (dot_nn(source, attend_ref[...]) + attend_bias_ref[...]).astype(LOW)
    query, key, value = projected[:, :D], projected[:, D : 2 * D], projected[:, 2 * D :]
    queries = by_head(query.astype(F32))
    scores = back_cols(queries, key) * scale
    weight = jnp.exp(scores - jnp.max(scores, axis=-1, keepdims=True))
    probs = weight / jnp.sum(weight, axis=-1, keepdims=True)
    probs_low = probs.astype(LOW)
    context = join_heads(dot_nn(probs_low, value)).astype(LOW)
    wait_all(waits[1])
    first = source.astype(F32) + dot_nn(context, merge_ref[...]) + merge_bias
    first_unit, first_spread = centre_rows(first)
    normed = (first_unit * gain + shift).astype(LOW)
    left_ref[:, :D] = source
    left_ref[:, D : 2 * D] = context
    left_ref[:, 2 * D : 3 * D] = normed
    second = normed.astype(F32) + reduce_bias
    slopes = {}
    wait_all(waits[2])
    wait_all(waits[3])
    for start in range(0, wide, D):
        span = slice(start, start + D)
        active, slopes[start] = gelu_pair(
            dot_nn(normed, expand_ref[:, span]) + expand_bias_ref[:, span]
        )
        active = active.astype(LOW)
        left_ref[:, 3 * D + start : 4 * D + start] = active
        second = second + dot_nn(active, reduce_ref[span, :])
    unit, spread = centre_rows(second)
    out_ref[...] = (unit * final_gain + final_shift) * keep
    grad = cotangent_ref[...].astype(F32) * keep
    sums = [column_sums(grad * unit), column_sums(grad)]
    branch, hidden, grad_normed = feed_rows_back(
        grad, unit, spread, lambda span: slopes[span.start], reduce_ref, expand_ref, final_gain
    )
    sums += [column_sums(grad_normed * first_unit), column_sums(grad_normed)]
    grad_first = norm_back(grad_normed * gain, first_unit, first_spread)
    attn = grad_first.astype(LOW)
    grads = by_head(back_cols(attn, merge_ref[...]).astype(LOW).astype(F32))
    grad_probs = back_cols(grads, value)
    total = jnp.sum(grad_probs * probs, axis=-1, keepdims=True)
    grad_scores = (probs * (grad_probs - total)).astype(LOW)
    grad_query = (join_heads(dot_nn(grad_scores, key)) * scale).astype(LOW)
    grad_key = (cross_rows(grad_scores, queries) * scale).astype(LOW)
    grad_value = cross_rows(probs_low, grads).astype(LOW)
    grad_projected = jnp.concatenate([grad_query, grad_key, grad_value], axis=1)
    right_ref[:, : 3 * D] = grad_projected
    right_ref[:, 3 * D : 4 * D] = attn
    for number, part in enumerate(hidden):
        right_ref[:, (4 + number) * D : (5 + number) * D] = part
    right_ref[:, 4 * D + wide :] = branch
    sums_ref[...] = jnp.concatenate(sums + [jnp.zeros((4, D), F32)], axis=0)
    grad = grad_first + back_cols(grad_projected, attend_ref[...])
    grad_ref[...] = grad

    wait_all(inner_waits)
    inner_merge_ref, inner_expand_ref, inner_reduce_ref = inner_refs
    gain, final_gain = inner_vectors_ref[1:2, :], inner_vectors_ref[4:5, :]
    first_unit, first_spread = centre_rows(heads_ref[:, D : 2 * D])
    unit, spread = centre_rows(heads_ref[:, 2 * D : 3 * D])
    sums = [column_sums(grad * unit), column_sums(grad)]
    branch, hidden, grad_normed = feed_rows_back(
        grad,
        unit,
        spread,
        lambda span: wide_heads_ref[:, span],
        inner_reduce_ref,
        inner_expand_ref,
        final_gain,
    )
    branch_ref[...] = branch
    sums.append(column_sums(branch.astype(F32)))
    for number, part in enumerate(hidden):
        span = slice(number * D, (number + 1) * D)
        hidden_ref[:, span] = part
        hidden_sums_ref[:, span] = column_sums(part.astype(F32))
    sums += [column_sums(grad_normed * first_unit), column_sums(grad_normed)]
    grad_first = norm_back(grad_normed * gain, first_unit, first_spread)
    first_ref[...] = grad_first
    attn = grad_first.astype(LOW)
    attn_ref[...] = attn
    sums.append(column_sums(attn.astype(F32)))
    context_ref[...] = back_cols(attn, inner_merge_ref[...]).astype(LOW).astype(F32)
    inner_sums_ref[...] = jnp.concatenate(sums + [jnp.zeros((2, D), F32)], axis=0)


def mid_moves_of(pieces):
    if len(pieces) == 1:
        return [(0, 0, pieces[0].shape[0], 0, 0, None, 0)]
    quarter = pieces[0].shape[0]
    half = quarter // 2
    moves = [(0, 0, quarter, 0, quarter, None, 0)]
    for side in range(2):
        moves += [
            (1 + 4 * side, 0, half, 1, quarter, side, 0),
            (2 + 4 * side, 0, half, 2, quarter, side, 0),
            (3 + 4 * side, 0, half // 2, 3, quarter, side, 0),
            (4 + 4 * side, 0, half // 2, 3, quarter, side, half // 2),
        ]
    return moves


def late_moves_of(piece, linked):
    if not linked:
        return [(0, 0, piece.shape[0], 0, 0, None, 0)]
    rows = piece.shape[0] // 32
    return [
        (0, (4 * slot + turn) * rows, rows, turn, 8 * rows, None, slot * rows)
        for slot in range(8)
        for turn in range(4)
    ]


def heads_step(counts, heads, wide_heads, table, cotangent, small, mid, late, inner, linked):
    attend_bias, expand_bias, vectors, inner_vectors = small
    wide = expand_bias.shape[1]
    mid_moves, end_moves = mid_moves_of(mid), late_moves_of(late, linked)
    plane, depth, core = place_here()
    place = jnp.stack([plane, depth, core]).astype(jnp.int32)
    vmem = pl.BlockSpec(memory_space=pltpu.VMEM)
    smem = pl.BlockSpec(memory_space=pltpu.SMEM)
    outs = [
        ((SEGS, D), F32),
        ((SEGS, D), F32),
        ((SEGS, 3 * D + wide), LOW),
        ((SEGS, 5 * D + wide), LOW),
        ((8, D), F32),
        ((SEGS, D), LOW),
        ((SEGS, wide), LOW),
        ((SEGS, D), LOW),
        ((SEGS, D), F32),
        ((SEGS, D), F32),
        ((8, D), F32),
        ((1, wide), F32),
    ]
    flops = 6 * SEGS * D * (5 * D + 4 * wide)
    moved = 2 * D * (6 * D + 4 * wide)
    return pl.pallas_call(
        partial(heads_kernel, (len(mid), 1), mid_moves, end_moves),
        out_shape=[jax.ShapeDtypeStruct(shape, kind) for shape, kind in outs],
        in_specs=[smem, smem] + [vmem] * 8 + [pl.BlockSpec(memory_space=pl.ANY)] * (len(mid) + 4),
        out_specs=[vmem] * len(outs),
        scratch_shapes=[
            pltpu.VMEM((D, 3 * D), LOW),
            pltpu.VMEM((D, D), LOW),
            pltpu.VMEM((D, wide), LOW),
            pltpu.VMEM((wide, D), LOW),
            pltpu.VMEM((D, D), LOW),
            pltpu.VMEM((D, wide), LOW),
            pltpu.VMEM((wide, D), LOW),
            pltpu.SemaphoreType.DMA((3 * len(mid_moves) + len(end_moves) + 3,)),
        ],
        compiler_params=pltpu.CompilerParams(vmem_limit_bytes=60 << 20),
        cost_estimate=pl.CostEstimate(flops=flops, bytes_accessed=moved, transcendentals=0),
        name="heads",
    )(
        place,
        counts,
        heads,
        wide_heads,
        table,
        cotangent,
        attend_bias,
        expand_bias,
        vectors,
        inner_vectors,
        *mid,
        late,
        *inner,
    )


UNIT = 384


def grads_kernel(jobs, adds, side_ref, *refs):
    refs, came_ref, out_ref = refs[: -1 - adds], refs[-2], refs[-1]
    unit = pl.program_id(0)

    def put(chips, units, shape, total):
        total = total.reshape(shape)
        if adds:
            total = total + came_ref[chips, units].astype(F32)
        out_ref[chips, units] = total.astype(LOW)

    for folded, first, count, number in jobs:
        (left_ref, right_ref), heads, refs = refs[:2], refs[2:number], refs[number:]

        @pl.when((unit >= first) & (unit < first + count))
        def _(folded=folded, first=first, left_ref=left_ref, right_ref=right_ref, heads=heads):
            total = cross_rows(left_ref[...], right_ref[...])
            if heads:
                total = total + cross_rows(heads[0][...].astype(LOW), heads[1][...])
            if folded:
                chips = pl.ds(4 * (unit - first), 4)
                put(chips, slice(first, first + 4), (4, 4, 48, UNIT), total)
            else:
                put(slice(None), pl.ds(unit, 1), (16, 1, 48, UNIT), total)


def half_grads(jobs, side, came=None):
    rules, operands, specs, first = [], [], [], 0
    for left, right, head_left, column, head_right in jobs:
        folded = left.shape[1] > D
        count = left.shape[1] // D if folded else right.shape[1] // (2 * UNIT)
        start = first

        def place(unit, start=start, count=count):
            return lax.min(lax.max(unit - start, 0), count - 1)

        def left_index(unit, side, place=place, folded=folded):
            return (0, place(unit) if folded else 0)

        def right_index(unit, side, place=place, folded=folded, count=count):
            return (0, side[0] if folded else side[0] * count + place(unit))

        def head_index(unit, side, place=place, folded=folded, column=column):
            return (0, column + (place(unit) if folded else 0))

        operands += [left, right]
        specs += [
            pl.BlockSpec((left.shape[0], D), left_index),
            pl.BlockSpec((right.shape[0], UNIT), right_index),
        ]
        if head_left is not None:
            operands += [head_left, head_right]
            specs += [
                pl.BlockSpec((SEGS, D), head_index),
                pl.BlockSpec((SEGS, UNIT), right_index),
            ]
        rules.append((folded, first, count, 2 if head_left is None else 4))
        first += count
    shape = (16, first, 48, UNIT)
    whole = pl.BlockSpec(shape, lambda unit, side: (0, 0, 0, 0))
    if came is not None:
        operands.append(came)
        specs.append(whole)
    size = operands[0].shape[0]
    return pl.pallas_call(
        partial(grads_kernel, rules, int(came is not None)),
        grid_spec=pltpu.PrefetchScalarGridSpec(
            num_scalar_prefetch=1, grid=(first,), in_specs=specs, out_specs=whole
        ),
        out_shape=jax.ShapeDtypeStruct(shape, LOW),
        compiler_params=pltpu.CompilerParams(vmem_limit_bytes=60 << 20),
        cost_estimate=pl.CostEstimate(
            flops=2 * first * size * D * UNIT, bytes_accessed=30 << 20, transcendentals=0
        ),
        name="half_grads",
    )(side.astype(jnp.int32)[None], *operands)


def scatter_planes(kept):
    plane = place_here()[0]
    kept = kept.reshape(4, 4, *kept.shape[1:])
    return [
        lax.dynamic_index_in_dim(kept, plane ^ turn, axis=0, keepdims=False)
        for turn in range(4)
    ]


def scatter_across(planes, gate):
    here, next_x, next_y, across = planes
    from_y, from_x = over_y(across[:2]), over_x(across[2:])
    next_x, next_y = after(gate, next_x, next_y)
    next_x = jnp.concatenate([next_x[:2] + from_y, next_x[2:]], axis=0)
    next_y = jnp.concatenate([next_y[:2], next_y[2:] + from_x], axis=0)
    return here, next_x, next_y


def scatter_next(here, next_x, next_y, gate):
    came_x, came_y = after(gate, over_x(next_x), over_y(next_y))
    return (
        here.astype(jnp.float32) + came_x.astype(jnp.float32) + came_y.astype(jnp.float32)
    ).astype(jnp.bfloat16)


def scatter_line(here):
    depth = place_here()[1]
    slabs = [
        lax.dynamic_index_in_dim(here, (depth + step) & 3, axis=0, keepdims=False)
        for step in range(4)
    ]
    total = slabs[0].astype(jnp.float32)
    for step in (1, 2, 3):
        total = total + over_z(slabs[step], step).astype(jnp.float32)
    return total


def scatter_along(here):
    chips = here.shape[0]
    groups = [[2 * chip + core for chip in range(chips)] for core in range(2)]
    total = lax.psum_scatter(
        here.reshape(-1, here.shape[-1]),
        "fsdp",
        scatter_dimension=0,
        axis_index_groups=groups,
        tiled=True,
    )
    return total.reshape(here.shape[1:]).astype(jnp.float32)


def scatter_end(total, shapes):
    core = place_here()[2]
    mine, sent, start = [], [], 0
    for height, width in shapes:
        groups = height // 768
        count = groups if groups > 1 else width // (2 * UNIT)
        rows = jnp.concatenate(
            [total[unit] for unit in range(start, start + count)], axis=0 if groups > 1 else 1
        )
        start += count
        mine.append(fold_rows(lax.dynamic_slice_in_dim(rows, core * 24 * groups, 24 * groups), 24))
        sent.append(
            fold_rows(lax.dynamic_slice_in_dim(rows, (1 - core) * 24 * groups, 24 * groups), 24)
        )
    other = over_core(jnp.concatenate(sent, axis=1))
    owned, start = [], 0
    for (height, width), part in zip(shapes, mine):
        width = width // 2
        pair = [unfold_cols(side, width) for side in (part, other[:, start : start + part.shape[1]])]
        owned.append(both_cores(pair[0], pair[1], core, 1))
        start += part.shape[1]
    return owned


def unfold(packed, parts, ratio):
    width = packed.shape[1] // ratio
    return jnp.stack(
        [
            packed[:, width * group : width * (group + 1)].reshape(-1, parts, width)
            for group in range(ratio)
        ],
        axis=1,
    ).reshape(-1, width)


def gather_flat(shards):
    parts = min(shard.shape[0] for shard in shards)
    pieces = split_cols(
        gather(jnp.concatenate([fold_rows(shard, parts) for shard in shards], axis=1)),
        [shard.size // parts for shard in shards],
    )
    return [
        unfold(piece, parts, shard.shape[0] // parts) if shard.shape[0] > parts else piece
        for piece, shard in zip(pieces, shards)
    ]


def scatter_flat(grads):
    devices = lax.axis_size(AXES)
    parts = min(grad.shape[0] for grad in grads) // devices
    packed = jnp.concatenate(
        [
            jnp.transpose(grad.reshape(devices, -1, parts, grad.shape[1]), (0, 2, 1, 3)).reshape(
                devices * parts, -1
            )
            for grad in grads
        ],
        axis=1,
    )
    owned = split_cols(
        scatter(packed).astype(jnp.float32), [grad.size // (devices * parts) for grad in grads]
    )
    return [unfold_cols(piece, grad.shape[1]) for piece, grad in zip(owned, grads)]


def on_device(
    tokens,
    counts,
    inner_attend,
    inner_attend_bias,
    inner_merge,
    inner_merge_bias,
    inner_gain,
    inner_shift,
    inner_expand,
    inner_expand_bias,
    inner_reduce,
    inner_reduce_bias,
    inner_final_gain,
    inner_final_shift,
    outer_attend,
    outer_attend_bias,
    outer_merge,
    outer_merge_bias,
    outer_gain,
    outer_shift,
    outer_expand,
    outer_expand_bias,
    outer_reduce,
    outer_reduce_bias,
    outer_final_gain,
    outer_final_shift,
    segment_place,
    cotangent,
):
    parts = inner_merge.shape[0]
    devices = D // parts
    ratio = inner_reduce.shape[0] // parts
    here = lax.axis_index(AXES)
    linked = lax.axis_size("dp") == 4 and lax.axis_size("fsdp") == 8
    wide = inner_expand.shape[1]
    inner_rest = [inner_merge, inner_expand, inner_reduce]
    outer_all = [outer_attend, outer_merge, outer_expand, outer_reduce]
    docs = counts.shape[0]
    head_cotangent = cotangent.reshape(docs * SEGS, SEG, D)[:, 0, :]
    small_parts = (
        inner_attend_bias,
        inner_merge_bias,
        inner_gain,
        inner_shift,
        inner_expand_bias,
        inner_reduce_bias,
        inner_final_gain,
        inner_final_shift,
        outer_attend_bias,
        outer_merge_bias,
        outer_gain,
        outer_shift,
        outer_expand_bias,
        outer_reduce_bias,
        outer_final_gain,
        outer_final_shift,
    )
    sizes = [part.shape[0] for part in small_parts] + [parts]
    small = pack_small(small_parts, segment_place)
    if linked:
        slab, line = attend_line(inner_attend, small)
        late_first = late_hops(after(slab, outer_reduce))
        line = after(late_first[1:], line)
        pieces = attend_pieces(line)
        mid_line = along_z(after(line, *inner_rest[:2]))
        end_line = along_z([after(line, inner_rest[2])])
        outer_line = along_z(after(line, *outer_all[:3]))
        small_pieces = pieces[:5]
    else:
        pieces = gather_flat([inner_attend])
        small_pieces = [gather(small)]
    (
        expand_bias,
        vectors,
        outer_attend_bias_full,
        outer_expand_bias_full,
        outer_vectors,
        place_rows,
    ) = unpack_small(sizes, devices, small_pieces)
    if linked:
        mid_half = half_rows(after((pieces[3], pieces[4]), mid_line))
        late = late_pieces(late_first, mid_half)
        attend_tokens = after(mid_half, tokens)
    else:
        attend_tokens = tokens
    projected, context, probs, attend = inner_attention(
        attend_tokens, counts, pieces, small_pieces, sizes[0]
    )
    if linked:
        mid = first_hops(mid_line, mid_half)
        end = first_hops(end_line, half_rows(after((context, mid[1], mid[2]), end_line)))
        mid = last_hops(mid, context)
        end = last_hops(end, (mid[3], mid[4], vectors))
        outer = first_hops(
            outer_line, half_rows(after((mid[3], mid[4], end[1], end[2]), outer_line))
        )
    else:
        rest = gather_flat(inner_rest)
        mid, end = [jnp.concatenate(rest[:2], axis=1)], rest[2:]
    mixed, heads, wide_heads, saved, inner_full = inner_feed(
        tokens, counts, projected, context, mid, end, expand_bias, vectors
    )
    inner_weights = (*inner_full, vectors)
    branch, grad_hidden, grad_attn, grad_context, grad_first, inner_sums, hidden_sums = (
        inner_feed_back(cotangent, counts, saved, inner_weights)
    )
    if linked:
        outer = last_hops(outer, heads, inner_sums)
    else:
        outer_full = gather_flat(outer_all)
        outer, late = [jnp.concatenate(outer_full[:3], axis=1)], outer_full[3:]
    first, normed, active, slope, second = saved
    low = jnp.bfloat16
    (
        head_out,
        grad_heads,
        left_pack,
        right_pack,
        outer_sums,
        head_branch,
        head_hidden,
        head_attn,
        head_context,
        head_first,
        head_sums,
        head_hidden_sums,
    ) = heads_step(
        counts,
        heads,
        wide_heads,
        place_rows,
        head_cotangent,
        (outer_attend_bias_full, outer_expand_bias_full, outer_vectors, vectors),
        outer,
        late[0],
        inner_full,
        linked,
    )
    grad_place = jnp.transpose(jnp.sum(grad_heads.reshape(docs, SEGS, D), axis=0))
    inner_sums = inner_sums + head_sums
    hidden_sums = hidden_sums + head_hidden_sums
    operands = (projected, probs, grad_context, grad_first, mixed)
    head_rows = (head_context, head_first, head_out)
    steps = tokens.shape[0] // ROWS
    right_all = gather(right_pack)

    def left_factors(left_pack):
        rows = jnp.concatenate(
            [
                factor.reshape(factor.shape[0], devices, -1)
                for factor in split_cols(left_pack, (D, D, D, wide))
            ],
            axis=2,
        )
        return jnp.transpose(rows, (1, 0, 2))

    def exchange(rows):
        return lax.all_to_all(rows, AXES, split_axis=0, concat_axis=0, tiled=True)

    def outer_grads(left_all, right_all):
        left_all = left_all.reshape(-1, left_all.shape[-1])
        left_pieces = split_cols(left_all, (parts, parts, parts, parts * ratio))
        right_pieces = split_cols(right_all, (3 * D, D, wide, D))
        big = [cross_rows(left, right) for left, right in zip(left_pieces, right_pieces)]
        bias = [
            lax.dynamic_slice_in_dim(
                jnp.sum(right.astype(jnp.float32), axis=0), here * width, width, axis=0
            )
            for right, width in zip(right_pieces, (3 * parts, parts, wide // devices, parts))
        ]
        return big, bias

    if linked:
        core = place_here()[2]
        jobs = [
            (normed, grad_hidden, heads, 3, head_hidden),
            (active, branch, wide_heads, wide // D, head_branch),
        ]
        sent = half_grads(jobs, 1 - core)
        left_all = exchange(left_factors(after(sent, left_pack)))
        part = inner_attend_back(
            after(sent, *operands), attend, head_rows, 0, 1, ()
        )
        kept = half_grads(jobs, after((part[3], left_all), core), over_core(sent))
        planes = scatter_planes(kept)
        middle = inner_attend_back(
            after(planes, *operands), attend, head_rows, 1, steps - 2, part[:3]
        )
        tall = scatter_across(planes, middle[3])
        rest = inner_attend_back(
            after(tall, *operands), attend, head_rows, steps - 1, 1, middle[:3]
        )
        grad_projected, tokens_grad, mixed = rest[:3]
        attend_sums = part[3] + middle[3] + rest[3]
        outer_big, outer_bias = outer_grads(*after(rest[3], left_all, right_all))
        jobs = [
            (tokens, grad_projected, None, 0, None),
            (context, grad_attn, heads, 4, head_attn),
        ]
        tall = scatter_next(*tall, (outer_big, outer_bias))
        sent = half_grads(jobs, after(tall, 1 - core))
        tall = scatter_along(tall)
        kept = half_grads(jobs, core, over_core(sent))
        short = scatter_next(*scatter_across(scatter_planes(kept), ()), ())
        sums_gate = short
        tall = held(tall, short)
        short = scatter_line(short)
        own_expand, own_reduce = scatter_end(tall, [(D, wide), (wide, D)])
        own_attend, own_merge = scatter_end(short, [(D, 3 * D), (D, D)])
    else:
        sums_gate = ()
        left_all = exchange(left_factors(left_pack))
        outer_big, outer_bias = outer_grads(left_all, right_all)
        grad_projected, tokens_grad, mixed, attend_sums = inner_attend_back(
            operands, attend, head_rows, 0, steps, ()
        )
        grad_attend = cross_rows(tokens, grad_projected).astype(low)
        grad_reduce, grad_expand, grad_merge = [
            (cross_rows(left, right) + cross_rows(head_left.astype(low), head_right)).astype(low)
            for left, right, head_left, head_right in (
                (active, branch, wide_heads[:, wide:], head_branch),
                (normed, grad_hidden, heads[:, 3 * D : 4 * D], head_hidden),
                (context, grad_attn, heads[:, 4 * D :], head_attn),
            )
        ]
        own_expand, own_reduce = scatter_flat([grad_expand, grad_reduce])
        own_attend, own_merge = scatter_flat([grad_attend, grad_merge])
    row_sums = (
        attend_sums,
        inner_sums[5],
        inner_sums[3],
        inner_sums[4],
        hidden_sums,
        inner_sums[2],
        inner_sums[0],
        inner_sums[1],
        outer_sums[2],
        outer_sums[3],
        outer_sums[0],
        outer_sums[1],
        grad_place,
    )
    sums = sum_rows(jnp.concatenate([entry.reshape(devices, -1) for entry in row_sums], axis=1), sums_gate)
    sums = split_cols(sums, [entry.size // devices for entry in row_sums])
    return (
        mixed,
        tokens_grad,
        own_attend,
        sums[0],
        own_merge,
        sums[1],
        sums[2],
        sums[3],
        own_expand,
        sums[4],
        own_reduce,
        sums[5],
        sums[6],
        sums[7],
        outer_big[0],
        outer_bias[0],
        outer_big[1],
        outer_bias[1],
        sums[8],
        sums[9],
        outer_big[2],
        outer_bias[2],
        outer_big[3],
        outer_bias[3],
        sums[10],
        sums[11],
        sums[12].reshape(parts, SEGS),
    )


def solution(mesh):
    return jax.shard_map(
        on_device,
        mesh=mesh,
        in_specs=(
            P(("dp", "fsdp"), None),
            P(("dp", "fsdp")),
            P(("dp", "fsdp"), None),
            P(("dp", "fsdp")),
            P(("dp", "fsdp"), None),
            P(("dp", "fsdp")),
            P(("dp", "fsdp")),
            P(("dp", "fsdp")),
            P(("dp", "fsdp"), None),
            P(("dp", "fsdp")),
            P(("dp", "fsdp"), None),
            P(("dp", "fsdp")),
            P(("dp", "fsdp")),
            P(("dp", "fsdp")),
            P(("dp", "fsdp"), None),
            P(("dp", "fsdp")),
            P(("dp", "fsdp"), None),
            P(("dp", "fsdp")),
            P(("dp", "fsdp")),
            P(("dp", "fsdp")),
            P(("dp", "fsdp"), None),
            P(("dp", "fsdp")),
            P(("dp", "fsdp"), None),
            P(("dp", "fsdp")),
            P(("dp", "fsdp")),
            P(("dp", "fsdp")),
            P(("dp", "fsdp"), None),
            P(("dp", "fsdp"), None),
        ),
        out_specs=(
            P(("dp", "fsdp"), None),
            P(("dp", "fsdp"), None),
            P(("dp", "fsdp"), None),
            P(("dp", "fsdp")),
            P(("dp", "fsdp"), None),
            P(("dp", "fsdp")),
            P(("dp", "fsdp")),
            P(("dp", "fsdp")),
            P(("dp", "fsdp"), None),
            P(("dp", "fsdp")),
            P(("dp", "fsdp"), None),
            P(("dp", "fsdp")),
            P(("dp", "fsdp")),
            P(("dp", "fsdp")),
            P(("dp", "fsdp"), None),
            P(("dp", "fsdp")),
            P(("dp", "fsdp"), None),
            P(("dp", "fsdp")),
            P(("dp", "fsdp")),
            P(("dp", "fsdp")),
            P(("dp", "fsdp"), None),
            P(("dp", "fsdp")),
            P(("dp", "fsdp"), None),
            P(("dp", "fsdp")),
            P(("dp", "fsdp")),
            P(("dp", "fsdp")),
            P(("dp", "fsdp"), None),
        ),
        check_vma=False,
    )
```
